512 devices in a mesh: segment: 2 (over x_lo), dc: 32 (over x_hi, z, core), head: 8 (over y).
Axes of the slice: x: 4 (x_hi: 2, x_lo: 2; x = x_hi * 2 + x_lo), y: 8, z: 8, core: 2. Of those that a mesh axis runs over, the one named last changes fastest.
Arguments:
- queries: bfloat16 [2, 2, 2048, 8192], P('segment', None, 'dc', 'head'), may hold values from -160 to 160
- keys: bfloat16 [2, 2, 2048, 1024], P('segment', None, 'dc', 'head'), may hold values from -6 to 6
- values: bfloat16 [2, 2, 2048, 1024], P('segment', None, 'dc', 'head'), may hold values from -18 to 18
- block_order: int32 [2, 64], replicated, may hold values from 0 to 63, each once within a row
- doc_lengths: int32 [2, 16], replicated, may hold values from 1 to 1024, 2048 in all within a row
Outputs:
- attended: bfloat16 [2, 2, 2048, 8192], P('segment', None, 'dc', 'head')
The draws below stay inside these ranges and needn't reach their ends.
Inputs may be any that keep to these rules, and one draw needn't show every extreme that they name: `block_order`: slots g of dc index r run over blocks 2r and 2r + 1 of the row: the row is a permutation of the blocks of 32 pack positions. `doc_lengths`: each row sums to 2048; its largest entry is exactly 1024.
All inputs are finite; a program needn't handle non-finite values.
Results may differ from the reference program's by a relative error of at most 0.013.
Values may be sent and summed in bfloat16 or wider, within the bound.
A program may use at most 64 MiB of HBM per device.

```python
import math
import jax
import jax.numpy as jnp
import numpy as np
from jax import lax

HEADS = 64
KV_HEADS = 8
HEAD_DIM = 128
MICRO = 2
DOCS = 16
LAYERS = 2
BLOCK = 32
TOKENS = 2048
N_DC = 32


def shared_draw(key):
    base = jnp.clip(jax.random.normal(jax.random.fold_in(key, 11), (LAYERS, MICRO, TOKENS, KV_HEADS * HEAD_DIM), jnp.float32), -6.0, 6.0)
    return base


def draw_keys(key, part):
    base = shared_draw(key)
    result = base
    return result.astype(jnp.bfloat16)


def draw_queries(key, part):
    key = jax.random.fold_in(key, 5)
    drawn = jnp.clip(jax.random.normal(key, (LAYERS, MICRO, TOKENS, HEADS * HEAD_DIM), jnp.float32), -6.0, 6.0)
    result = drawn
    return result.astype(jnp.bfloat16)


def draw_values(key, part):
    key = jax.random.fold_in(key, 7)
    columns = jnp.arange(KV_HEADS * HEAD_DIM, dtype=jnp.int32) // HEAD_DIM
    rising = 1.0 + 2.0 * columns.astype(jnp.float32) / (KV_HEADS - 1)
    shape = (LAYERS, MICRO, TOKENS, KV_HEADS * HEAD_DIM)
    result = jnp.clip(jax.random.normal(key, shape, jnp.float32), -6.0, 6.0) * rising
    return result.astype(jnp.bfloat16)


def split_up(number_of, total, limit, skew):
    portions = [(1 << 20) // math.isqrt(grade ** skew) + 1 for grade in range(2, number_of + 1)]
    spare, given = total - limit - (number_of - 1), [1] * (number_of - 1)
    while spare > 0:
        movable = [i for i in range(number_of - 1) if given[i] < limit]
        mass, remaining = sum([portions[i] for i in movable]), spare
        for i in movable:
            extra = min(limit - given[i], max(1, remaining * portions[i] // mass), spare)
            given[i] = given[i] + extra
            spare = spare - extra
    return np.array([limit] + given)


def uneven(rng, count, total, most, slope):
    if count == 2:
        one = jax.random.randint(rng, (), max(1, total - most), min(most, total - 1) + 1)
        return jnp.stack([one, total - one])
    sizes = jnp.asarray(split_up(count, total, most, slope), jnp.int32)
    twos = (count - 1) // 2
    donor, sink = sizes[1:1 + 2 * twos:2], sizes[2:2 + 2 * twos:2]
    margin = jnp.minimum(donor - 1, most - sink)
    shifted = jax.random.randint(jax.random.fold_in(rng, 1), (twos,), 0, 1 << 20) % (margin + 1)
    sizes = sizes.at[1:1 + 2 * twos:2].set(donor - shifted).at[2:2 + 2 * twos:2].set(sink + shifted)
    return sizes[jax.random.permutation(jax.random.fold_in(rng, 2), count)]


def setup_inputs(seed: int = 0) -> dict:
    arg_keys = jax.random.split(jax.random.key(seed), 6)
    return {
        "queries": draw_queries(jax.random.fold_in(arg_keys[5], 71), 0),
        "keys": draw_keys(jax.random.fold_in(arg_keys[5], 71), 0),
        "values": draw_values(jax.random.fold_in(arg_keys[5], 71), 0),
        "block_order": jax.vmap(lambda own: jax.random.permutation(own, 2 * N_DC))(jax.random.split(arg_keys[3], MICRO)).reshape((MICRO, 2 * N_DC)).astype(jnp.int32),
        "doc_lengths": jax.vmap(lambda own: uneven(own, DOCS, TOKENS, TOKENS // 2, 2))(jax.random.split(arg_keys[4], MICRO)).reshape((MICRO, DOCS)).astype(jnp.int32),
    }


NEG_FILL = -1e+30

def slot_layout(order_row, lengths_row):
    slots = jnp.arange(TOKENS, dtype=jnp.int32)
    position = jnp.take(order_row, slots // BLOCK).astype(jnp.int32) * BLOCK + slots % BLOCK
    ends = jnp.cumsum(lengths_row).astype(jnp.int32)
    document = lax.optimization_barrier(jnp.sum((position[:, None] >= ends[None, :]).astype(jnp.int32), axis=1))
    return (position, document)

def attend_all(query_rows, key_rows, value_rows, visible):
    group_size = HEADS // KV_HEADS
    scale_factor = 1.0 / math.sqrt(HEAD_DIM)

    def one_head(head):
        kv_head = head // group_size
        query_head = lax.dynamic_slice_in_dim(query_rows, head * HEAD_DIM, HEAD_DIM, 1).astype(jnp.float32)
        key_head = lax.dynamic_slice_in_dim(key_rows, kv_head * HEAD_DIM, HEAD_DIM, 1).astype(jnp.float32)
        value_head = lax.dynamic_slice_in_dim(value_rows, kv_head * HEAD_DIM, HEAD_DIM, 1).astype(jnp.float32)
        scores = jnp.dot(query_head, key_head.T, preferred_element_type=jnp.float32) * scale_factor
        scores = jnp.where(visible, scores, NEG_FILL)
        peak = lax.optimization_barrier(jnp.max(scores, axis=1, keepdims=True))
        weights = jnp.where(visible, jnp.exp(scores - peak), 0.0)
        total = lax.optimization_barrier(jnp.sum(weights, axis=1))
        rounded = lax.optimization_barrier(weights.astype(jnp.bfloat16)).astype(jnp.float32)
        mixed = jnp.dot(rounded, value_head, preferred_element_type=jnp.float32) / total[:, None]
        return mixed.astype(jnp.bfloat16)
    stacked = lax.map(one_head, jnp.arange(HEADS, dtype=jnp.int32))
    return jnp.transpose(stacked, (1, 0, 2)).reshape(TOKENS, HEADS * HEAD_DIM)

def reference(queries, keys, values, block_order, doc_lengths):
    first_layer = []
    second_layer = []
    for micro in range(MICRO):
        position, document = slot_layout(block_order[micro], doc_lengths[micro])
        visible = (document[:, None] == document[None, :]) & (position[None, :] <= position[:, None])
        layer_one = attend_all(queries[0, micro], keys[0, micro], values[0, micro], visible)
        widened = layer_one.astype(jnp.float32)
        norm_scale = 1.0 / jnp.sqrt(lax.optimization_barrier(jnp.mean(widened * widened, axis=1)) + 1e-05)
        lifted = (queries[1, micro].astype(jnp.float32) + widened * norm_scale[:, None]).astype(jnp.bfloat16)
        layer_two = attend_all(lifted, keys[1, micro], values[1, micro], visible)
        first_layer.append(layer_one)
        second_layer.append(layer_two)
    return jnp.stack([jnp.stack(first_layer), jnp.stack(second_layer)])
```

```python
import math

import jax
import jax.numpy as jnp
from jax import lax
from jax.experimental import pallas as pl
from jax.experimental.pallas import tpu as pltpu
from jax.sharding import PartitionSpec as P

HEAD_DIM = 128
BLOCK = 32
MICRO = 2
DOCS = 16
HEADS_LOCAL = 8
N_HEAD = 8
ROWS = 64
FEATURES = 8192
NZ = 8
FAR = NZ // 2
PLUS, MINUS = 0, 1
HIDDEN = -1e30
MESH = pl.DeviceIdType.MESH
EXP_SCALE = math.log2(math.e) / math.sqrt(HEAD_DIM)
GROUP_ROWS = 256


def kernel(
    order_ref,
    lengths_ref,
    q_hbm,
    k_hbm,
    v_hbm,
    o_ref,
    q_ref,
    buf,
    key_mask,
    query_mask,
    qx,
    acc,
    peak,
    att,
    ss_out,
    ss_in,
    load_sem,
    z_send,
    z_recv,
    s_send,
    s_recv,
    x_send,
    x_recv,
    a_send,
    a_recv,
    n_send,
    n_recv,
):
    seg = lax.axis_index("segment")
    dc = lax.axis_index("dc")
    head = lax.axis_index("head")
    core = dc % 2
    z = (dc // 2) % NZ
    xh = dc // (2 * NZ)

    def place(x_hi, z_at, core_at):
        return (x_hi * NZ + z_at) * 2 + core_at

    def z_of(direction, distance):
        if direction == PLUS:
            return (z + NZ - distance) % NZ
        return (z + distance) % NZ

    sibling = (seg, place(xh, z, 1 - core), head)
    x_peer = (seg, place(1 - xh, z, core), head)
    z_next = (
        (seg, place(xh, (z + 1) % NZ, core), head),
        (seg, place(xh, (z + NZ - 1) % NZ, core), head),
    )

    loads = []
    for m in range(MICRO):
        mine = buf.at[m, core, z, xh]
        loads.append(
            (
                pltpu.make_async_copy(k_hbm.at[0, m], mine.at[0], load_sem.at[m, 0]),
                pltpu.make_async_copy(v_hbm.at[0, m], mine.at[1], load_sem.at[m, 1]),
                pltpu.make_async_copy(q_hbm.at[0, m], q_ref.at[m], load_sem.at[m, 2]),
            )
        )
    for one in range(3):
        for m in range(MICRO):
            loads[m][one].start()

    barrier = pltpu.get_barrier_semaphore()
    for device in (sibling, x_peer) + z_next:
        pl.semaphore_signal(barrier, inc=1, device_id=device, device_id_type=MESH)
    for h in range(N_HEAD):
        pl.semaphore_signal(
            barrier, inc=1, device_id=(1 - seg, dc, h), device_id_type=MESH
        )
    pl.semaphore_wait(barrier, 4 + N_HEAD)

    def shard_x(part):
        return xh if part == 0 else 1 - xh

    def z_copy(m, direction, distance, part):
        source_z = z_of(direction, distance - 1)
        block = buf.at[m, core, source_z, shard_x(part)]
        return pltpu.make_async_remote_copy(
            src_ref=block,
            dst_ref=block,
            send_sem=z_send.at[m, direction, distance - 1, part],
            recv_sem=z_recv.at[m, direction, distance - 1, part],
            device_id=z_next[direction],
            device_id_type=MESH,
        )

    def s_copy(m, direction, distance, part):
        block = buf.at[m, core, z_of(direction, distance), shard_x(part)]
        return pltpu.make_async_remote_copy(
            src_ref=block,
            dst_ref=block,
            send_sem=s_send.at[m, direction, distance, part],
            recv_sem=s_recv.at[m, direction, distance, part],
            device_id=sibling,
            device_id_type=MESH,
        )

    def x_copy(m):
        block = buf.at[m, core, z, xh]
        return pltpu.make_async_remote_copy(
            src_ref=block,
            dst_ref=block,
            send_sem=x_send.at[m],
            recv_sem=x_recv.at[m],
            device_id=x_peer,
            device_id_type=MESH,
        )

    def travels(direction, distance, part):
        return distance < FAR or direction == part

    def offer_own(m):
        loads[m][0].wait()
        loads[m][1].wait()
        x_copy(m).start()
        z_copy(m, PLUS, 1, 0).start()
        z_copy(m, MINUS, 1, 0).start()
        s_copy(m, PLUS, 0, 0).start()

    def pass_x(m):
        x_copy(m).wait_recv()
        z_copy(m, PLUS, 1, 1).start()
        z_copy(m, MINUS, 1, 1).start()
        s_copy(m, PLUS, 0, 1).start()

    def pass_z(m, distance, part):
        for direction in (PLUS, MINUS):
            if travels(direction, distance, part):
                z_copy(m, direction, distance, part).wait_recv()
                if distance < FAR and travels(direction, distance + 1, part):
                    z_copy(m, direction, distance + 1, part).start()
                s_copy(m, direction, distance, part).start()

    def wait_sibling(m, distance):
        for part in (0, 1):
            for direction in (PLUS, MINUS):
                if distance == 0:
                    if direction == PLUS:
                        s_copy(m, PLUS, 0, part).wait_recv()
                elif travels(direction, distance, part):
                    s_copy(m, direction, distance, part).wait_recv()

    def finish_sends(m):
        x_copy(m).wait_send()
        for part in (0, 1):
            s_copy(m, PLUS, 0, part).wait_send()
            for distance in range(1, FAR + 1):
                for direction in (PLUS, MINUS):
                    if travels(direction, distance, part):
                        z_copy(m, direction, distance, part).wait_send()
                        s_copy(m, direction, distance, part).wait_send()

    def build_masks(m):
        lane = lax.broadcasted_iota(jnp.int32, (1, 128), 1)
        none = jnp.int32(1 << 20)
        low = jnp.full((1, 128), none, jnp.int32)
        high = jnp.zeros((1, 128), jnp.int32)
        run = jnp.int32(0)
        for d in range(DOCS):
            low = jnp.where(lane == d, run, low)
            run = run + lengths_ref[m, d]
            high = jnp.where(lane == d, run, high)
        for half in range(2):
            first = order_ref[m, dc * 2 + half] * BLOCK
            low = jnp.where(lane == DOCS + half, first + BLOCK, low)
            high = jnp.where(lane == DOCS + half, none, high)
            fine = (lane >= 32 + 32 * half) & (lane < 64 + 32 * half)
            low = jnp.where(fine, first + lane - (32 + 32 * half), low)
            high = jnp.where(fine, first + lane - (31 + 32 * half), high)
        high_q = jnp.where(lane < DOCS, high, none)
        row = lax.broadcasted_iota(jnp.int32, (BLOCK, 128), 0)
        for half in range(2):
            pos = order_ref[m, dc * 2 + half] * BLOCK + row
            hidden = (pos < low) | (pos >= high_q)
            query_mask[m, half * BLOCK : (half + 1) * BLOCK, :] = jnp.where(
                hidden, HIDDEN, 0.0
            ).astype(jnp.bfloat16)

        def one_z(z_at, carry):
            for c_at in range(2):
                for x_at in range(2):
                    for half in range(2):
                        number = place(x_at, z_at, c_at) * 2 + half
                        pos = order_ref[m, number] * BLOCK + row
                        inside = (pos >= low) & (pos < high)
                        key_mask[
                            m, z_at, c_at, x_at, half * BLOCK : (half + 1) * BLOCK, :
                        ] = jnp.where(inside, 1.0, 0.0).astype(jnp.bfloat16)
            return carry

        lax.fori_loop(0, NZ, one_z, 0)

    def start_rows(first, count):
        acc[first : first + count, :] = jnp.zeros((count, 256), jnp.float32)
        peak[first : first + count, :] = jnp.full((count, 128), HIDDEN, jnp.float32)

    def fold(m, z_list, first, count):
        keys, values = [], []
        for z_at in z_list:
            k = buf[m, :, z_at, :, 0].reshape(256, HEAD_DIM)
            v = buf[m, :, z_at, :, 1].reshape(256, HEAD_DIM)
            b = key_mask[m, z_at].reshape(256, 128)
            keys.append(jnp.concatenate([k, b], axis=1))
            values.append(jnp.concatenate([v, jnp.ones_like(v)], axis=1))
        kx = jnp.concatenate(keys, axis=0) if len(keys) > 1 else keys[0]
        vx = jnp.concatenate(values, axis=0) if len(values) > 1 else values[0]
        for start in range(first, first + count, GROUP_ROWS):
            rows = slice(start, start + GROUP_ROWS)
            scores = lax.dot_general(
                qx[rows, :], kx, (((1,), (1,)), ((), ())), preferred_element_type=jnp.float32
            )
            old = peak[rows, :]
            new = jnp.maximum(old, jnp.max(scores, axis=1, keepdims=True))
            peak[rows, :] = new
            weights = jnp.exp2((scores - new[:, :1]) * EXP_SCALE).astype(jnp.bfloat16)
            fade = jnp.exp2((old - new) * EXP_SCALE)
            acc[rows, :] = acc[rows, :] * jnp.concatenate([fade, fade], axis=1) + jnp.dot(
                weights, vx, preferred_element_type=jnp.float32
            )

    def finished(m, h):
        rows = slice(h * ROWS, (h + 1) * ROWS)
        out = (acc[rows, :HEAD_DIM] / acc[rows, HEAD_DIM:]).astype(jnp.bfloat16)
        o_ref[0, m, :, h * HEAD_DIM : (h + 1) * HEAD_DIM] = out
        return out

    def a_copy(m, h):
        return pltpu.make_async_remote_copy(
            src_ref=att.at[m, h],
            dst_ref=att.at[m, h],
            send_sem=a_send.at[m, h],
            recv_sem=a_recv.at[m, h],
            device_id=(1, dc, head),
            device_id_type=MESH,
        )

    def n_copy(m, h):
        return pltpu.make_async_remote_copy(
            src_ref=ss_out.at[m],
            dst_ref=ss_in.at[m, head],
            send_sem=n_send.at[m, h],
            recv_sem=n_recv.at[m, head],
            device_id=(1, dc, h),
            device_id_type=MESH,
        )

    def n_arrival(m, h):
        return pltpu.make_async_remote_copy(
            src_ref=ss_out.at[m],
            dst_ref=ss_in.at[m, h],
            send_sem=n_send.at[m, h],
            recv_sem=n_recv.at[m, h],
            device_id=(0, dc, h),
            device_id_type=MESH,
        )

    def stage_query(m, h, value):
        rows = slice(h * ROWS, (h + 1) * ROWS)
        qx[rows, :HEAD_DIM] = value
        qx[rows, HEAD_DIM:] = query_mask[m]

    def hand_over(m):
        squares = jnp.zeros((ROWS, HEAD_DIM), jnp.float32)
        for h in range(HEADS_LOCAL):
            out = finished(m, h)
            att[m, h] = out
            a_copy(m, h).start()
            wide = out.astype(jnp.float32)
            squares = squares + wide * wide
        ss_out[m, :, :ROWS] = jnp.sum(jnp.transpose(squares), axis=0, keepdims=True)
        for h in range(N_HEAD):
            n_copy(m, h).start()

    def near(distance):
        if distance == 0:
            return (z,)
        if distance == FAR:
            return (z_of(PLUS, FAR),)
        return (z_of(PLUS, distance), z_of(MINUS, distance))

    def compute(m, distance):
        wait_sibling(m, distance)
        fold(m, near(distance), 0, HEADS_LOCAL * ROWS)

    def begin(m):
        loads[m][2].wait()
        for h in range(HEADS_LOCAL):
            stage_query(m, h, q_ref[m, :, h * HEAD_DIM : (h + 1) * HEAD_DIM])
        start_rows(0, HEADS_LOCAL * ROWS)

    @pl.when(seg == 0)
    def _():
        offer_own(0)
        build_masks(0)
        begin(0)
        pass_x(0)
        pass_z(0, 1, 0)
        pass_z(0, 1, 1)
        compute(0, 0)
        pass_z(0, 2, 0)
        pass_z(0, 2, 1)
        offer_own(1)
        compute(0, 1)
        pass_z(0, 3, 0)
        pass_z(0, 3, 1)
        pass_x(1)
        compute(0, 2)
        pass_z(0, 4, 0)
        pass_z(0, 4, 1)
        pass_z(1, 1, 0)
        pass_z(1, 1, 1)
        compute(0, 3)
        compute(0, 4)
        hand_over(0)
        pass_z(1, 2, 0)
        pass_z(1, 2, 1)
        build_masks(1)
        begin(1)
        compute(1, 0)
        compute(1, 1)
        pass_z(1, 3, 0)
        pass_z(1, 3, 1)
        compute(1, 2)
        pass_z(1, 4, 0)
        pass_z(1, 4, 1)
        compute(1, 3)
        compute(1, 4)
        hand_over(1)
        for m in range(MICRO):
            finish_sends(m)
            for h in range(HEADS_LOCAL):
                a_copy(m, h).wait_send()
                n_copy(m, h).wait_send()

    @pl.when(seg == 1)
    def _():
        offer_own(0)
        build_masks(0)
        pass_x(0)
        for distance in range(1, FAR + 1):
            if distance == 3:
                offer_own(1)
            if distance == 4:
                pass_x(1)
            pass_z(0, distance, 0)
            pass_z(0, distance, 1)
        build_masks(1)
        for distance in range(1, FAR + 1):
            pass_z(1, distance, 0)
            pass_z(1, distance, 1)
        for m in range(MICRO):
            for distance in range(FAR + 1):
                wait_sibling(m, distance)
            finish_sends(m)
        for m in range(MICRO):
            loads[m][2].wait()
            for h in range(N_HEAD):
                n_arrival(m, h).wait_recv()
            total = ss_in[m, 0]
            for h in range(1, N_HEAD):
                total = total + ss_in[m, h]
            wide_total = jnp.broadcast_to(total[:, :ROWS], (HEAD_DIM, ROWS))
            norm = lax.rsqrt(jnp.transpose(wide_total) / FEATURES + 1e-05)
            start_rows(0, HEADS_LOCAL * ROWS)
            per_group = GROUP_ROWS // ROWS
            for group in range(HEADS_LOCAL // per_group):
                for h in range(group * per_group, (group + 1) * per_group):
                    a_copy(m, h).wait_recv()
                    lifted = (
                        q_ref[m, :, h * HEAD_DIM : (h + 1) * HEAD_DIM].astype(jnp.float32)
                        + att[m, h].astype(jnp.float32) * norm
                    )
                    stage_query(m, h, lifted.astype(jnp.bfloat16))
                for distance in range(FAR + 1):
                    fold(m, near(distance), group * GROUP_ROWS, GROUP_ROWS)
                for h in range(group * per_group, (group + 1) * per_group):
                    finished(m, h)


def on_device(queries, keys, values, block_order, doc_lengths):
    dma = pltpu.SemaphoreType.DMA
    z_shape = (MICRO, 2, FAR, 2)
    s_shape = (MICRO, 2, FAR + 1, 2)
    return pl.pallas_call(
        kernel,
        out_shape=jax.ShapeDtypeStruct(queries.shape, jnp.bfloat16),
        in_specs=[
            pl.BlockSpec(memory_space=pltpu.SMEM),
            pl.BlockSpec(memory_space=pltpu.SMEM),
            pl.BlockSpec(memory_space=pl.ANY),
            pl.BlockSpec(memory_space=pl.ANY),
            pl.BlockSpec(memory_space=pl.ANY),
        ],
        out_specs=pl.BlockSpec(memory_space=pltpu.VMEM),
        scratch_shapes=[
            pltpu.VMEM((MICRO, ROWS, HEADS_LOCAL * HEAD_DIM), jnp.bfloat16),
            pltpu.VMEM((MICRO, 2, NZ, 2, 2, ROWS, HEAD_DIM), jnp.bfloat16),
            pltpu.VMEM((MICRO, NZ, 2, 2, ROWS, 128), jnp.bfloat16),
            pltpu.VMEM((MICRO, ROWS, 128), jnp.bfloat16),
            pltpu.VMEM((HEADS_LOCAL * ROWS, 256), jnp.bfloat16),
            pltpu.VMEM((HEADS_LOCAL * ROWS, 256), jnp.float32),
            pltpu.VMEM((HEADS_LOCAL * ROWS, 128), jnp.float32),
            pltpu.VMEM((MICRO, HEADS_LOCAL, ROWS, HEAD_DIM), jnp.bfloat16),
            pltpu.VMEM((MICRO, 1, 128), jnp.float32),
            pltpu.VMEM((MICRO, N_HEAD, 1, 128), jnp.float32),
            dma((MICRO, 3)),
            dma(z_shape),
            dma(z_shape),
            dma(s_shape),
            dma(s_shape),
            dma((MICRO,)),
            dma((MICRO,)),
            dma((MICRO, HEADS_LOCAL)),
            dma((MICRO, HEADS_LOCAL)),
            dma((MICRO, N_HEAD)),
            dma((MICRO, N_HEAD)),
        ],
        compiler_params=pltpu.CompilerParams(
            collective_id=0, has_side_effects=True, vmem_limit_bytes=48 * 1024 * 1024
        ),
        name="attend_two_layers",
    )(block_order, doc_lengths, queries, keys, values)


def solution(mesh):
    placed = (
        P("segment", None, "dc", "head"),
        P("segment", None, "dc", "head"),
        P("segment", None, "dc", "head"),
        P(),
        P(),
    )
    return jax.shard_map(
        on_device,
        mesh=mesh,
        in_specs=placed,
        out_specs=P("segment", None, "dc", "head"),
        check_vma=False,
    )
```

```python
import math

import jax
import jax.numpy as jnp
from jax import lax
from jax.experimental import pallas as pl
from jax.experimental.pallas import tpu as pltpu
from jax.sharding import PartitionSpec as P

HEAD_DIM = 128
BLOCK = 32
MICRO = 2
DOCS = 16
HEADS_LOCAL = 8
N_HEAD = 8
ROWS = 64
FEATURES = 8192
NZ = 8
FAR = NZ // 2
HIDDEN = -1e30
MESH = pl.DeviceIdType.MESH
EXP_SCALE = math.log2(math.e) / math.sqrt(HEAD_DIM)
GROUP_ROWS = 256


def start_rank(head):
    if isinstance(head, int):
        return 2 * head - 1 if 1 <= head <= N_HEAD // 2 else 2 * ((N_HEAD - head) % N_HEAD)
    return jnp.where(
        (head >= 1) & (head <= N_HEAD // 2), 2 * head - 1, 2 * ((N_HEAD - head) % N_HEAD)
    )


def kernel(
    order_hbm,
    lengths_hbm,
    q_hbm,
    k_hbm,
    v_hbm,
    o_ref,
    order_ref,
    lengths_ref,
    q_ref,
    buf,
    key_mask,
    query_mask,
    qx,
    acc,
    peak,
    att,
    ss_out,
    ss_in,
    load_sem,
    small_sem,
    z_send,
    z_recv,
    x_send,
    x_recv,
    s_send,
    s_recv,
    a_send,
    a_recv,
    n_send,
    n_recv,
    x_in,
    s_in,
    seg_in,
    y_in,
    y_all,
):
    seg = lax.axis_index("segment")
    dc = lax.axis_index("dc")
    head = lax.axis_index("head")
    core = dc % 2
    z = (dc // 2) % NZ
    xh = dc // (2 * NZ)
    half = z // FAR
    rank = start_rank(head)

    def place(x_hi, z_at, core_at):
        return (x_hi * NZ + z_at) * 2 + core_at

    sibling = (seg, place(xh, z, 1 - core), head)
    x_peer = (seg, place(1 - xh, z, core), head)

    def z_peer(z_at):
        return (seg, place(xh, z_at, core), head)

    def tell(sem, device):
        pl.semaphore_signal(sem, inc=1, device_id=device, device_id_type=MESH)

    small = (
        pltpu.make_async_copy(order_hbm, order_ref, small_sem.at[0]),
        pltpu.make_async_copy(lengths_hbm, lengths_ref, small_sem.at[1]),
    )
    loads = []
    for m in range(MICRO):
        mine = buf.at[m, core, z, xh]
        loads.append(
            (
                pltpu.make_async_copy(k_hbm.at[0, m], mine.at[0], load_sem.at[m, 0]),
                pltpu.make_async_copy(v_hbm.at[0, m], mine.at[1], load_sem.at[m, 1]),
                pltpu.make_async_copy(q_hbm.at[0, m], q_ref.at[m], load_sem.at[m, 2]),
            )
        )
    for m in range(MICRO):
        loads[m][0].start()
        loads[m][1].start()
    for copy in small:
        copy.start()
    for m in range(MICRO):
        loads[m][2].start()

    barrier = pltpu.get_barrier_semaphore()
    for z_at in range(NZ):
        @pl.when(z_at > z)
        def _():
            tell(barrier, z_peer(z_at))

    @pl.when(xh == 0)
    def _():
        tell(barrier, x_peer)

    @pl.when(core == 1)
    def _():
        tell(barrier, sibling)

    @pl.when(seg == 0)
    def _():
        tell(barrier, (1, dc, head))
        for h in range(N_HEAD):
            @pl.when(start_rank(h) > rank)
            def _():
                tell(barrier, (0, dc, h))

    greetings = z + xh + (1 - core) + seg + (1 - seg) * rank

    @pl.when(greetings > 0)
    def _():
        pl.semaphore_wait(barrier, greetings)

    @pl.when(xh == 1)
    def _():
        tell(x_in, x_peer)

    @pl.when(core == 0)
    def _():
        tell(s_in, sibling)

    @pl.when(seg == 1)
    def _():
        tell(seg_in, (0, dc, head))

    def z_send_copy(m, z_at):
        block = buf.at[m, core, z, xh]
        return pltpu.make_async_remote_copy(
            src_ref=block,
            dst_ref=block,
            send_sem=z_send.at[m, z_at],
            recv_sem=z_recv.at[m, z],
            device_id=z_peer(z_at),
            device_id_type=MESH,
        )

    def z_arrival(m, z_at):
        block = buf.at[m, core, z_at, xh]
        return pltpu.make_async_remote_copy(
            src_ref=block,
            dst_ref=block,
            send_sem=z_send.at[m, z_at],
            recv_sem=z_recv.at[m, z_at],
            device_id=z_peer(z_at),
            device_id_type=MESH,
        )

    def x_copy(m, z_at, x_at):
        block = buf.at[m, core, z_at, x_at]
        return pltpu.make_async_remote_copy(
            src_ref=block,
            dst_ref=block,
            send_sem=x_send.at[m, z_at],
            recv_sem=x_recv.at[m, z_at],
            device_id=x_peer,
            device_id_type=MESH,
        )

    def s_copy(m, z_at, core_at):
        block = buf.at[m, core_at, z_at]
        return pltpu.make_async_remote_copy(
            src_ref=block,
            dst_ref=block,
            send_sem=s_send.at[m, z_at],
            recv_sem=s_recv.at[m, z_at],
            device_id=sibling,
            device_id_type=MESH,
        )

    def near(i):
        return half * FAR + (z + i) % FAR

    def far(i):
        return (1 - half) * FAR + (z + i) % FAR

    def pass_z(m, z_at):
        z_arrival(m, z_at).wait_recv()

        @pl.when(z_at > z)
        def _():
            z_send_copy(m, z_at).start()

        x_copy(m, z_at, xh).start()

    def pass_x(m, z_at):
        x_copy(m, z_at, 1 - xh).wait_recv()
        s_copy(m, z_at, core).start()

    def wait_s(m, z_at):
        s_copy(m, z_at, 1 - core).wait_recv()

    def finish_sends(m):
        for z_at in range(NZ):
            @pl.when(z_at != z)
            def _():
                z_send_copy(m, z_at).wait_send()
            x_copy(m, z_at, xh).wait_send()
            s_copy(m, z_at, core).wait_send()

    def build_masks(m):
        lane = lax.broadcasted_iota(jnp.int32, (1, 128), 1)
        none = jnp.int32(1 << 20)
        low = jnp.full((1, 128), none, jnp.int32)
        high = jnp.zeros((1, 128), jnp.int32)
        run = jnp.int32(0)
        for d in range(DOCS):
            low = jnp.where(lane == d, run, low)
            run = run + lengths_ref[m, d]
            high = jnp.where(lane == d, run, high)
        for half in range(2):
            first = order_ref[m, dc * 2 + half] * BLOCK
            low = jnp.where(lane == DOCS + half, first + BLOCK, low)
            high = jnp.where(lane == DOCS + half, none, high)
            fine = (lane >= 32 + 32 * half) & (lane < 64 + 32 * half)
            low = jnp.where(fine, first + lane - (32 + 32 * half), low)
            high = jnp.where(fine, first + lane - (31 + 32 * half), high)
        high_q = jnp.where(lane < DOCS, high, none)
        row = lax.broadcasted_iota(jnp.int32, (BLOCK, 128), 0)
        for half in range(2):
            pos = order_ref[m, dc * 2 + half] * BLOCK + row
            hidden = (pos < low) | (pos >= high_q)
            query_mask[m, half * BLOCK : (half + 1) * BLOCK, :] = jnp.where(
                hidden, HIDDEN, 0.0
            ).astype(jnp.bfloat16)

        def one_z(z_at, carry):
            for c_at in range(2):
                for x_at in range(2):
                    for half in range(2):
                        number = place(x_at, z_at, c_at) * 2 + half
                        pos = order_ref[m, number] * BLOCK + row
                        inside = (pos >= low) & (pos < high)
                        key_mask[
                            m, z_at, c_at, x_at, half * BLOCK : (half + 1) * BLOCK, :
                        ] = jnp.where(inside, 1.0, 0.0).astype(jnp.bfloat16)
            return carry

        lax.fori_loop(0, NZ, one_z, 0)

    def start_rows(m):
        acc[m] = jnp.zeros((HEADS_LOCAL * ROWS, 256), jnp.float32)
        peak[m] = jnp.full((HEADS_LOCAL * ROWS, 128), HIDDEN, jnp.float32)

    def fold(m, z_list, first, count):
        keys, values = [], []
        for z_at in z_list:
            k = buf[m, :, z_at, :, 0].reshape(256, HEAD_DIM)
            v = buf[m, :, z_at, :, 1].reshape(256, HEAD_DIM)
            b = key_mask[m, z_at].reshape(256, 128)
            keys.append(jnp.concatenate([k, b], axis=1))
            values.append(jnp.concatenate([v, jnp.ones_like(v)], axis=1))
        kx = jnp.concatenate(keys, axis=0)
        vx = jnp.concatenate(values, axis=0)
        for start in range(first, first + count, GROUP_ROWS):
            rows = slice(start, start + GROUP_ROWS)
            scores = lax.dot_general(
                qx[m, rows, :], kx, (((1,), (1,)), ((), ())), preferred_element_type=jnp.float32
            )
            old = peak[m, rows, :]
            new = jnp.maximum(old, jnp.max(scores, axis=1, keepdims=True))
            peak[m, rows, :] = new
            weights = jnp.exp2((scores - new[:, :1]) * EXP_SCALE).astype(jnp.bfloat16)
            fade = jnp.exp2((old - new) * EXP_SCALE)
            acc[m, rows, :] = acc[m, rows, :] * jnp.concatenate([fade, fade], axis=1) + jnp.dot(
                weights, vx, preferred_element_type=jnp.float32
            )

    def finished(m, h):
        rows = slice(h * ROWS, (h + 1) * ROWS)
        out = (acc[m, rows, :HEAD_DIM] / acc[m, rows, HEAD_DIM:]).astype(jnp.bfloat16)
        o_ref[0, m, :, h * HEAD_DIM : (h + 1) * HEAD_DIM] = out
        return out

    def a_copy(m, h):
        return pltpu.make_async_remote_copy(
            src_ref=att.at[m, h],
            dst_ref=att.at[m, h],
            send_sem=a_send.at[m, h],
            recv_sem=a_recv.at[m, h],
            device_id=(1, dc, head),
            device_id_type=MESH,
        )

    def n_copy(m, h):
        return pltpu.make_async_remote_copy(
            src_ref=ss_out.at[m],
            dst_ref=ss_in.at[m, head],
            send_sem=n_send.at[m, h],
            recv_sem=n_recv.at[m, head],
            device_id=(1, dc, h),
            device_id_type=MESH,
        )

    def n_arrival(m, h):
        return pltpu.make_async_remote_copy(
            src_ref=ss_out.at[m],
            dst_ref=ss_in.at[m, h],
            send_sem=n_send.at[m, h],
            recv_sem=n_recv.at[m, h],
            device_id=(0, dc, h),
            device_id_type=MESH,
        )

    def stage_query(m, h, value):
        rows = slice(h * ROWS, (h + 1) * ROWS)
        qx[m, rows, :HEAD_DIM] = value
        qx[m, rows, HEAD_DIM:] = query_mask[m]

    def hand_over(m):
        squares = jnp.zeros((ROWS, HEAD_DIM), jnp.float32)
        for h in range(HEADS_LOCAL):
            out = finished(m, h)
            att[m, h] = out
            a_copy(m, h).start()
            wide = out.astype(jnp.float32)
            squares = squares + wide * wide
        ss_out[m, :, :ROWS] = jnp.sum(jnp.transpose(squares), axis=0, keepdims=True)
        for h in range(N_HEAD):
            n_copy(m, h).start()

    def fold_two(m, z_a, z_b):
        wait_s(m, z_a)
        wait_s(m, z_b)
        fold(m, (z_a, z_b), 0, HEADS_LOCAL * ROWS)

    for m in range(MICRO):
        loads[m][0].wait()
        loads[m][1].wait()
        for z_at in range(NZ):
            @pl.when(z_at < z)
            def _():
                z_send_copy(m, z_at).start()
    for copy in small:
        copy.wait()
    for m in range(MICRO):
        build_masks(m)
        start_rows(m)
        loads[m][2].wait()

    @pl.when(seg == 0)
    def _():
        for m in range(MICRO):
            for h in range(HEADS_LOCAL):
                stage_query(m, h, q_ref[m, :, h * HEAD_DIM : (h + 1) * HEAD_DIM])
        for h in range(N_HEAD):
            @pl.when(start_rank(h) < rank)
            def _():
                tell(y_in, (0, dc, h))

    @pl.when(xh == 0)
    def _():
        pl.semaphore_wait(x_in, 1)

    @pl.when(core == 1)
    def _():
        pl.semaphore_wait(s_in, 1)

    for m in range(MICRO):
        x_copy(m, z, xh).start()
    for i in range(1, FAR):
        for m in range(MICRO):
            pass_z(m, near(i))
    for i in range(FAR - 1):
        for m in range(MICRO):
            pass_x(m, near(i))

    @pl.when(seg == 0)
    def _():
        pl.semaphore_wait(seg_in, 1)

        @pl.when(rank < N_HEAD - 1)
        def _():
            pl.semaphore_wait(y_in, N_HEAD - 1 - rank)

        for h in range(N_HEAD):
            @pl.when(head != h)
            def _():
                tell(y_all, (0, dc, h))

    for i in range(FAR):
        pass_z(0, far(i))
    for m in range(MICRO):
        pass_x(m, near(FAR - 1))
    for i in range(FAR):
        pass_z(1, far(i))

    @pl.when(seg == 0)
    def _():
        fold_two(0, near(0), near(1))
        fold_two(0, near(2), near(3))

    for i in range(FAR):
        pass_x(0, far(i))

    @pl.when(seg == 0)
    def _():
        fold_two(1, near(0), near(1))
        fold_two(1, near(2), near(3))
        fold_two(0, far(0), far(1))
        fold_two(0, far(2), far(3))
        pl.semaphore_wait(y_all, N_HEAD - 1)
        hand_over(0)

    for i in range(FAR):
        pass_x(1, far(i))

    @pl.when(seg == 0)
    def _():
        fold_two(1, far(0), far(1))
        fold_two(1, far(2), far(3))
        hand_over(1)
        for m in range(MICRO):
            for h in range(HEADS_LOCAL):
                a_copy(m, h).wait_send()
                n_copy(m, h).wait_send()

    @pl.when(seg == 1)
    def _():
        for m in range(MICRO):
            for z_at in range(NZ):
                wait_s(m, z_at)
        for m in range(MICRO):
            for h in range(N_HEAD):
                n_arrival(m, h).wait_recv()
            total = ss_in[m, 0]
            for h in range(1, N_HEAD):
                total = total + ss_in[m, h]
            wide_total = jnp.broadcast_to(total[:, :ROWS], (HEAD_DIM, ROWS))
            norm = lax.rsqrt(jnp.transpose(wide_total) / FEATURES + 1e-05)
            per_group = GROUP_ROWS // ROWS
            for group in range(HEADS_LOCAL // per_group):
                for h in range(group * per_group, (group + 1) * per_group):
                    a_copy(m, h).wait_recv()
                    lifted = (
                        q_ref[m, :, h * HEAD_DIM : (h + 1) * HEAD_DIM].astype(jnp.float32)
                        + att[m, h].astype(jnp.float32) * norm
                    )
                    stage_query(m, h, lifted.astype(jnp.bfloat16))
                for pair in range(FAR):
                    fold(m, (2 * pair, 2 * pair + 1), group * GROUP_ROWS, GROUP_ROWS)
                for h in range(group * per_group, (group + 1) * per_group):
                    finished(m, h)

    for m in range(MICRO):
        finish_sends(m)


def on_device(queries, keys, values, block_order, doc_lengths):
    dma = pltpu.SemaphoreType.DMA
    regular = pltpu.SemaphoreType.REGULAR
    rows = HEADS_LOCAL * ROWS
    return pl.pallas_call(
        kernel,
        out_shape=jax.ShapeDtypeStruct(queries.shape, jnp.bfloat16),
        in_specs=[pl.BlockSpec(memory_space=pltpu.HBM)] * 5,
        out_specs=pl.BlockSpec(memory_space=pltpu.VMEM),
        scratch_shapes=[
            pltpu.SMEM((MICRO, 64), jnp.int32),
            pltpu.SMEM((MICRO, DOCS), jnp.int32),
            pltpu.VMEM((MICRO, ROWS, HEADS_LOCAL * HEAD_DIM), jnp.bfloat16),
            pltpu.VMEM((MICRO, 2, NZ, 2, 2, ROWS, HEAD_DIM), jnp.bfloat16),
            pltpu.VMEM((MICRO, NZ, 2, 2, ROWS, 128), jnp.bfloat16),
            pltpu.VMEM((MICRO, ROWS, 128), jnp.bfloat16),
            pltpu.VMEM((MICRO, rows, 256), jnp.bfloat16),
            pltpu.VMEM((MICRO, rows, 256), jnp.float32),
            pltpu.VMEM((MICRO, rows, 128), jnp.float32),
            pltpu.VMEM((MICRO, HEADS_LOCAL, ROWS, HEAD_DIM), jnp.bfloat16),
            pltpu.VMEM((MICRO, 1, 128), jnp.float32),
            pltpu.VMEM((MICRO, N_HEAD, 1, 128), jnp.float32),
            dma((MICRO, 3)),
            dma((2,)),
            dma((MICRO, NZ)),
            dma((MICRO, NZ)),
            dma((MICRO, NZ)),
            dma((MICRO, NZ)),
            dma((MICRO, NZ)),
            dma((MICRO, NZ)),
            dma((MICRO, HEADS_LOCAL)),
            dma((MICRO, HEADS_LOCAL)),
            dma((MICRO, N_HEAD)),
            dma((MICRO, N_HEAD)),
            regular,
            regular,
            regular,
            regular,
            regular,
        ],
        compiler_params=pltpu.CompilerParams(
            collective_id=0, has_side_effects=True, vmem_limit_bytes=48 * 1024 * 1024
        ),
        name="attend_two_layers",
    )(block_order, doc_lengths, queries, keys, values)


def solution(mesh):
    placed = (
        P("segment", None, "dc", "head"),
        P("segment", None, "dc", "head"),
        P("segment", None, "dc", "head"),
        P(),
        P(),
    )
    return jax.shard_map(
        on_device,
        mesh=mesh,
        in_specs=placed,
        out_specs=P("segment", None, "dc", "head"),
        check_vma=False,
    )
```

```python
import math

import jax
import jax.numpy as jnp
from jax import lax
from jax.experimental import pallas as pl
from jax.experimental.pallas import tpu as pltpu
from jax.sharding import PartitionSpec as P

HEAD_DIM = 128
BLOCK = 32
MICRO = 2
DOCS = 16
HEADS_LOCAL = 8
N_HEAD = 8
ROWS = 64
FEATURES = 8192
NZ = 8
FAR = NZ // 2
HIDDEN = -1e30
MESH = pl.DeviceIdType.MESH
EXP_SCALE = math.log2(math.e) / math.sqrt(HEAD_DIM)
GROUP_ROWS = 256


def start_rank(head):
    if isinstance(head, int):
        return 2 * head - 1 if 1 <= head <= N_HEAD // 2 else 2 * ((N_HEAD - head) % N_HEAD)
    return jnp.where(
        (head >= 1) & (head <= N_HEAD // 2), 2 * head - 1, 2 * ((N_HEAD - head) % N_HEAD)
    )


def kernel(
    order_hbm,
    lengths_hbm,
    q_hbm,
    k_hbm,
    v_hbm,
    o_ref,
    order_ref,
    lengths_ref,
    q_ref,
    buf,
    key_mask,
    query_mask,
    qx,
    acc,
    peak,
    att,
    ss_out,
    ss_in,
    load_sem,
    small_sem,
    z_send,
    z_recv,
    x_send,
    x_recv,
    s_send,
    s_recv,
    a_send,
    a_recv,
    n_send,
    n_recv,
    z_in,
    x_in,
    s_in,
    seg_in,
    y_in,
    y_all,
):
    seg = lax.axis_index("segment")
    dc = lax.axis_index("dc")
    head = lax.axis_index("head")
    core = dc % 2
    z = (dc // 2) % NZ
    xh = dc // (2 * NZ)
    half = z // FAR
    rank = start_rank(head)

    def place(x_hi, z_at, core_at):
        return (x_hi * NZ + z_at) * 2 + core_at

    sibling = (seg, place(xh, z, 1 - core), head)
    x_peer = (seg, place(1 - xh, z, core), head)

    def z_peer(z_at):
        return (seg, place(xh, z_at, core), head)

    def tell(sem, device):
        pl.semaphore_signal(sem, inc=1, device_id=device, device_id_type=MESH)

    small = (
        pltpu.make_async_copy(order_hbm, order_ref, small_sem.at[0]),
        pltpu.make_async_copy(lengths_hbm, lengths_ref, small_sem.at[1]),
    )
    loads = []
    for m in range(MICRO):
        mine = buf.at[m, core, z, xh]
        loads.append(
            (
                pltpu.make_async_copy(k_hbm.at[0, m], mine.at[0], load_sem.at[m, 0]),
                pltpu.make_async_copy(v_hbm.at[0, m], mine.at[1], load_sem.at[m, 1]),
                pltpu.make_async_copy(q_hbm.at[0, m], q_ref.at[m], load_sem.at[m, 2]),
            )
        )
    for m in range(MICRO):
        loads[m][0].start()
        loads[m][1].start()
    for copy in small:
        copy.start()
    for m in range(MICRO):
        loads[m][2].start()

    barrier = pltpu.get_barrier_semaphore()
    for z_at in range(NZ):
        @pl.when(z_at > z)
        def _():
            tell(barrier, z_peer(z_at))

    @pl.when(xh == 0)
    def _():
        tell(barrier, x_peer)

    @pl.when(core == 1)
    def _():
        tell(barrier, sibling)

    @pl.when(seg == 0)
    def _():
        tell(barrier, (1, dc, head))
        for h in range(N_HEAD):
            @pl.when(start_rank(h) > rank)
            def _():
                tell(barrier, (0, dc, h))

    greetings = z + xh + (1 - core) + seg + (1 - seg) * rank

    @pl.when(greetings > 0)
    def _():
        pl.semaphore_wait(barrier, greetings)

    for z_at in range(NZ):
        @pl.when(z_at < z)
        def _():
            tell(z_in.at[z], z_peer(z_at))

    @pl.when(xh == 1)
    def _():
        tell(x_in, x_peer)

    @pl.when(core == 0)
    def _():
        tell(s_in, sibling)

    @pl.when(seg == 1)
    def _():
        tell(seg_in, (0, dc, head))

    @pl.when(seg == 0)
    def _():
        for h in range(N_HEAD):
            @pl.when(start_rank(h) < rank)
            def _():
                tell(y_in, (0, dc, h))

    def z_send_copy(m, z_at):
        block = buf.at[m, core, z, xh]
        return pltpu.make_async_remote_copy(
            src_ref=block,
            dst_ref=block,
            send_sem=z_send.at[m, z_at],
            recv_sem=z_recv.at[m, z],
            device_id=z_peer(z_at),
            device_id_type=MESH,
        )

    def z_arrival(m, z_at):
        block = buf.at[m, core, z_at, xh]
        return pltpu.make_async_remote_copy(
            src_ref=block,
            dst_ref=block,
            send_sem=z_send.at[m, z_at],
            recv_sem=z_recv.at[m, z_at],
            device_id=z_peer(z_at),
            device_id_type=MESH,
        )

    def x_copy(m, z_at, x_at):
        block = buf.at[m, core, z_at, x_at]
        return pltpu.make_async_remote_copy(
            src_ref=block,
            dst_ref=block,
            send_sem=x_send.at[m, z_at],
            recv_sem=x_recv.at[m, z_at],
            device_id=x_peer,
            device_id_type=MESH,
        )

    def s_copy(m, z_at, core_at):
        block = buf.at[m, core_at, z_at]
        return pltpu.make_async_remote_copy(
            src_ref=block,
            dst_ref=block,
            send_sem=s_send.at[m, z_at],
            recv_sem=s_recv.at[m, z_at],
            device_id=sibling,
            device_id_type=MESH,
        )

    def near(i):
        return half * FAR + (z + i) % FAR

    def far(i):
        return (1 - half) * FAR + (z + i) % FAR

    def pass_z(m, z_at):
        z_arrival(m, z_at).wait_recv()
        x_copy(m, z_at, xh).start()

    def pass_x(m, z_at):
        x_copy(m, z_at, 1 - xh).wait_recv()
        s_copy(m, z_at, core).start()

    def wait_s(m, z_at):
        s_copy(m, z_at, 1 - core).wait_recv()

    def finish_sends(m):
        for z_at in range(NZ):
            @pl.when(z_at != z)
            def _():
                z_send_copy(m, z_at).wait_send()
            x_copy(m, z_at, xh).wait_send()
            s_copy(m, z_at, core).wait_send()

    def build_masks(m):
        lane = lax.broadcasted_iota(jnp.int32, (1, 128), 1)
        none = jnp.int32(1 << 20)
        low = jnp.full((1, 128), none, jnp.int32)
        high = jnp.zeros((1, 128), jnp.int32)
        run = jnp.int32(0)
        for d in range(DOCS):
            low = jnp.where(lane == d, run, low)
            run = run + lengths_ref[m, d]
            high = jnp.where(lane == d, run, high)
        for half in range(2):
            first = order_ref[m, dc * 2 + half] * BLOCK
            low = jnp.where(lane == DOCS + half, first + BLOCK, low)
            high = jnp.where(lane == DOCS + half, none, high)
            fine = (lane >= 32 + 32 * half) & (lane < 64 + 32 * half)
            low = jnp.where(fine, first + lane - (32 + 32 * half), low)
            high = jnp.where(fine, first + lane - (31 + 32 * half), high)
        high_q = jnp.where(lane < DOCS, high, none)
        row = lax.broadcasted_iota(jnp.int32, (BLOCK, 128), 0)
        for half in range(2):
            pos = order_ref[m, dc * 2 + half] * BLOCK + row
            hidden = (pos < low) | (pos >= high_q)
            query_mask[m, half * BLOCK : (half + 1) * BLOCK, :] = jnp.where(
                hidden, HIDDEN, 0.0
            ).astype(jnp.bfloat16)

        def one_z(z_at, carry):
            for c_at in range(2):
                for x_at in range(2):
                    for half in range(2):
                        number = place(x_at, z_at, c_at) * 2 + half
                        pos = order_ref[m, number] * BLOCK + row
                        inside = (pos >= low) & (pos < high)
                        key_mask[
                            m, z_at, c_at, x_at, half * BLOCK : (half + 1) * BLOCK, :
                        ] = jnp.where(inside, 1.0, 0.0).astype(jnp.bfloat16)
            return carry

        lax.fori_loop(0, NZ, one_z, 0)

    def start_rows(m):
        acc[m] = jnp.zeros((HEADS_LOCAL * ROWS, 256), jnp.float32)
        peak[m] = jnp.full((HEADS_LOCAL * ROWS, 128), HIDDEN, jnp.float32)

    def gathered(m, z_list):
        keys, values = [], []
        for z_at in z_list:
            k = buf[m, :, z_at, :, 0].reshape(256, HEAD_DIM)
            v = buf[m, :, z_at, :, 1].reshape(256, HEAD_DIM)
            b = key_mask[m, z_at].reshape(256, 128)
            keys.append(jnp.concatenate([k, b], axis=1))
            values.append(jnp.concatenate([v, jnp.ones_like(v)], axis=1))
        return jnp.concatenate(keys, axis=0), jnp.concatenate(values, axis=0)

    def score(m, rows, kx):
        return lax.dot_general(
            qx[m, rows, :], kx, (((1,), (1,)), ((), ())), preferred_element_type=jnp.float32
        )

    def fold(m, z_list):
        kx, vx = gathered(m, z_list)
        for start in range(0, HEADS_LOCAL * ROWS, GROUP_ROWS):
            rows = slice(start, start + GROUP_ROWS)
            scores = score(m, rows, kx)
            old = peak[m, rows, :]
            new = jnp.maximum(old, jnp.max(scores, axis=1, keepdims=True))
            peak[m, rows, :] = new
            weights = jnp.exp2((scores - new[:, :1]) * EXP_SCALE).astype(jnp.bfloat16)
            fade = jnp.exp2((old - new) * EXP_SCALE)
            acc[m, rows, :] = acc[m, rows, :] * jnp.concatenate([fade, fade], axis=1) + jnp.dot(
                weights, vx, preferred_element_type=jnp.float32
            )

    def fold_all(m, start):
        kx, vx = gathered(m, range(NZ))
        rows = slice(start, start + GROUP_ROWS)
        scores = score(m, rows, kx)
        top = jnp.max(scores, axis=1, keepdims=True)
        weights = jnp.exp2((scores - top) * EXP_SCALE).astype(jnp.bfloat16)
        acc[m, rows, :] = jnp.dot(weights, vx, preferred_element_type=jnp.float32)

    def finished(m, h):
        rows = slice(h * ROWS, (h + 1) * ROWS)
        out = (acc[m, rows, :HEAD_DIM] / acc[m, rows, HEAD_DIM:]).astype(jnp.bfloat16)
        o_ref[0, m, :, h * HEAD_DIM : (h + 1) * HEAD_DIM] = out
        return out

    def a_copy(m, h):
        return pltpu.make_async_remote_copy(
            src_ref=att.at[m, h],
            dst_ref=att.at[m, h],
            send_sem=a_send.at[m, h],
            recv_sem=a_recv.at[m, h],
            device_id=(1, dc, head),
            device_id_type=MESH,
        )

    def n_copy(m, h):
        return pltpu.make_async_remote_copy(
            src_ref=ss_out.at[m],
            dst_ref=ss_in.at[m, head],
            send_sem=n_send.at[m, h],
            recv_sem=n_recv.at[m, head],
            device_id=(1, dc, h),
            device_id_type=MESH,
        )

    def n_arrival(m, h):
        return pltpu.make_async_remote_copy(
            src_ref=ss_out.at[m],
            dst_ref=ss_in.at[m, h],
            send_sem=n_send.at[m, h],
            recv_sem=n_recv.at[m, h],
            device_id=(0, dc, h),
            device_id_type=MESH,
        )

    def stage_query(m, h, value):
        rows = slice(h * ROWS, (h + 1) * ROWS)
        qx[m, rows, :HEAD_DIM] = value
        qx[m, rows, HEAD_DIM:] = query_mask[m]

    def hand_over(m):
        squares = jnp.zeros((ROWS, HEAD_DIM), jnp.float32)
        for h in range(HEADS_LOCAL):
            out = finished(m, h)
            att[m, h] = out
            a_copy(m, h).start()
            wide = out.astype(jnp.float32)
            squares = squares + wide * wide
        ss_out[m, :, :ROWS] = jnp.sum(jnp.transpose(squares), axis=0, keepdims=True)
        for h in range(N_HEAD):
            n_copy(m, h).start()

    def fold_four(m, z_list):
        for z_at in z_list:
            wait_s(m, z_at)
        fold(m, z_list)

    def prepare(m):
        build_masks(m)
        loads[m][2].wait()

        @pl.when(seg == 0)
        def _():
            start_rows(m)
            for h in range(HEADS_LOCAL):
                stage_query(m, h, q_ref[m, :, h * HEAD_DIM : (h + 1) * HEAD_DIM])

    for m in range(MICRO):
        loads[m][0].wait()
        loads[m][1].wait()
        for z_at in range(NZ):
            @pl.when(z_at < z)
            def _():
                z_send_copy(m, z_at).start()
    for i in range(1, FAR):
        @pl.when(near(i) > z)
        def _():
            pl.semaphore_wait(z_in.at[near(i)], 1)
            for m in range(MICRO):
                z_send_copy(m, near(i)).start()

    for copy in small:
        copy.wait()
    prepare(0)

    @pl.when(xh == 0)
    def _():
        pl.semaphore_wait(x_in, 1)

    @pl.when(core == 1)
    def _():
        pl.semaphore_wait(s_in, 1)

    for m in range(MICRO):
        x_copy(m, z, xh).start()
    prepare(1)
    for i in range(1, FAR):
        for m in range(MICRO):
            pass_z(m, near(i))

    @pl.when(half == 0)
    def _():
        for i in range(FAR):
            pl.semaphore_wait(z_in.at[far(i)], 1)
            z_send_copy(0, far(i)).start()
        for i in range(FAR):
            z_send_copy(1, far(i)).start()

    for i in range(FAR - 1):
        for m in range(MICRO):
            pass_x(m, near(i))

    @pl.when(seg == 0)
    def _():
        pl.semaphore_wait(seg_in, 1)

        @pl.when(rank < N_HEAD - 1)
        def _():
            pl.semaphore_wait(y_in, N_HEAD - 1 - rank)

        for h in range(N_HEAD):
            @pl.when(head != h)
            def _():
                tell(y_all, (0, dc, h))

    for i in range(FAR):
        pass_z(0, far(i))
    for m in range(MICRO):
        pass_x(m, near(FAR - 1))
    for i in range(FAR):
        pass_z(1, far(i))

    nears = tuple(near(i) for i in range(FAR))
    fars = tuple(far(i) for i in range(FAR))

    @pl.when(seg == 0)
    def _():
        fold_four(0, nears)

    for i in range(FAR):
        pass_x(0, far(i))

    @pl.when(seg == 0)
    def _():
        fold_four(0, fars)
        pl.semaphore_wait(y_all, N_HEAD - 1)
        hand_over(0)
        fold_four(1, nears)

    for i in range(FAR):
        pass_x(1, far(i))

    @pl.when(seg == 0)
    def _():
        fold_four(1, fars)
        hand_over(1)
        for m in range(MICRO):
            for h in range(HEADS_LOCAL):
                a_copy(m, h).wait_send()
                n_copy(m, h).wait_send()

    @pl.when(seg == 1)
    def _():
        for m in range(MICRO):
            for z_at in range(NZ):
                wait_s(m, z_at)
        for m in range(MICRO):
            for h in range(N_HEAD):
                n_arrival(m, h).wait_recv()
            total = ss_in[m, 0]
            for h in range(1, N_HEAD):
                total = total + ss_in[m, h]
            wide_total = jnp.broadcast_to(total[:, :ROWS], (HEAD_DIM, ROWS))
            norm = lax.rsqrt(jnp.transpose(wide_total) / FEATURES + 1e-05)
            per_group = GROUP_ROWS // ROWS
            for group in range(HEADS_LOCAL // per_group):
                for h in range(group * per_group, (group + 1) * per_group):
                    a_copy(m, h).wait_recv()
                    lifted = (
                        q_ref[m, :, h * HEAD_DIM : (h + 1) * HEAD_DIM].astype(jnp.float32)
                        + att[m, h].astype(jnp.float32) * norm
                    )
                    stage_query(m, h, lifted.astype(jnp.bfloat16))
                fold_all(m, group * GROUP_ROWS)
                for h in range(group * per_group, (group + 1) * per_group):
                    finished(m, h)

    for m in range(MICRO):
        finish_sends(m)


def on_device(queries, keys, values, block_order, doc_lengths):
    dma = pltpu.SemaphoreType.DMA
    regular = pltpu.SemaphoreType.REGULAR
    rows = HEADS_LOCAL * ROWS
    return pl.pallas_call(
        kernel,
        out_shape=jax.ShapeDtypeStruct(queries.shape, jnp.bfloat16),
        in_specs=[pl.BlockSpec(memory_space=pltpu.HBM)] * 5,
        out_specs=pl.BlockSpec(memory_space=pltpu.VMEM),
        scratch_shapes=[
            pltpu.SMEM((MICRO, 64), jnp.int32),
            pltpu.SMEM((MICRO, DOCS), jnp.int32),
            pltpu.VMEM((MICRO, ROWS, HEADS_LOCAL * HEAD_DIM), jnp.bfloat16),
            pltpu.VMEM((MICRO, 2, NZ, 2, 2, ROWS, HEAD_DIM), jnp.bfloat16),
            pltpu.VMEM((MICRO, NZ, 2, 2, ROWS, 128), jnp.bfloat16),
            pltpu.VMEM((MICRO, ROWS, 128), jnp.bfloat16),
            pltpu.VMEM((MICRO, rows, 256), jnp.bfloat16),
            pltpu.VMEM((MICRO, rows, 256), jnp.float32),
            pltpu.VMEM((MICRO, rows, 128), jnp.float32),
            pltpu.VMEM((MICRO, HEADS_LOCAL, ROWS, HEAD_DIM), jnp.bfloat16),
            pltpu.VMEM((MICRO, 1, 128), jnp.float32),
            pltpu.VMEM((MICRO, N_HEAD, 1, 128), jnp.float32),
            dma((MICRO, 3)),
            dma((2,)),
            dma((MICRO, NZ)),
            dma((MICRO, NZ)),
            dma((MICRO, NZ)),
            dma((MICRO, NZ)),
            dma((MICRO, NZ)),
            dma((MICRO, NZ)),
            dma((MICRO, HEADS_LOCAL)),
            dma((MICRO, HEADS_LOCAL)),
            dma((MICRO, N_HEAD)),
            dma((MICRO, N_HEAD)),
            pltpu.SemaphoreType.REGULAR((NZ,)),
            regular,
            regular,
            regular,
            regular,
            regular,
        ],
        compiler_params=pltpu.CompilerParams(
            collective_id=0, has_side_effects=True, vmem_limit_bytes=62 * 1024 * 1024
        ),
        name="attend_two_layers",
    )(block_order, doc_lengths, queries, keys, values)


def solution(mesh):
    placed = (
        P("segment", None, "dc", "head"),
        P("segment", None, "dc", "head"),
        P("segment", None, "dc", "head"),
        P(),
        P(),
    )
    return jax.shard_map(
        on_device,
        mesh=mesh,
        in_specs=placed,
        out_specs=P("segment", None, "dc", "head"),
        check_vma=False,
    )
```

```python
import math

import jax
import jax.numpy as jnp
from jax import lax
from jax.experimental import pallas as pl
from jax.experimental.pallas import tpu as pltpu
from jax.sharding import PartitionSpec as P

HEAD_DIM = 128
BLOCK = 32
MICRO = 2
DOCS = 16
HEADS_LOCAL = 8
N_HEAD = 8
ROWS = 64
FEATURES = 8192
NZ = 8
FAR = NZ // 2
HIDDEN = -1e30
MESH = pl.DeviceIdType.MESH
EXP_SCALE = math.log2(math.e) / math.sqrt(HEAD_DIM)
GROUP_ROWS = 256


def start_rank(head):
    if isinstance(head, int):
        return 2 * head - 1 if 1 <= head <= N_HEAD // 2 else 2 * ((N_HEAD - head) % N_HEAD)
    return jnp.where(
        (head >= 1) & (head <= N_HEAD // 2), 2 * head - 1, 2 * ((N_HEAD - head) % N_HEAD)
    )


def kernel(
    order_hbm,
    lengths_hbm,
    q_hbm,
    k_hbm,
    v_hbm,
    o_ref,
    order_ref,
    lengths_ref,
    q_ref,
    buf,
    key_mask,
    query_mask,
    qx,
    acc,
    peak,
    att,
    ss_out,
    ss_in,
    load_sem,
    small_sem,
    z_send,
    z_recv,
    x_send,
    x_recv,
    s_send,
    s_recv,
    a_send,
    a_recv,
    n_send,
    n_recv,
    z_in,
    x_in,
    s_in,
    seg_in,
    y_in,
    y_all,
):
    seg = lax.axis_index("segment")
    dc = lax.axis_index("dc")
    head = lax.axis_index("head")
    core = dc % 2
    z = (dc // 2) % NZ
    xh = dc // (2 * NZ)
    half = z // FAR
    rank = start_rank(head)

    def place(x_hi, z_at, core_at):
        return (x_hi * NZ + z_at) * 2 + core_at

    sibling = (seg, place(xh, z, 1 - core), head)
    x_peer = (seg, place(1 - xh, z, core), head)

    def z_peer(z_at):
        return (seg, place(xh, z_at, core), head)

    def tell(sem, device):
        pl.semaphore_signal(sem, inc=1, device_id=device, device_id_type=MESH)

    small = (
        pltpu.make_async_copy(order_hbm, order_ref, small_sem.at[0]),
        pltpu.make_async_copy(lengths_hbm, lengths_ref, small_sem.at[1]),
    )
    loads = []
    for m in range(MICRO):
        mine = buf.at[m, core, z, xh]
        loads.append(
            (
                pltpu.make_async_copy(k_hbm.at[0, m], mine.at[0], load_sem.at[m, 0]),
                pltpu.make_async_copy(v_hbm.at[0, m], mine.at[1], load_sem.at[m, 1]),
                pltpu.make_async_copy(q_hbm.at[0, m], q_ref.at[m], load_sem.at[m, 2]),
            )
        )
    for m in range(MICRO):
        loads[m][0].start()
        loads[m][1].start()
    for copy in small:
        copy.start()
    for m in range(MICRO):
        loads[m][2].start()

    barrier = pltpu.get_barrier_semaphore()
    for z_at in range(NZ):
        @pl.when(z_at > z)
        def _():
            tell(barrier, z_peer(z_at))

    @pl.when(xh == 0)
    def _():
        tell(barrier, x_peer)

    @pl.when(core == 1)
    def _():
        tell(barrier, sibling)

    @pl.when(seg == 0)
    def _():
        tell(barrier, (1, dc, head))
        for h in range(N_HEAD):
            @pl.when(start_rank(h) > rank)
            def _():
                tell(barrier, (0, dc, h))

    greetings = z + xh + (1 - core) + seg + (1 - seg) * rank

    @pl.when(greetings > 0)
    def _():
        pl.semaphore_wait(barrier, greetings)

    for z_at in range(NZ):
        @pl.when(z_at < z)
        def _():
            tell(z_in.at[z], z_peer(z_at))

    @pl.when(xh == 1)
    def _():
        tell(x_in, x_peer)

    @pl.when(core == 0)
    def _():
        tell(s_in, sibling)

    @pl.when(seg == 1)
    def _():
        tell(seg_in, (0, dc, head))

    @pl.when(seg == 0)
    def _():
        for h in range(N_HEAD):
            @pl.when(start_rank(h) < rank)
            def _():
                tell(y_in, (0, dc, h))

    def z_send_copy(m, z_at):
        block = buf.at[m, core, z, xh]
        return pltpu.make_async_remote_copy(
            src_ref=block,
            dst_ref=block,
            send_sem=z_send.at[m, z_at],
            recv_sem=z_recv.at[m, z],
            device_id=z_peer(z_at),
            device_id_type=MESH,
        )

    def z_arrival(m, z_at):
        block = buf.at[m, core, z_at, xh]
        return pltpu.make_async_remote_copy(
            src_ref=block,
            dst_ref=block,
            send_sem=z_send.at[m, z_at],
            recv_sem=z_recv.at[m, z_at],
            device_id=z_peer(z_at),
            device_id_type=MESH,
        )

    def x_copy(m, z_at, x_at):
        block = buf.at[m, core, z_at, x_at]
        return pltpu.make_async_remote_copy(
            src_ref=block,
            dst_ref=block,
            send_sem=x_send.at[m, z_at],
            recv_sem=x_recv.at[m, z_at],
            device_id=x_peer,
            device_id_type=MESH,
        )

    def s_copy(m, z_at, core_at):
        block = buf.at[m, core_at, z_at]
        return pltpu.make_async_remote_copy(
            src_ref=block,
            dst_ref=block,
            send_sem=s_send.at[m, z_at],
            recv_sem=s_recv.at[m, z_at],
            device_id=sibling,
            device_id_type=MESH,
        )

    def near(i):
        return half * FAR + (z + i) % FAR

    def far(i):
        return (1 - half) * FAR + (z + i) % FAR

    def pass_z(m, z_at):
        z_arrival(m, z_at).wait_recv()
        x_copy(m, z_at, xh).start()

    def pass_x(m, z_at):
        x_copy(m, z_at, 1 - xh).wait_recv()
        s_copy(m, z_at, core).start()

    def wait_s(m, z_at):
        s_copy(m, z_at, 1 - core).wait_recv()

    def finish_sends(m):
        for z_at in range(NZ):
            @pl.when(z_at != z)
            def _():
                z_send_copy(m, z_at).wait_send()
            x_copy(m, z_at, xh).wait_send()
            s_copy(m, z_at, core).wait_send()

    def build_masks(m):
        lane = lax.broadcasted_iota(jnp.int32, (1, 128), 1)
        none = jnp.int32(1 << 20)
        low = jnp.full((1, 128), none, jnp.int32)
        high = jnp.zeros((1, 128), jnp.int32)
        run = jnp.int32(0)
        for d in range(DOCS):
            low = jnp.where(lane == d, run, low)
            run = run + lengths_ref[m, d]
            high = jnp.where(lane == d, run, high)
        for half in range(2):
            first = order_ref[m, dc * 2 + half] * BLOCK
            low = jnp.where(lane == DOCS + half, first + BLOCK, low)
            high = jnp.where(lane == DOCS + half, none, high)
            fine = (lane >= 32 + 32 * half) & (lane < 64 + 32 * half)
            low = jnp.where(fine, first + lane - (32 + 32 * half), low)
            high = jnp.where(fine, first + lane - (31 + 32 * half), high)
        high_q = jnp.where(lane < DOCS, high, none)
        row = lax.broadcasted_iota(jnp.int32, (BLOCK, 128), 0)
        for half in range(2):
            pos = order_ref[m, dc * 2 + half] * BLOCK + row
            hidden = (pos < low) | (pos >= high_q)
            query_mask[m, half * BLOCK : (half + 1) * BLOCK, :] = jnp.where(
                hidden, HIDDEN, 0.0
            ).astype(jnp.bfloat16)

        def one_z(z_at, carry):
            for c_at in range(2):
                for x_at in range(2):
                    for half in range(2):
                        number = place(x_at, z_at, c_at) * 2 + half
                        pos = order_ref[m, number] * BLOCK + row
                        inside = (pos >= low) & (pos < high)
                        key_mask[
                            m, z_at, c_at, x_at, half * BLOCK : (half + 1) * BLOCK, :
                        ] = jnp.where(inside, 1.0, 0.0).astype(jnp.bfloat16)
            return carry

        lax.fori_loop(0, NZ, one_z, 0)

    def start_rows(m):
        acc[m] = jnp.zeros((HEADS_LOCAL * ROWS, 256), jnp.float32)
        peak[m] = jnp.full((HEADS_LOCAL * ROWS, 128), HIDDEN, jnp.float32)

    def gathered(m, z_list):
        keys, values = [], []
        for z_at in z_list:
            k = buf[m, :, z_at, :, 0].reshape(256, HEAD_DIM)
            v = buf[m, :, z_at, :, 1].reshape(256, HEAD_DIM)
            b = key_mask[m, z_at].reshape(256, 128)
            keys.append(jnp.concatenate([k, b], axis=1))
            values.append(jnp.concatenate([v, jnp.ones_like(v)], axis=1))
        return jnp.concatenate(keys, axis=0), jnp.concatenate(values, axis=0)

    def score(m, rows, kx):
        return lax.dot_general(
            qx[m, rows, :], kx, (((1,), (1,)), ((), ())), preferred_element_type=jnp.float32
        )

    groups = [
        slice(start, start + GROUP_ROWS) for start in range(0, HEADS_LOCAL * ROWS, GROUP_ROWS)
    ]

    def fold(m, z_list):
        kx, vx = gathered(m, z_list)
        scores = [score(m, rows, kx) for rows in groups]
        for rows, one in zip(groups, scores):
            old = peak[m, rows, :]
            new = jnp.maximum(old, jnp.max(one, axis=1, keepdims=True))
            peak[m, rows, :] = new
            weights = jnp.exp2((one - new[:, :1]) * EXP_SCALE).astype(jnp.bfloat16)
            fade = jnp.exp2((old - new) * EXP_SCALE)
            acc[m, rows, :] = acc[m, rows, :] * jnp.concatenate([fade, fade], axis=1) + jnp.dot(
                weights, vx, preferred_element_type=jnp.float32
            )

    def settle(m, vx, rows, scores):
        top = jnp.max(scores, axis=1, keepdims=True)
        weights = jnp.exp2((scores - top) * EXP_SCALE).astype(jnp.bfloat16)
        acc[m, rows, :] = jnp.dot(weights, vx, preferred_element_type=jnp.float32)

    def finished(m, h):
        rows = slice(h * ROWS, (h + 1) * ROWS)
        return (acc[m, rows, :HEAD_DIM] / acc[m, rows, HEAD_DIM:]).astype(jnp.bfloat16)

    def put(m, h, out):
        o_ref[0, m, :, h * HEAD_DIM : (h + 1) * HEAD_DIM] = out

    def a_copy(m, h):
        return pltpu.make_async_remote_copy(
            src_ref=att.at[m, h],
            dst_ref=att.at[m, h],
            send_sem=a_send.at[m, h],
            recv_sem=a_recv.at[m, h],
            device_id=(1, dc, head),
            device_id_type=MESH,
        )

    def n_copy(m, h):
        return pltpu.make_async_remote_copy(
            src_ref=ss_out.at[m],
            dst_ref=ss_in.at[m, head],
            send_sem=n_send.at[m, h],
            recv_sem=n_recv.at[m, head],
            device_id=(1, dc, h),
            device_id_type=MESH,
        )

    def n_arrival(m, h):
        return pltpu.make_async_remote_copy(
            src_ref=ss_out.at[m],
            dst_ref=ss_in.at[m, h],
            send_sem=n_send.at[m, h],
            recv_sem=n_recv.at[m, h],
            device_id=(0, dc, h),
            device_id_type=MESH,
        )

    def stage_query(m, h, value):
        rows = slice(h * ROWS, (h + 1) * ROWS)
        qx[m, rows, :HEAD_DIM] = value
        qx[m, rows, HEAD_DIM:] = query_mask[m]

    def hand_over(m):
        squares = jnp.zeros((ROWS, HEAD_DIM), jnp.float32)
        for h in range(HEADS_LOCAL):
            out = finished(m, h)
            att[m, h] = out
            wide = out.astype(jnp.float32)
            squares = squares + wide * wide
        ss_out[m, :, :ROWS] = jnp.sum(jnp.transpose(squares), axis=0, keepdims=True)
        for h in range(N_HEAD):
            n_copy(m, h).start()
        for h in range(HEADS_LOCAL):
            a_copy(m, h).start()
        for h in range(HEADS_LOCAL):
            put(m, h, att[m, h])

    def fold_four(m, z_list):
        for z_at in z_list:
            wait_s(m, z_at)
        fold(m, z_list)

    def prepare(m):
        build_masks(m)
        loads[m][2].wait()

        @pl.when(seg == 0)
        def _():
            start_rows(m)
            for h in range(HEADS_LOCAL):
                stage_query(m, h, q_ref[m, :, h * HEAD_DIM : (h + 1) * HEAD_DIM])

    for m in range(MICRO):
        loads[m][0].wait()
        loads[m][1].wait()
        for z_at in range(NZ):
            @pl.when(z_at < z)
            def _():
                z_send_copy(m, z_at).start()
    for i in range(1, FAR):
        @pl.when(near(i) > z)
        def _():
            pl.semaphore_wait(z_in.at[near(i)], 1)
            for m in range(MICRO):
                z_send_copy(m, near(i)).start()

    for copy in small:
        copy.wait()
    prepare(0)

    @pl.when(xh == 0)
    def _():
        pl.semaphore_wait(x_in, 1)

    @pl.when(core == 1)
    def _():
        pl.semaphore_wait(s_in, 1)

    for m in range(MICRO):
        x_copy(m, z, xh).start()
    prepare(1)
    for i in range(1, FAR):
        for m in range(MICRO):
            pass_z(m, near(i))

    @pl.when(half == 0)
    def _():
        for i in range(FAR):
            pl.semaphore_wait(z_in.at[far(i)], 1)
            z_send_copy(0, far(i)).start()
        for i in range(FAR):
            z_send_copy(1, far(i)).start()

    for i in range(FAR - 1):
        for m in range(MICRO):
            pass_x(m, near(i))

    @pl.when(seg == 0)
    def _():
        pl.semaphore_wait(seg_in, 1)

        @pl.when(rank < N_HEAD - 1)
        def _():
            pl.semaphore_wait(y_in, N_HEAD - 1 - rank)

        for h in range(N_HEAD):
            @pl.when(head != h)
            def _():
                tell(y_all, (0, dc, h))

    for i in range(FAR):
        pass_z(0, far(i))
    for m in range(MICRO):
        pass_x(m, near(FAR - 1))
    for i in range(FAR):
        pass_z(1, far(i))

    nears = tuple(near(i) for i in range(FAR))
    fars = tuple(far(i) for i in range(FAR))

    @pl.when(seg == 0)
    def _():
        fold_four(0, nears)

    for i in range(FAR):
        pass_x(0, far(i))

    @pl.when(seg == 0)
    def _():
        fold_four(0, fars)
        pl.semaphore_wait(y_all, N_HEAD - 1)
        hand_over(0)
        fold_four(1, nears)

    for i in range(FAR):
        pass_x(1, far(i))

    @pl.when(seg == 0)
    def _():
        fold_four(1, fars)
        hand_over(1)
        for m in range(MICRO):
            for h in range(HEADS_LOCAL):
                a_copy(m, h).wait_send()
                n_copy(m, h).wait_send()

    @pl.when(seg == 1)
    def _():
        for m in range(MICRO):
            for z_at in range(NZ):
                wait_s(m, z_at)
        for m in range(MICRO):
            for h in range(N_HEAD):
                n_arrival(m, h).wait_recv()
            total = ss_in[m, 0]
            for h in range(1, N_HEAD):
                total = total + ss_in[m, h]
            wide_total = jnp.broadcast_to(total[:, :ROWS], (HEAD_DIM, ROWS))
            norm = lax.rsqrt(jnp.transpose(wide_total) / FEATURES + 1e-05)
            kx, vx = gathered(m, range(NZ))
            scores = []
            for rows in groups:
                for h in range(rows.start // ROWS, rows.stop // ROWS):
                    a_copy(m, h).wait_recv()
                    lifted = (
                        q_ref[m, :, h * HEAD_DIM : (h + 1) * HEAD_DIM].astype(jnp.float32)
                        + att[m, h].astype(jnp.float32) * norm
                    )
                    stage_query(m, h, lifted.astype(jnp.bfloat16))
                scores.append(score(m, rows, kx))
            for rows, one in zip(groups, scores):
                settle(m, vx, rows, one)
            for h in range(HEADS_LOCAL):
                put(m, h, finished(m, h))

    for m in range(MICRO):
        finish_sends(m)


def on_device(queries, keys, values, block_order, doc_lengths):
    dma = pltpu.SemaphoreType.DMA
    regular = pltpu.SemaphoreType.REGULAR
    rows = HEADS_LOCAL * ROWS
    operands = [
        pltpu.with_memory_space_constraint(one, pltpu.HBM)
        for one in (block_order, doc_lengths, queries, keys, values)
    ]
    return pl.pallas_call(
        kernel,
        out_shape=jax.ShapeDtypeStruct(queries.shape, jnp.bfloat16),
        in_specs=[pl.BlockSpec(memory_space=pltpu.HBM)] * 5,
        out_specs=pl.BlockSpec(memory_space=pltpu.VMEM),
        scratch_shapes=[
            pltpu.SMEM((MICRO, 64), jnp.int32),
            pltpu.SMEM((MICRO, DOCS), jnp.int32),
            pltpu.VMEM((MICRO, ROWS, HEADS_LOCAL * HEAD_DIM), jnp.bfloat16),
            pltpu.VMEM((MICRO, 2, NZ, 2, 2, ROWS, HEAD_DIM), jnp.bfloat16),
            pltpu.VMEM((MICRO, NZ, 2, 2, ROWS, 128), jnp.bfloat16),
            pltpu.VMEM((MICRO, ROWS, 128), jnp.bfloat16),
            pltpu.VMEM((MICRO, rows, 256), jnp.bfloat16),
            pltpu.VMEM((MICRO, rows, 256), jnp.float32),
            pltpu.VMEM((MICRO, rows, 128), jnp.float32),
            pltpu.VMEM((MICRO, HEADS_LOCAL, ROWS, HEAD_DIM), jnp.bfloat16),
            pltpu.VMEM((MICRO, 1, 128), jnp.float32),
            pltpu.VMEM((MICRO, N_HEAD, 1, 128), jnp.float32),
            dma((MICRO, 3)),
            dma((2,)),
            dma((MICRO, NZ)),
            dma((MICRO, NZ)),
            dma((MICRO, NZ)),
            dma((MICRO, NZ)),
            dma((MICRO, NZ)),
            dma((MICRO, NZ)),
            dma((MICRO, HEADS_LOCAL)),
            dma((MICRO, HEADS_LOCAL)),
            dma((MICRO, N_HEAD)),
            dma((MICRO, N_HEAD)),
            pltpu.SemaphoreType.REGULAR((NZ,)),
            regular,
            regular,
            regular,
            regular,
            regular,
        ],
        compiler_params=pltpu.CompilerParams(
            collective_id=0, has_side_effects=True, vmem_limit_bytes=48 * 1024 * 1024
        ),
        name="attend_two_layers",
    )(*operands)


def solution(mesh):
    placed = (
        P("segment", None, "dc", "head"),
        P("segment", None, "dc", "head"),
        P("segment", None, "dc", "head"),
        P(),
        P(),
    )
    return jax.shard_map(
        on_device,
        mesh=mesh,
        in_specs=placed,
        out_specs=P("segment", None, "dc", "head"),
        check_vma=False,
    )
```

```python
import math

import jax
import jax.numpy as jnp
from jax import lax
from jax.experimental import pallas as pl
from jax.experimental.pallas import tpu as pltpu
from jax.sharding import PartitionSpec as P

HEAD_DIM = 128
BLOCK = 32
MICRO = 2
DOCS = 16
HEADS_LOCAL = 8
N_HEAD = 8
ROWS = 64
FEATURES = 8192
NZ = 8
FAR = NZ // 2
HIDDEN = -1e30
MESH = pl.DeviceIdType.MESH
EXP_SCALE = math.log2(math.e) / math.sqrt(HEAD_DIM)
GROUP_ROWS = 256


def start_rank(head):
    if isinstance(head, int):
        return 2 * head - 1 if 1 <= head <= N_HEAD // 2 else 2 * ((N_HEAD - head) % N_HEAD)
    return jnp.where(
        (head >= 1) & (head <= N_HEAD // 2), 2 * head - 1, 2 * ((N_HEAD - head) % N_HEAD)
    )


def kernel(
    order_hbm,
    lengths_hbm,
    q_hbm,
    k_hbm,
    v_hbm,
    o_ref,
    order_ref,
    lengths_ref,
    q_ref,
    buf,
    key_mask,
    query_mask,
    qx,
    acc,
    peak,
    att,
    ss_out,
    ss_in,
    load_sem,
    small_sem,
    z_send,
    z_recv,
    r_send,
    x_send,
    x_recv,
    s_send,
    s_recv,
    a_send,
    a_recv,
    n_send,
    n_recv,
    z_in,
    x_in,
    s_in,
    seg_in,
    y_in,
    y_all,
):
    seg = lax.axis_index("segment")
    dc = lax.axis_index("dc")
    head = lax.axis_index("head")
    core = dc % 2
    z = (dc // 2) % NZ
    xh = dc // (2 * NZ)
    half = z // FAR
    side = (z % FAR) // 2
    rank = start_rank(head)

    def place(x_hi, z_at, core_at):
        return (x_hi * NZ + z_at) * 2 + core_at

    sibling = (seg, place(xh, z, 1 - core), head)
    x_peer = (seg, place(1 - xh, z, core), head)

    def z_peer(z_at):
        return (seg, place(xh, z_at, core), head)

    def tell(sem, device):
        pl.semaphore_signal(sem, inc=1, device_id=device, device_id_type=MESH)

    small = (
        pltpu.make_async_copy(order_hbm, order_ref, small_sem.at[0]),
        pltpu.make_async_copy(lengths_hbm, lengths_ref, small_sem.at[1]),
    )
    loads = []
    for m in range(MICRO):
        mine = buf.at[m, core, z, xh]
        loads.append(
            (
                pltpu.make_async_copy(k_hbm.at[0, m], mine.at[0], load_sem.at[m, 0]),
                pltpu.make_async_copy(v_hbm.at[0, m], mine.at[1], load_sem.at[m, 1]),
                pltpu.make_async_copy(q_hbm.at[0, m], q_ref.at[m], load_sem.at[m, 2]),
            )
        )
    for m in range(MICRO):
        loads[m][0].start()
        loads[m][1].start()
    for copy in small:
        copy.start()
    for m in range(MICRO):
        loads[m][2].start()

    def near(i):
        return half * FAR + (z + i) % FAR

    def far(i):
        return (1 - half) * FAR + jnp.where(i < 2, 1 - side, side) * 2 + (z + i) % 2

    def direct(i):
        return (side == 0) | (i < 2)

    def across(i):
        return half * FAR + (1 - side) * 2 + i

    barrier = pltpu.get_barrier_semaphore()
    for i in range(1, FAR):
        @pl.when(near(i) > z)
        def _():
            tell(barrier, z_peer(near(i)))
    for i in range(FAR):
        @pl.when((far(i) > z) & direct(i))
        def _():
            tell(barrier, z_peer(far(i)))

    @pl.when(xh == 0)
    def _():
        tell(barrier, x_peer)

    @pl.when(core == 1)
    def _():
        tell(barrier, sibling)

    @pl.when(seg == 0)
    def _():
        tell(barrier, (1, dc, head))
        for h in range(N_HEAD):
            @pl.when(start_rank(h) > rank)
            def _():
                tell(barrier, (0, dc, h))

    greetings = z % FAR + half * (4 - 2 * side) + xh + (1 - core) + seg + (1 - seg) * rank

    @pl.when(greetings > 0)
    def _():
        pl.semaphore_wait(barrier, greetings)

    for i in range(1, FAR):
        @pl.when(near(i) < z)
        def _():
            tell(z_in.at[z], z_peer(near(i)))
    for i in range(FAR):
        @pl.when((far(i) < z) & direct(i))
        def _():
            tell(z_in.at[z], z_peer(far(i)))

    @pl.when(xh == 1)
    def _():
        tell(x_in, x_peer)

    @pl.when(core == 0)
    def _():
        tell(s_in, sibling)

    @pl.when(seg == 1)
    def _():
        tell(seg_in, (0, dc, head))

    @pl.when(seg == 0)
    def _():
        for h in range(N_HEAD):
            @pl.when(start_rank(h) < rank)
            def _():
                tell(y_in, (0, dc, h))

    def z_send_copy(m, z_at):
        block = buf.at[m, core, z, xh]
        return pltpu.make_async_remote_copy(
            src_ref=block,
            dst_ref=block,
            send_sem=z_send.at[m, z_at],
            recv_sem=z_recv.at[m, z],
            device_id=z_peer(z_at),
            device_id_type=MESH,
        )

    def z_arrival(m, z_at):
        block = buf.at[m, core, z_at, xh]
        return pltpu.make_async_remote_copy(
            src_ref=block,
            dst_ref=block,
            send_sem=z_send.at[m, z_at],
            recv_sem=z_recv.at[m, z_at],
            device_id=z_peer(z_at),
            device_id_type=MESH,
        )

    def x_copy(m, z_at, x_at):
        block = buf.at[m, core, z_at, x_at]
        return pltpu.make_async_remote_copy(
            src_ref=block,
            dst_ref=block,
            send_sem=x_send.at[m, z_at],
            recv_sem=x_recv.at[m, z_at],
            device_id=x_peer,
            device_id_type=MESH,
        )

    def s_copy(m, z_at, core_at):
        block = buf.at[m, core_at, z_at]
        return pltpu.make_async_remote_copy(
            src_ref=block,
            dst_ref=block,
            send_sem=s_send.at[m, z_at],
            recv_sem=s_recv.at[m, z_at],
            device_id=sibling,
            device_id_type=MESH,
        )

    def relays():
        return z % FAR == 1

    def relay_copy(m, i, j):
        block = buf.at[m, core, far(i), xh]
        return pltpu.make_async_remote_copy(
            src_ref=block,
            dst_ref=block,
            send_sem=r_send.at[m, i, j],
            recv_sem=z_recv.at[m, far(i)],
            device_id=z_peer(across(j)),
            device_id_type=MESH,
        )

    def pass_far(m, i):
        z_arrival(m, far(i)).wait_recv()
        if i < 2:
            @pl.when(relays())
            def _():
                for j in range(2):
                    relay_copy(m, i, j).start()

        x_copy(m, far(i), xh).start()

    def pass_z(m, z_at):
        z_arrival(m, z_at).wait_recv()
        x_copy(m, z_at, xh).start()

    def pass_x(m, z_at):
        x_copy(m, z_at, 1 - xh).wait_recv()
        s_copy(m, z_at, core).start()

    def wait_s(m, z_at):
        s_copy(m, z_at, 1 - core).wait_recv()

    def finish_sends(m):
        for i in range(1, FAR):
            z_send_copy(m, near(i)).wait_send()
        for i in range(FAR):
            @pl.when(direct(i))
            def _():
                z_send_copy(m, far(i)).wait_send()

        @pl.when(relays())
        def _():
            for i in range(2):
                for j in range(2):
                    relay_copy(m, i, j).wait_send()

        for z_at in range(NZ):
            x_copy(m, z_at, xh).wait_send()
            s_copy(m, z_at, core).wait_send()

    def build_masks(m):
        lane = lax.broadcasted_iota(jnp.int32, (1, 128), 1)
        none = jnp.int32(1 << 20)
        low = jnp.full((1, 128), none, jnp.int32)
        high = jnp.zeros((1, 128), jnp.int32)
        run = jnp.int32(0)
        for d in range(DOCS):
            low = jnp.where(lane == d, run, low)
            run = run + lengths_ref[m, d]
            high = jnp.where(lane == d, run, high)
        for half in range(2):
            first = order_ref[m, dc * 2 + half] * BLOCK
            low = jnp.where(lane == DOCS + half, first + BLOCK, low)
            high = jnp.where(lane == DOCS + half, none, high)
            fine = (lane >= 32 + 32 * half) & (lane < 64 + 32 * half)
            low = jnp.where(fine, first + lane - (32 + 32 * half), low)
            high = jnp.where(fine, first + lane - (31 + 32 * half), high)
        high_q = jnp.where(lane < DOCS, high, none)
        row = lax.broadcasted_iota(jnp.int32, (BLOCK, 128), 0)
        for half in range(2):
            pos = order_ref[m, dc * 2 + half] * BLOCK + row
            hidden = (pos < low) | (pos >= high_q)
            query_mask[m, half * BLOCK : (half + 1) * BLOCK, :] = jnp.where(
                hidden, HIDDEN, 0.0
            ).astype(jnp.bfloat16)

        def one_z(z_at, carry):
            for c_at in range(2):
                for x_at in range(2):
                    for half in range(2):
                        number = place(x_at, z_at, c_at) * 2 + half
                        pos = order_ref[m, number] * BLOCK + row
                        inside = (pos >= low) & (pos < high)
                        key_mask[
                            m, z_at, c_at, x_at, half * BLOCK : (half + 1) * BLOCK, :
                        ] = jnp.where(inside, 1.0, 0.0).astype(jnp.bfloat16)
            return carry

        lax.fori_loop(0, NZ, one_z, 0)

    def start_rows(m):
        acc[m] = jnp.zeros((HEADS_LOCAL * ROWS, 256), jnp.float32)
        peak[m] = jnp.full((HEADS_LOCAL * ROWS, 128), HIDDEN, jnp.float32)

    def gathered(m, z_list):
        keys, values = [], []
        for z_at in z_list:
            k = buf[m, :, z_at, :, 0].reshape(256, HEAD_DIM)
            v = buf[m, :, z_at, :, 1].reshape(256, HEAD_DIM)
            b = key_mask[m, z_at].reshape(256, 128)
            keys.append(jnp.concatenate([k, b], axis=1))
            values.append(jnp.concatenate([v, jnp.ones_like(v)], axis=1))
        return jnp.concatenate(keys, axis=0), jnp.concatenate(values, axis=0)

    def score(m, rows, kx):
        return lax.dot_general(
            qx[m, rows, :], kx, (((1,), (1,)), ((), ())), preferred_element_type=jnp.float32
        )

    groups = [
        slice(start, start + GROUP_ROWS) for start in range(0, HEADS_LOCAL * ROWS, GROUP_ROWS)
    ]

    def fold(m, z_list):
        kx, vx = gathered(m, z_list)
        scores = [score(m, rows, kx) for rows in groups]
        for rows, one in zip(groups, scores):
            old = peak[m, rows, :]
            new = jnp.maximum(old, jnp.max(one, axis=1, keepdims=True))
            peak[m, rows, :] = new
            weights = jnp.exp2((one - new[:, :1]) * EXP_SCALE).astype(jnp.bfloat16)
            fade = jnp.exp2((old - new) * EXP_SCALE)
            acc[m, rows, :] = acc[m, rows, :] * jnp.concatenate([fade, fade], axis=1) + jnp.dot(
                weights, vx, preferred_element_type=jnp.float32
            )

    def settle(m, vx, rows, scores):
        top = jnp.max(scores, axis=1, keepdims=True)
        weights = jnp.exp2((scores - top) * EXP_SCALE).astype(jnp.bfloat16)
        acc[m, rows, :] = jnp.dot(weights, vx, preferred_element_type=jnp.float32)

    def finished(m, h):
        rows = slice(h * ROWS, (h + 1) * ROWS)
        return (acc[m, rows, :HEAD_DIM] / acc[m, rows, HEAD_DIM:]).astype(jnp.bfloat16)

    def put(m, h, out):
        o_ref[0, m, :, h * HEAD_DIM : (h + 1) * HEAD_DIM] = out

    def a_copy(m, h):
        return pltpu.make_async_remote_copy(
            src_ref=att.at[m, h],
            dst_ref=att.at[m, h],
            send_sem=a_send.at[m, h],
            recv_sem=a_recv.at[m, h],
            device_id=(1, dc, head),
            device_id_type=MESH,
        )

    def n_copy(m, h):
        return pltpu.make_async_remote_copy(
            src_ref=ss_out.at[m],
            dst_ref=ss_in.at[m, head],
            send_sem=n_send.at[m, h],
            recv_sem=n_recv.at[m, head],
            device_id=(1, dc, h),
            device_id_type=MESH,
        )

    def n_arrival(m, h):
        return pltpu.make_async_remote_copy(
            src_ref=ss_out.at[m],
            dst_ref=ss_in.at[m, h],
            send_sem=n_send.at[m, h],
            recv_sem=n_recv.at[m, h],
            device_id=(0, dc, h),
            device_id_type=MESH,
        )

    def stage_query(m, h, value):
        rows = slice(h * ROWS, (h + 1) * ROWS)
        qx[m, rows, :HEAD_DIM] = value
        qx[m, rows, HEAD_DIM:] = query_mask[m]

    def hand_over(m):
        squares = jnp.zeros((ROWS, HEAD_DIM), jnp.float32)
        for h in range(HEADS_LOCAL):
            out = finished(m, h)
            att[m, h] = out
            wide = out.astype(jnp.float32)
            squares = squares + wide * wide
        ss_out[m, :, :ROWS] = jnp.sum(jnp.transpose(squares), axis=0, keepdims=True)
        for h in range(N_HEAD):
            n_copy(m, h).start()
        for h in range(HEADS_LOCAL):
            a_copy(m, h).start()
        for h in range(HEADS_LOCAL):
            put(m, h, att[m, h])

    def fold_four(m, z_list):
        for z_at in z_list:
            wait_s(m, z_at)
        fold(m, z_list)

    def prepare(m):
        build_masks(m)
        loads[m][2].wait()

        @pl.when(seg == 0)
        def _():
            start_rows(m)
            for h in range(HEADS_LOCAL):
                stage_query(m, h, q_ref[m, :, h * HEAD_DIM : (h + 1) * HEAD_DIM])

    for m in range(MICRO):
        loads[m][0].wait()
        loads[m][1].wait()
        for i in range(FAR):
            @pl.when((far(i) < z) & direct(i))
            def _():
                z_send_copy(m, far(i)).start()
        for i in range(1, FAR):
            @pl.when(near(i) < z)
            def _():
                z_send_copy(m, near(i)).start()
    def answer_near(i):
        @pl.when(near(i) > z)
        def _():
            pl.semaphore_wait(z_in.at[near(i)], 1)
            for m in range(MICRO):
                z_send_copy(m, near(i)).start()

    for copy in small:
        copy.wait()
    prepare(0)
    answer_near(1)
    answer_near(2)

    @pl.when(xh == 0)
    def _():
        pl.semaphore_wait(x_in, 1)

    @pl.when(core == 1)
    def _():
        pl.semaphore_wait(s_in, 1)

    for m in range(MICRO):
        x_copy(m, z, xh).start()
    answer_near(3)
    prepare(1)
    for i in range(1, FAR):
        for m in range(MICRO):
            pass_z(m, near(i))

    @pl.when(half == 0)
    def _():
        for i in range(FAR):
            @pl.when(direct(i))
            def _():
                pl.semaphore_wait(z_in.at[far(i)], 1)
                z_send_copy(0, far(i)).start()
        for i in range(FAR):
            @pl.when(direct(i))
            def _():
                z_send_copy(1, far(i)).start()

    for i in range(FAR - 1):
        for m in range(MICRO):
            pass_x(m, near(i))

    @pl.when(seg == 0)
    def _():
        pl.semaphore_wait(seg_in, 1)

        @pl.when(rank < N_HEAD - 1)
        def _():
            pl.semaphore_wait(y_in, N_HEAD - 1 - rank)

        for h in range(N_HEAD):
            @pl.when(head != h)
            def _():
                tell(y_all, (0, dc, h))

    nears = tuple(near(i) for i in range(FAR))
    fars = tuple(far(i) for i in range(FAR))

    @pl.when(side == 0)
    def _():
        for i in range(FAR):
            pass_far(0, i)
        for i in range(2):
            pass_far(1, i)

    @pl.when(side == 1)
    def _():
        for m in range(MICRO):
            for i in range(2):
                pass_far(m, i)
        for i in range(2, FAR):
            pass_far(0, i)

    for m in range(MICRO):
        pass_x(m, near(FAR - 1))

    @pl.when(seg == 0)
    def _():
        fold_four(0, nears)

    for i in range(2, FAR):
        pass_far(1, i)
    for i in range(FAR):
        pass_x(0, far(i))

    @pl.when(seg == 0)
    def _():
        fold_four(1, nears)
        fold_four(0, fars)

    for i in range(2):
        pass_x(1, far(i))

    @pl.when(seg == 0)
    def _():
        pl.semaphore_wait(y_all, N_HEAD - 1)
        hand_over(0)

    for i in range(2, FAR):
        pass_x(1, far(i))

    @pl.when(seg == 0)
    def _():
        fold_four(1, fars)
        hand_over(1)
        for m in range(MICRO):
            for h in range(HEADS_LOCAL):
                a_copy(m, h).wait_send()
                n_copy(m, h).wait_send()

    @pl.when(seg == 1)
    def _():
        for m in range(MICRO):
            for z_at in range(NZ):
                wait_s(m, z_at)
        for m in range(MICRO):
            for h in range(N_HEAD):
                n_arrival(m, h).wait_recv()
            total = ss_in[m, 0]
            for h in range(1, N_HEAD):
                total = total + ss_in[m, h]
            wide_total = jnp.broadcast_to(total[:, :ROWS], (HEAD_DIM, ROWS))
            norm = lax.rsqrt(jnp.transpose(wide_total) / FEATURES + 1e-05)
            kx, vx = gathered(m, range(NZ))
            scores = []
            for rows in groups:
                for h in range(rows.start // ROWS, rows.stop // ROWS):
                    a_copy(m, h).wait_recv()
                    lifted = (
                        q_ref[m, :, h * HEAD_DIM : (h + 1) * HEAD_DIM].astype(jnp.float32)
                        + att[m, h].astype(jnp.float32) * norm
                    )
                    stage_query(m, h, lifted.astype(jnp.bfloat16))
                scores.append(score(m, rows, kx))
            for rows, one in zip(groups, scores):
                settle(m, vx, rows, one)
            for h in range(HEADS_LOCAL):
                put(m, h, finished(m, h))

    for m in range(MICRO):
        finish_sends(m)


def on_device(queries, keys, values, block_order, doc_lengths):
    dma = pltpu.SemaphoreType.DMA
    regular = pltpu.SemaphoreType.REGULAR
    rows = HEADS_LOCAL * ROWS
    operands = [
        pltpu.with_memory_space_constraint(one, pltpu.HBM)
        for one in (block_order, doc_lengths, queries, keys, values)
    ]
    return pl.pallas_call(
        kernel,
        out_shape=jax.ShapeDtypeStruct(queries.shape, jnp.bfloat16),
        in_specs=[pl.BlockSpec(memory_space=pltpu.HBM)] * 5,
        out_specs=pl.BlockSpec(memory_space=pltpu.VMEM),
        scratch_shapes=[
            pltpu.SMEM((MICRO, 64), jnp.int32),
            pltpu.SMEM((MICRO, DOCS), jnp.int32),
            pltpu.VMEM((MICRO, ROWS, HEADS_LOCAL * HEAD_DIM), jnp.bfloat16),
            pltpu.VMEM((MICRO, 2, NZ, 2, 2, ROWS, HEAD_DIM), jnp.bfloat16),
            pltpu.VMEM((MICRO, NZ, 2, 2, ROWS, 128), jnp.bfloat16),
            pltpu.VMEM((MICRO, ROWS, 128), jnp.bfloat16),
            pltpu.VMEM((MICRO, rows, 256), jnp.bfloat16),
            pltpu.VMEM((MICRO, rows, 256), jnp.float32),
            pltpu.VMEM((MICRO, rows, 128), jnp.float32),
            pltpu.VMEM((MICRO, HEADS_LOCAL, ROWS, HEAD_DIM), jnp.bfloat16),
            pltpu.VMEM((MICRO, 1, 128), jnp.float32),
            pltpu.VMEM((MICRO, N_HEAD, 1, 128), jnp.float32),
            dma((MICRO, 3)),
            dma((2,)),
            dma((MICRO, NZ)),
            dma((MICRO, NZ)),
            dma((MICRO, 2, 2)),
            dma((MICRO, NZ)),
            dma((MICRO, NZ)),
            dma((MICRO, NZ)),
            dma((MICRO, NZ)),
            dma((MICRO, HEADS_LOCAL)),
            dma((MICRO, HEADS_LOCAL)),
            dma((MICRO, N_HEAD)),
            dma((MICRO, N_HEAD)),
            pltpu.SemaphoreType.REGULAR((NZ,)),
            regular,
            regular,
            regular,
            regular,
            regular,
        ],
        compiler_params=pltpu.CompilerParams(
            collective_id=0, has_side_effects=True, vmem_limit_bytes=48 * 1024 * 1024
        ),
        name="attend_two_layers",
    )(*operands)


def solution(mesh):
    placed = (
        P("segment", None, "dc", "head"),
        P("segment", None, "dc", "head"),
        P("segment", None, "dc", "head"),
        P(),
        P(),
    )
    return jax.shard_map(
        on_device,
        mesh=mesh,
        in_specs=placed,
        out_specs=P("segment", None, "dc", "head"),
        check_vma=False,
    )
```

```python
import math

import jax
import jax.numpy as jnp
from jax import lax
from jax.experimental import pallas as pl
from jax.experimental.pallas import tpu as pltpu
from jax.sharding import PartitionSpec as P

HEAD_DIM = 128
BLOCK = 32
MICRO = 2
DOCS = 16
HEADS_LOCAL = 8
N_HEAD = 8
ROWS = 64
FEATURES = 8192
NZ = 8
FAR = NZ // 2
HIDDEN = -1e30
MESH = pl.DeviceIdType.MESH
EXP_SCALE = math.log2(math.e) / math.sqrt(HEAD_DIM)
GROUP_ROWS = 256
WINDOW = 1024 // BLOCK + 1


def start_rank(head):
    if isinstance(head, int):
        return 2 * head - 1 if 1 <= head <= N_HEAD // 2 else 2 * ((N_HEAD - head) % N_HEAD)
    return jnp.where(
        (head >= 1) & (head <= N_HEAD // 2), 2 * head - 1, 2 * ((N_HEAD - head) % N_HEAD)
    )


def kernel(
    order_hbm,
    lengths_hbm,
    q_hbm,
    k_hbm,
    v_hbm,
    o_ref,
    order_ref,
    lengths_ref,
    q_ref,
    buf,
    key_mask,
    query_mask,
    qx,
    acc,
    peak,
    att,
    ss_out,
    ss_in,
    inverse_v,
    inverse,
    k_win,
    v_win,
    b_win,
    load_sem,
    small_sem,
    inverse_sem,
    z_send,
    z_recv,
    r_send,
    x_send,
    x_recv,
    s_send,
    s_recv,
    a_send,
    a_recv,
    n_send,
    n_recv,
    z_in,
    x_in,
    s_in,
    seg_in,
    y_in,
    y_all,
):
    seg = lax.axis_index("segment")
    dc = lax.axis_index("dc")
    head = lax.axis_index("head")
    core = dc % 2
    z = (dc // 2) % NZ
    xh = dc // (2 * NZ)
    half = z // FAR
    side = (z % FAR) // 2
    rank = start_rank(head)

    def place(x_hi, z_at, core_at):
        return (x_hi * NZ + z_at) * 2 + core_at

    sibling = (seg, place(xh, z, 1 - core), head)
    x_peer = (seg, place(1 - xh, z, core), head)

    def z_peer(z_at):
        return (seg, place(xh, z_at, core), head)

    def tell(sem, device):
        pl.semaphore_signal(sem, inc=1, device_id=device, device_id_type=MESH)

    small = (
        pltpu.make_async_copy(order_hbm, order_ref, small_sem.at[0]),
        pltpu.make_async_copy(lengths_hbm, lengths_ref, small_sem.at[1]),
    )
    loads = []
    for m in range(MICRO):
        mine = buf.at[m, core, z, xh]
        loads.append(
            [
                pltpu.make_async_copy(
                    source.at[0, m, pl.ds(part * BLOCK, BLOCK)],
                    mine.at[which, part],
                    load_sem.at[m, which * 2 + part],
                )
                for which, source in enumerate((k_hbm, v_hbm))
                for part in range(2)
            ]
            + [pltpu.make_async_copy(q_hbm.at[0, m], q_ref.at[m], load_sem.at[m, 4])]
        )
    for m in range(MICRO):
        for one in loads[m][:4]:
            one.start()
    for copy in small:
        copy.start()
    for m in range(MICRO):
        loads[m][4].start()

    def near(i):
        return half * FAR + (z + i) % FAR

    def far(i):
        return (1 - half) * FAR + jnp.where(i < 2, 1 - side, side) * 2 + (z + i) % 2

    def direct(i):
        return (side == 0) | (i < 2)

    def across(i):
        return half * FAR + (1 - side) * 2 + i

    barrier = pltpu.get_barrier_semaphore()
    for i in range(1, FAR):
        @pl.when(near(i) > z)
        def _():
            tell(barrier, z_peer(near(i)))
    for i in range(FAR):
        @pl.when((far(i) > z) & direct(i))
        def _():
            tell(barrier, z_peer(far(i)))

    @pl.when(xh == 0)
    def _():
        tell(barrier, x_peer)

    @pl.when(core == 1)
    def _():
        tell(barrier, sibling)

    @pl.when(seg == 0)
    def _():
        tell(barrier, (1, dc, head))
        for h in range(N_HEAD):
            @pl.when(start_rank(h) > rank)
            def _():
                tell(barrier, (0, dc, h))

    greetings = z % FAR + half * (4 - 2 * side) + xh + (1 - core) + seg + (1 - seg) * rank

    @pl.when(greetings > 0)
    def _():
        pl.semaphore_wait(barrier, greetings)

    for i in range(1, FAR):
        @pl.when(near(i) < z)
        def _():
            tell(z_in.at[z], z_peer(near(i)))
    for i in range(FAR):
        @pl.when((far(i) < z) & direct(i))
        def _():
            tell(z_in.at[z], z_peer(far(i)))

    @pl.when(xh == 1)
    def _():
        tell(x_in, x_peer)

    @pl.when(core == 0)
    def _():
        tell(s_in, sibling)

    @pl.when(seg == 1)
    def _():
        tell(seg_in, (0, dc, head))

    @pl.when(seg == 0)
    def _():
        for h in range(N_HEAD):
            @pl.when(start_rank(h) < rank)
            def _():
                tell(y_in, (0, dc, h))

    def z_send_copy(m, z_at):
        block = buf.at[m, core, z, xh]
        return pltpu.make_async_remote_copy(
            src_ref=block,
            dst_ref=block,
            send_sem=z_send.at[m, z_at],
            recv_sem=z_recv.at[m, z],
            device_id=z_peer(z_at),
            device_id_type=MESH,
        )

    def z_arrival(m, z_at):
        block = buf.at[m, core, z_at, xh]
        return pltpu.make_async_remote_copy(
            src_ref=block,
            dst_ref=block,
            send_sem=z_send.at[m, z_at],
            recv_sem=z_recv.at[m, z_at],
            device_id=z_peer(z_at),
            device_id_type=MESH,
        )

    def x_copy(m, z_at, x_at):
        block = buf.at[m, core, z_at, x_at]
        return pltpu.make_async_remote_copy(
            src_ref=block,
            dst_ref=block,
            send_sem=x_send.at[m, z_at],
            recv_sem=x_recv.at[m, z_at],
            device_id=x_peer,
            device_id_type=MESH,
        )

    def s_copy(m, z_at, core_at):
        block = buf.at[m, core_at, z_at]
        return pltpu.make_async_remote_copy(
            src_ref=block,
            dst_ref=block,
            send_sem=s_send.at[m, z_at],
            recv_sem=s_recv.at[m, z_at],
            device_id=sibling,
            device_id_type=MESH,
        )

    def relays():
        return z % FAR == 1

    def relay_copy(m, i, j):
        block = buf.at[m, core, far(i), xh]
        return pltpu.make_async_remote_copy(
            src_ref=block,
            dst_ref=block,
            send_sem=r_send.at[m, i, j],
            recv_sem=z_recv.at[m, far(i)],
            device_id=z_peer(across(j)),
            device_id_type=MESH,
        )

    def pass_far(m, i):
        z_arrival(m, far(i)).wait_recv()
        if i < 2:
            @pl.when(relays())
            def _():
                for j in range(2):
                    relay_copy(m, i, j).start()

        x_copy(m, far(i), xh).start()

    def pass_z(m, z_at):
        z_arrival(m, z_at).wait_recv()
        x_copy(m, z_at, xh).start()

    def pass_x(m, z_at):
        x_copy(m, z_at, 1 - xh).wait_recv()
        s_copy(m, z_at, core).start()

    def wait_s(m, z_at):
        s_copy(m, z_at, 1 - core).wait_recv()

    def finish_sends(m):
        for i in range(1, FAR):
            z_send_copy(m, near(i)).wait_send()
        for i in range(FAR):
            @pl.when(direct(i))
            def _():
                z_send_copy(m, far(i)).wait_send()

        @pl.when(relays())
        def _():
            for i in range(2):
                for j in range(2):
                    relay_copy(m, i, j).wait_send()

        for z_at in range(NZ):
            x_copy(m, z_at, xh).wait_send()
            s_copy(m, z_at, core).wait_send()

    def build_masks(m):
        lane = lax.broadcasted_iota(jnp.int32, (1, 128), 1)
        none = jnp.int32(1 << 20)
        low = jnp.full((1, 128), none, jnp.int32)
        high = jnp.zeros((1, 128), jnp.int32)
        run = jnp.int32(0)
        for d in range(DOCS):
            low = jnp.where(lane == d, run, low)
            run = run + lengths_ref[m, d]
            high = jnp.where(lane == d, run, high)
        for half in range(2):
            first = order_ref[m, dc * 2 + half] * BLOCK
            low = jnp.where(lane == DOCS + half, first + BLOCK, low)
            high = jnp.where(lane == DOCS + half, none, high)
            fine = (lane >= 32 + 32 * half) & (lane < 64 + 32 * half)
            low = jnp.where(fine, first + lane - (32 + 32 * half), low)
            high = jnp.where(fine, first + lane - (31 + 32 * half), high)
        high_q = jnp.where(lane < DOCS, high, none)
        row = lax.broadcasted_iota(jnp.int32, (BLOCK, 128), 0)
        for half in range(2):
            pos = order_ref[m, dc * 2 + half] * BLOCK + row
            hidden = (pos < low) | (pos >= high_q)
            query_mask[m, half * BLOCK : (half + 1) * BLOCK, :] = jnp.where(
                hidden, HIDDEN, 0.0
            ).astype(jnp.bfloat16)

        def one_z(z_at, carry):
            for c_at in range(2):
                for x_at in range(2):
                    for half in range(2):
                        number = place(x_at, z_at, c_at) * 2 + half
                        pos = order_ref[m, number] * BLOCK + row
                        inside = (pos >= low) & (pos < high)
                        key_mask[m, z_at, c_at, x_at, half] = jnp.where(inside, 1.0, 0.0).astype(jnp.bfloat16)
            return carry

        lax.fori_loop(0, NZ, one_z, 0)

    def start_rows(m):
        acc[m] = jnp.zeros((HEADS_LOCAL * ROWS, 256), jnp.float32)
        peak[m] = jnp.full((HEADS_LOCAL * ROWS, 128), HIDDEN, jnp.float32)

    def gathered(m, z_list):
        keys, values = [], []
        for z_at in z_list:
            k = buf[m, :, z_at, :, 0].reshape(256, HEAD_DIM)
            v = buf[m, :, z_at, :, 1].reshape(256, HEAD_DIM)
            b = key_mask[m, z_at].reshape(256, 128)
            keys.append(jnp.concatenate([k, b], axis=1))
            values.append(jnp.concatenate([v, jnp.ones_like(v)], axis=1))
        return jnp.concatenate(keys, axis=0), jnp.concatenate(values, axis=0)

    def score(m, rows, kx):
        return lax.dot_general(
            qx[m, rows, :], kx, (((1,), (1,)), ((), ())), preferred_element_type=jnp.float32
        )

    groups = [
        slice(start, start + GROUP_ROWS) for start in range(0, HEADS_LOCAL * ROWS, GROUP_ROWS)
    ]

    def fold(m, z_list):
        kx, vx = gathered(m, z_list)
        scores = [score(m, rows, kx) for rows in groups]
        for rows, one in zip(groups, scores):
            old = peak[m, rows, :]
            new = jnp.maximum(old, jnp.max(one, axis=1, keepdims=True))
            peak[m, rows, :] = new
            weights = jnp.exp2((one - new[:, :1]) * EXP_SCALE).astype(jnp.bfloat16)
            fade = jnp.exp2((old - new) * EXP_SCALE)
            acc[m, rows, :] = acc[m, rows, :] * jnp.concatenate([fade, fade], axis=1) + jnp.dot(
                weights, vx, preferred_element_type=jnp.float32
            )

    def settle(m, vx, rows, scores):
        top = jnp.max(scores, axis=1, keepdims=True)
        weights = jnp.exp2((scores - top) * EXP_SCALE).astype(jnp.bfloat16)
        acc[m, rows, :] = jnp.dot(weights, vx, preferred_element_type=jnp.float32)

    def finished(m, h):
        rows = slice(h * ROWS, (h + 1) * ROWS)
        return (acc[m, rows, :HEAD_DIM] / acc[m, rows, HEAD_DIM:]).astype(jnp.bfloat16)

    def put(m, h, out):
        o_ref[0, m, :, h * HEAD_DIM : (h + 1) * HEAD_DIM] = out

    def a_copy(m, h):
        return pltpu.make_async_remote_copy(
            src_ref=att.at[m, h],
            dst_ref=att.at[m, h],
            send_sem=a_send.at[m, h],
            recv_sem=a_recv.at[m, h],
            device_id=(1, dc, head),
            device_id_type=MESH,
        )

    def n_copy(m, h):
        return pltpu.make_async_remote_copy(
            src_ref=ss_out.at[m],
            dst_ref=ss_in.at[m, head],
            send_sem=n_send.at[m, h],
            recv_sem=n_recv.at[m, head],
            device_id=(1, dc, h),
            device_id_type=MESH,
        )

    def n_arrival(m, h):
        return pltpu.make_async_remote_copy(
            src_ref=ss_out.at[m],
            dst_ref=ss_in.at[m, h],
            send_sem=n_send.at[m, h],
            recv_sem=n_recv.at[m, h],
            device_id=(0, dc, h),
            device_id_type=MESH,
        )

    def stage_query(m, h, value):
        rows = slice(h * ROWS, (h + 1) * ROWS)
        qx[m, rows, :HEAD_DIM] = value
        qx[m, rows, HEAD_DIM:] = query_mask[m]

    def hand_over(m):
        squares = jnp.zeros((ROWS, HEAD_DIM), jnp.float32)
        for h in range(HEADS_LOCAL):
            out = finished(m, h)
            att[m, h] = out
            wide = out.astype(jnp.float32)
            squares = squares + wide * wide
        ss_out[m, :, :ROWS] = jnp.sum(jnp.transpose(squares), axis=0, keepdims=True)
        for h in range(N_HEAD):
            n_copy(m, h).start()
        for h in range(HEADS_LOCAL):
            a_copy(m, h).start()
        for h in range(HEADS_LOCAL):
            put(m, h, att[m, h])

    def inverse_copy(m):
        return pltpu.make_async_copy(inverse_v.at[m], inverse.at[m], inverse_sem.at[m])

    def invert_order(m):
        lane = lax.broadcasted_iota(jnp.int32, (1, 128), 1)
        slot_block = jnp.zeros((1, 128), jnp.int32)
        for number in range(64):
            slot_block = jnp.where(lane == order_ref[m, number], number, slot_block)
        inverse_v[m] = slot_block
        inverse_copy(m).start()

    def cut_windows(m):
        for own in range(2):
            base = jnp.maximum(order_ref[m, dc * 2 + own] - (WINDOW - 1), 0)

            def one_block(j, carry, own=own, base=base):
                number = inverse[m, 0, base + j]
                c_at = (number >> 1) & 1
                z_at = (number >> 2) & (NZ - 1)
                x_at = number >> 5
                h_at = number & 1
                target = pl.ds(pl.multiple_of(j * BLOCK, BLOCK), BLOCK)
                k_win[m, own, target, :] = buf[m, c_at, z_at, x_at, 0, h_at]
                v_win[m, own, target, :] = buf[m, c_at, z_at, x_at, 1, h_at]
                b_win[m, own, target, :] = key_mask[m, z_at, c_at, x_at, h_at]
                return carry

            lax.fori_loop(0, WINDOW, one_block, 0, unroll=3)

    def fold_four(m, z_list):
        for z_at in z_list:
            wait_s(m, z_at)
        fold(m, z_list)

    def prepare(m):
        build_masks(m)
        loads[m][4].wait()

        @pl.when(seg == 1)
        def _():
            invert_order(m)

        @pl.when(seg == 0)
        def _():
            start_rows(m)
            for h in range(HEADS_LOCAL):
                stage_query(m, h, q_ref[m, :, h * HEAD_DIM : (h + 1) * HEAD_DIM])

    for m in range(MICRO):
        for one in loads[m][:4]:
            one.wait()
        for i in range(FAR):
            @pl.when((far(i) < z) & direct(i))
            def _():
                z_send_copy(m, far(i)).start()
        for i in range(1, FAR):
            @pl.when(near(i) < z)
            def _():
                z_send_copy(m, near(i)).start()
    def answer_near(i):
        @pl.when(near(i) > z)
        def _():
            pl.semaphore_wait(z_in.at[near(i)], 1)
            for m in range(MICRO):
                z_send_copy(m, near(i)).start()

    for copy in small:
        copy.wait()
    prepare(0)
    answer_near(1)
    answer_near(2)

    @pl.when(xh == 0)
    def _():
        pl.semaphore_wait(x_in, 1)

    @pl.when(core == 1)
    def _():
        pl.semaphore_wait(s_in, 1)

    for m in range(MICRO):
        x_copy(m, z, xh).start()
    answer_near(3)
    prepare(1)
    for i in range(1, FAR):
        for m in range(MICRO):
            pass_z(m, near(i))

    @pl.when(half == 0)
    def _():
        for i in range(FAR):
            @pl.when(direct(i))
            def _():
                pl.semaphore_wait(z_in.at[far(i)], 1)
                z_send_copy(0, far(i)).start()
        for i in range(FAR):
            @pl.when(direct(i))
            def _():
                z_send_copy(1, far(i)).start()

    for i in range(FAR - 1):
        for m in range(MICRO):
            pass_x(m, near(i))

    @pl.when(seg == 0)
    def _():
        pl.semaphore_wait(seg_in, 1)

        @pl.when(rank < N_HEAD - 1)
        def _():
            pl.semaphore_wait(y_in, N_HEAD - 1 - rank)

        for h in range(N_HEAD):
            @pl.when(head != h)
            def _():
                tell(y_all, (0, dc, h))

    nears = tuple(near(i) for i in range(FAR))
    fars = tuple(far(i) for i in range(FAR))

    @pl.when(side == 0)
    def _():
        for i in range(FAR):
            pass_far(0, i)
        for i in range(2):
            pass_far(1, i)

    @pl.when(side == 1)
    def _():
        for m in range(MICRO):
            for i in range(2):
                pass_far(m, i)
        for i in range(2, FAR):
            pass_far(0, i)

    for m in range(MICRO):
        pass_x(m, near(FAR - 1))

    pass_far(1, 2)
    pass_far(1, 3)
    pass_x(0, far(0))
    pass_x(0, far(1))
    @pl.when(seg == 0)
    def _():
        fold_four(0, nears)

    pass_x(0, far(2))
    pass_x(0, far(3))
    @pl.when(seg == 0)
    def _():
        fold_four(1, nears)

    @pl.when(seg == 0)
    def _():
        fold_four(0, fars)

    pass_x(1, far(0))
    pass_x(1, far(1))
    pass_x(1, far(2))
    @pl.when(seg == 0)
    def _():
        pl.semaphore_wait(y_all, N_HEAD - 1)
        hand_over(0)

    pass_x(1, far(3))
    @pl.when(seg == 0)
    def _():
        fold_four(1, fars)
        hand_over(1)
        for m in range(MICRO):
            for h in range(HEADS_LOCAL):
                a_copy(m, h).wait_send()
                n_copy(m, h).wait_send()

    @pl.when(seg == 1)
    def _():
        for m in range(MICRO):
            for z_at in range(NZ):
                wait_s(m, z_at)
            inverse_copy(m).wait()
        for m in range(MICRO):
            cut_windows(m)
            for h in range(N_HEAD):
                n_arrival(m, h).wait_recv()
            total = ss_in[m, 0]
            for h in range(1, N_HEAD):
                total = total + ss_in[m, h]
            wide_total = jnp.broadcast_to(total[:, :ROWS], (HEAD_DIM, ROWS))
            norm = lax.rsqrt(jnp.transpose(wide_total) / FEATURES + 1e-05)
            for h in range(HEADS_LOCAL):
                a_copy(m, h).wait_recv()
                lifted = (
                    q_ref[m, :, h * HEAD_DIM : (h + 1) * HEAD_DIM].astype(jnp.float32)
                    + att[m, h].astype(jnp.float32) * norm
                ).astype(jnp.bfloat16)
                for own in range(2):
                    rows = slice(own * GROUP_ROWS + h * BLOCK, own * GROUP_ROWS + (h + 1) * BLOCK)
                    part = slice(own * BLOCK, (own + 1) * BLOCK)
                    qx[m, rows, :HEAD_DIM] = lifted[part]
                    qx[m, rows, HEAD_DIM:] = query_mask[m, part, :]
            scores = []
            for own, rows in enumerate(groups):
                kx = jnp.concatenate([k_win[m, own], b_win[m, own]], axis=1)
                scores.append(score(m, rows, kx))
            for own, rows in enumerate(groups):
                values = v_win[m, own]
                vx = jnp.concatenate([values, jnp.ones_like(values)], axis=1)
                settle(m, vx, rows, scores[own])
            for h in range(HEADS_LOCAL):
                for own in range(2):
                    rows = slice(own * GROUP_ROWS + h * BLOCK, own * GROUP_ROWS + (h + 1) * BLOCK)
                    out = acc[m, rows, :HEAD_DIM] / acc[m, rows, HEAD_DIM:]
                    o_ref[
                        0, m, own * BLOCK : (own + 1) * BLOCK, h * HEAD_DIM : (h + 1) * HEAD_DIM
                    ] = out.astype(jnp.bfloat16)

    for m in range(MICRO):
        finish_sends(m)


def on_device(queries, keys, values, block_order, doc_lengths):
    dma = pltpu.SemaphoreType.DMA
    regular = pltpu.SemaphoreType.REGULAR
    rows = HEADS_LOCAL * ROWS
    operands = [
        pltpu.with_memory_space_constraint(one, pltpu.HBM)
        for one in (block_order, doc_lengths, queries, keys, values)
    ]
    return pl.pallas_call(
        kernel,
        out_shape=jax.ShapeDtypeStruct(queries.shape, jnp.bfloat16),
        in_specs=[pl.BlockSpec(memory_space=pltpu.HBM)] * 5,
        out_specs=pl.BlockSpec(memory_space=pltpu.VMEM),
        scratch_shapes=[
            pltpu.SMEM((MICRO, 64), jnp.int32),
            pltpu.SMEM((MICRO, DOCS), jnp.int32),
            pltpu.VMEM((MICRO, ROWS, HEADS_LOCAL * HEAD_DIM), jnp.bfloat16),
            pltpu.VMEM((MICRO, 2, NZ, 2, 2, 2, BLOCK, HEAD_DIM), jnp.bfloat16),
            pltpu.VMEM((MICRO, NZ, 2, 2, 2, BLOCK, 128), jnp.bfloat16),
            pltpu.VMEM((MICRO, ROWS, 128), jnp.bfloat16),
            pltpu.VMEM((MICRO, rows, 256), jnp.bfloat16),
            pltpu.VMEM((MICRO, rows, 256), jnp.float32),
            pltpu.VMEM((MICRO, rows, 128), jnp.float32),
            pltpu.VMEM((MICRO, HEADS_LOCAL, ROWS, HEAD_DIM), jnp.bfloat16),
            pltpu.VMEM((MICRO, 1, 128), jnp.float32),
            pltpu.VMEM((MICRO, N_HEAD, 1, 128), jnp.float32),
            pltpu.VMEM((MICRO, 1, 128), jnp.int32),
            pltpu.SMEM((MICRO, 1, 128), jnp.int32),
            pltpu.VMEM((MICRO, 2, WINDOW * BLOCK, HEAD_DIM), jnp.bfloat16),
            pltpu.VMEM((MICRO, 2, WINDOW * BLOCK, HEAD_DIM), jnp.bfloat16),
            pltpu.VMEM((MICRO, 2, WINDOW * BLOCK, 128), jnp.bfloat16),
            dma((MICRO, 5)),
            dma((2,)),
            dma((MICRO,)),
            dma((MICRO, NZ)),
            dma((MICRO, NZ)),
            dma((MICRO, 2, 2)),
            dma((MICRO, NZ)),
            dma((MICRO, NZ)),
            dma((MICRO, NZ)),
            dma((MICRO, NZ)),
            dma((MICRO, HEADS_LOCAL)),
            dma((MICRO, HEADS_LOCAL)),
            dma((MICRO, N_HEAD)),
            dma((MICRO, N_HEAD)),
            pltpu.SemaphoreType.REGULAR((NZ,)),
            regular,
            regular,
            regular,
            regular,
            regular,
        ],
        compiler_params=pltpu.CompilerParams(
            collective_id=0, has_side_effects=True, vmem_limit_bytes=48 * 1024 * 1024
        ),
        name="attend_two_layers",
    )(*operands)


def solution(mesh):
    placed = (
        P("segment", None, "dc", "head"),
        P("segment", None, "dc", "head"),
        P("segment", None, "dc", "head"),
        P(),
        P(),
    )
    return jax.shard_map(
        on_device,
        mesh=mesh,
        in_specs=placed,
        out_specs=P("segment", None, "dc", "head"),
        check_vma=False,
    )
```

```python
import math

import jax
import jax.numpy as jnp
from jax import lax
from jax.experimental import pallas as pl
from jax.experimental.pallas import tpu as pltpu
from jax.sharding import PartitionSpec as P

HEAD_DIM = 128
BLOCK = 32
MICRO = 2
DOCS = 16
HEADS_LOCAL = 8
N_HEAD = 8
ROWS = 64
FEATURES = 8192
NZ = 8
FAR = NZ // 2
HIDDEN = -1e30
MESH = pl.DeviceIdType.MESH
EXP_SCALE = math.log2(math.e) / math.sqrt(HEAD_DIM)
GROUP_ROWS = 256
WINDOW = 1024 // BLOCK + 1


def start_rank(head):
    if isinstance(head, int):
        return 2 * head - 1 if 1 <= head <= N_HEAD // 2 else 2 * ((N_HEAD - head) % N_HEAD)
    return jnp.where(
        (head >= 1) & (head <= N_HEAD // 2), 2 * head - 1, 2 * ((N_HEAD - head) % N_HEAD)
    )


def kernel(
    order_hbm,
    lengths_hbm,
    q_hbm,
    k_hbm,
    v_hbm,
    o_ref,
    order_ref,
    lengths_ref,
    q_ref,
    buf,
    key_mask,
    query_mask,
    qx,
    acc,
    peak,
    att,
    ss_out,
    ss_in,
    inverse_v,
    inverse,
    k_win,
    v_win,
    b_win,
    load_sem,
    small_sem,
    inverse_sem,
    z_send,
    z_recv,
    r_send,
    x_send,
    x_recv,
    s_send,
    s_recv,
    a_send,
    a_recv,
    n_send,
    n_recv,
    z_in,
    x_in,
    s_in,
    seg_in,
    y_in,
    y_all,
):
    seg = lax.axis_index("segment")
    dc = lax.axis_index("dc")
    head = lax.axis_index("head")
    core = dc % 2
    z = (dc // 2) % NZ
    xh = dc // (2 * NZ)
    half = z // FAR
    side = (z % FAR) // 2
    rank = start_rank(head)

    def place(x_hi, z_at, core_at):
        return (x_hi * NZ + z_at) * 2 + core_at

    sibling = (seg, place(xh, z, 1 - core), head)
    x_peer = (seg, place(1 - xh, z, core), head)

    def z_peer(z_at):
        return (seg, place(xh, z_at, core), head)

    def tell(sem, device):
        pl.semaphore_signal(sem, inc=1, device_id=device, device_id_type=MESH)

    small = (
        pltpu.make_async_copy(order_hbm, order_ref, small_sem.at[0]),
        pltpu.make_async_copy(lengths_hbm, lengths_ref, small_sem.at[1]),
    )
    loads = []
    for m in range(MICRO):
        mine = buf.at[m, core, z, xh]
        loads.append(
            [
                pltpu.make_async_copy(
                    source.at[0, m, pl.ds(part * BLOCK, BLOCK)],
                    mine.at[which, part],
                    load_sem.at[m, which * 2 + part],
                )
                for which, source in enumerate((k_hbm, v_hbm))
                for part in range(2)
            ]
            + [pltpu.make_async_copy(q_hbm.at[0, m], q_ref.at[m], load_sem.at[m, 4])]
        )
    for m in range(MICRO):
        for one in loads[m][:4]:
            one.start()
    for copy in small:
        copy.start()
    for m in range(MICRO):
        loads[m][4].start()

    def near(i):
        return half * FAR + (z + i) % FAR

    def far(i):
        return (1 - half) * FAR + jnp.where(i < 2, 1 - side, side) * 2 + (z + i) % 2

    def direct(i):
        return (side == 0) | (i < 2)

    def across(i):
        return half * FAR + (1 - side) * 2 + i

    barrier = pltpu.get_barrier_semaphore()
    for i in range(1, FAR):
        @pl.when(near(i) > z)
        def _():
            tell(barrier, z_peer(near(i)))
    for i in range(FAR):
        @pl.when((far(i) > z) & direct(i))
        def _():
            tell(barrier, z_peer(far(i)))

    @pl.when(xh == 0)
    def _():
        tell(barrier, x_peer)

    @pl.when(core == 1)
    def _():
        tell(barrier, sibling)

    @pl.when(seg == 0)
    def _():
        tell(barrier, (1, dc, head))
        for h in range(N_HEAD):
            @pl.when(start_rank(h) > rank)
            def _():
                tell(barrier, (0, dc, h))

    greetings = z % FAR + half * (4 - 2 * side) + xh + (1 - core) + seg + (1 - seg) * rank

    @pl.when(greetings > 0)
    def _():
        pl.semaphore_wait(barrier, greetings)

    for i in range(1, FAR):
        @pl.when(near(i) < z)
        def _():
            tell(z_in.at[z], z_peer(near(i)))
    for i in range(FAR):
        @pl.when((far(i) < z) & direct(i))
        def _():
            tell(z_in.at[z], z_peer(far(i)))

    @pl.when(xh == 1)
    def _():
        tell(x_in, x_peer)

    @pl.when(core == 0)
    def _():
        tell(s_in, sibling)

    @pl.when(seg == 1)
    def _():
        tell(seg_in, (0, dc, head))

    @pl.when(seg == 0)
    def _():
        for h in range(N_HEAD):
            @pl.when(start_rank(h) < rank)
            def _():
                tell(y_in, (0, dc, h))

    def z_send_copy(m, z_at):
        block = buf.at[m, core, z, xh]
        return pltpu.make_async_remote_copy(
            src_ref=block,
            dst_ref=block,
            send_sem=z_send.at[m, z_at],
            recv_sem=z_recv.at[m, z],
            device_id=z_peer(z_at),
            device_id_type=MESH,
        )

    def z_arrival(m, z_at):
        block = buf.at[m, core, z_at, xh]
        return pltpu.make_async_remote_copy(
            src_ref=block,
            dst_ref=block,
            send_sem=z_send.at[m, z_at],
            recv_sem=z_recv.at[m, z_at],
            device_id=z_peer(z_at),
            device_id_type=MESH,
        )

    def x_copy(m, z_at, x_at):
        block = buf.at[m, core, z_at, x_at]
        return pltpu.make_async_remote_copy(
            src_ref=block,
            dst_ref=block,
            send_sem=x_send.at[m, z_at],
            recv_sem=x_recv.at[m, z_at],
            device_id=x_peer,
            device_id_type=MESH,
        )

    def s_copy(m, z_at, core_at):
        block = buf.at[m, core_at, z_at]
        return pltpu.make_async_remote_copy(
            src_ref=block,
            dst_ref=block,
            send_sem=s_send.at[m, z_at],
            recv_sem=s_recv.at[m, z_at],
            device_id=sibling,
            device_id_type=MESH,
        )

    def relays():
        return z % FAR == 1

    def relay_copy(m, i, j):
        block = buf.at[m, core, far(i), xh]
        return pltpu.make_async_remote_copy(
            src_ref=block,
            dst_ref=block,
            send_sem=r_send.at[m, i, j],
            recv_sem=z_recv.at[m, far(i)],
            device_id=z_peer(across(j)),
            device_id_type=MESH,
        )

    def pass_far(m, i):
        z_arrival(m, far(i)).wait_recv()
        if i < 2:
            @pl.when(relays())
            def _():
                for j in range(2):
                    relay_copy(m, i, j).start()

        x_copy(m, far(i), xh).start()

    def pass_z(m, z_at):
        z_arrival(m, z_at).wait_recv()
        x_copy(m, z_at, xh).start()

    def pass_x(m, z_at):
        x_copy(m, z_at, 1 - xh).wait_recv()
        s_copy(m, z_at, core).start()

    def wait_s(m, z_at):
        s_copy(m, z_at, 1 - core).wait_recv()

    def finish_sends(m):
        for i in range(1, FAR):
            z_send_copy(m, near(i)).wait_send()
        for i in range(FAR):
            @pl.when(direct(i))
            def _():
                z_send_copy(m, far(i)).wait_send()

        @pl.when(relays())
        def _():
            for i in range(2):
                for j in range(2):
                    relay_copy(m, i, j).wait_send()

        for z_at in range(NZ):
            x_copy(m, z_at, xh).wait_send()
            s_copy(m, z_at, core).wait_send()

    def build_masks(m):
        lane = lax.broadcasted_iota(jnp.int32, (1, 128), 1)
        none = jnp.int32(1 << 20)
        low = jnp.full((1, 128), none, jnp.int32)
        high = jnp.zeros((1, 128), jnp.int32)
        run = jnp.int32(0)
        for d in range(DOCS):
            low = jnp.where(lane == d, run, low)
            run = run + lengths_ref[m, d]
            high = jnp.where(lane == d, run, high)
        for half in range(2):
            first = order_ref[m, dc * 2 + half] * BLOCK
            low = jnp.where(lane == DOCS + half, first + BLOCK, low)
            high = jnp.where(lane == DOCS + half, none, high)
            fine = (lane >= 32 + 32 * half) & (lane < 64 + 32 * half)
            low = jnp.where(fine, first + lane - (32 + 32 * half), low)
            high = jnp.where(fine, first + lane - (31 + 32 * half), high)
        high_q = jnp.where(lane < DOCS, high, none)
        row = lax.broadcasted_iota(jnp.int32, (BLOCK, 128), 0)
        for half in range(2):
            pos = order_ref[m, dc * 2 + half] * BLOCK + row
            hidden = (pos < low) | (pos >= high_q)
            query_mask[m, half * BLOCK : (half + 1) * BLOCK, :] = jnp.where(
                hidden, HIDDEN, 0.0
            ).astype(jnp.bfloat16)

        def one_z(z_at, carry):
            for c_at in range(2):
                for x_at in range(2):
                    for half in range(2):
                        number = place(x_at, z_at, c_at) * 2 + half
                        pos = order_ref[m, number] * BLOCK + row
                        inside = (pos >= low) & (pos < high)
                        key_mask[m, z_at, c_at, x_at, half] = jnp.where(inside, 1.0, 0.0).astype(jnp.bfloat16)
            return carry

        lax.fori_loop(0, NZ, one_z, 0)

    def start_rows(m):
        acc[m] = jnp.zeros((HEADS_LOCAL * ROWS, 256), jnp.float32)
        peak[m] = jnp.full((HEADS_LOCAL * ROWS, 128), HIDDEN, jnp.float32)

    def gathered(m, z_list):
        keys, values = [], []
        for z_at in z_list:
            k = buf[m, :, z_at, :, 0].reshape(256, HEAD_DIM)
            v = buf[m, :, z_at, :, 1].reshape(256, HEAD_DIM)
            b = key_mask[m, z_at].reshape(256, 128)
            keys.append(jnp.concatenate([k, b], axis=1))
            values.append(jnp.concatenate([v, jnp.ones_like(v)], axis=1))
        return jnp.concatenate(keys, axis=0), jnp.concatenate(values, axis=0)

    def score(m, rows, kx):
        return lax.dot_general(
            qx[m, rows, :], kx, (((1,), (1,)), ((), ())), preferred_element_type=jnp.float32
        )

    groups = [
        slice(start, start + GROUP_ROWS) for start in range(0, HEADS_LOCAL * ROWS, GROUP_ROWS)
    ]

    def fold(m, z_list, last=False):
        kx, vx = gathered(m, z_list)
        scores = [score(m, rows, kx) for rows in groups]
        for rows, one in zip(groups, scores):
            old = peak[m, rows, :]
            new = jnp.maximum(old, jnp.max(one, axis=1, keepdims=True))
            peak[m, rows, :] = new
            weights = jnp.exp2((one - new[:, :1]) * EXP_SCALE).astype(jnp.bfloat16)
            fade = jnp.exp2((old - new) * EXP_SCALE)
            mixed = acc[m, rows, :] * jnp.concatenate([fade, fade], axis=1) + jnp.dot(
                weights, vx, preferred_element_type=jnp.float32
            )
            if last:
                out = (mixed[:, :HEAD_DIM] / mixed[:, HEAD_DIM:]).astype(jnp.bfloat16)
                for part in range(GROUP_ROWS // ROWS):
                    att[m, rows.start // ROWS + part] = out[part * ROWS : (part + 1) * ROWS]
            else:
                acc[m, rows, :] = mixed

    def settle(vx, scores):
        top = jnp.max(scores, axis=1, keepdims=True)
        weights = jnp.exp2((scores - top) * EXP_SCALE).astype(jnp.bfloat16)
        mixed = jnp.dot(weights, vx, preferred_element_type=jnp.float32)
        return (mixed[:, :HEAD_DIM] / mixed[:, HEAD_DIM:]).astype(jnp.bfloat16)

    def put(m, h, out):
        o_ref[0, m, :, h * HEAD_DIM : (h + 1) * HEAD_DIM] = out

    def a_copy(m, h):
        return pltpu.make_async_remote_copy(
            src_ref=att.at[m, h],
            dst_ref=att.at[m, h],
            send_sem=a_send.at[m, h],
            recv_sem=a_recv.at[m, h],
            device_id=(1, dc, head),
            device_id_type=MESH,
        )

    def n_copy(m, h):
        return pltpu.make_async_remote_copy(
            src_ref=ss_out.at[m],
            dst_ref=ss_in.at[m, head],
            send_sem=n_send.at[m, h],
            recv_sem=n_recv.at[m, head],
            device_id=(1, dc, h),
            device_id_type=MESH,
        )

    def n_arrival(m, h):
        return pltpu.make_async_remote_copy(
            src_ref=ss_out.at[m],
            dst_ref=ss_in.at[m, h],
            send_sem=n_send.at[m, h],
            recv_sem=n_recv.at[m, h],
            device_id=(0, dc, h),
            device_id_type=MESH,
        )

    def stage_query(m, h, value):
        rows = slice(h * ROWS, (h + 1) * ROWS)
        qx[m, rows, :HEAD_DIM] = value
        qx[m, rows, HEAD_DIM:] = query_mask[m]

    def hand_over(m):
        squares = jnp.zeros((ROWS, HEAD_DIM), jnp.float32)
        for h in range(HEADS_LOCAL):
            wide = att[m, h].astype(jnp.float32)
            squares = squares + wide * wide
        ss_out[m, :, :ROWS] = jnp.sum(jnp.transpose(squares), axis=0, keepdims=True)
        for h in range(N_HEAD):
            n_copy(m, h).start()
        for h in range(HEADS_LOCAL):
            a_copy(m, h).start()
        for h in range(HEADS_LOCAL):
            put(m, h, att[m, h])

    def inverse_copy(m):
        return pltpu.make_async_copy(inverse_v.at[m], inverse.at[m], inverse_sem.at[m])

    def invert_order(m):
        lane = lax.broadcasted_iota(jnp.int32, (1, 128), 1)
        slot_block = jnp.zeros((1, 128), jnp.int32)
        for number in range(64):
            slot_block = jnp.where(lane == order_ref[m, number], number, slot_block)
        inverse_v[m] = slot_block
        inverse_copy(m).start()

    def cut_windows(m):
        for own in range(2):
            base = jnp.maximum(order_ref[m, dc * 2 + own] - (WINDOW - 1), 0)

            def one_block(j, carry, own=own, base=base):
                number = inverse[m, 0, base + j]
                c_at = (number >> 1) & 1
                z_at = (number >> 2) & (NZ - 1)
                x_at = number >> 5
                h_at = number & 1
                target = pl.ds(pl.multiple_of(j * BLOCK, BLOCK), BLOCK)
                k_win[m, own, target, :] = buf[m, c_at, z_at, x_at, 0, h_at]
                v_win[m, own, target, :] = buf[m, c_at, z_at, x_at, 1, h_at]
                b_win[m, own, target, :] = key_mask[m, z_at, c_at, x_at, h_at]
                return carry

            lax.fori_loop(0, WINDOW, one_block, 0, unroll=3)

    def fold_four(m, z_list, last=False):
        for z_at in z_list:
            wait_s(m, z_at)
        fold(m, z_list, last)

    def prepare(m):
        build_masks(m)
        loads[m][4].wait()

        @pl.when(seg == 1)
        def _():
            invert_order(m)

        @pl.when(seg == 0)
        def _():
            start_rows(m)
            for h in range(HEADS_LOCAL):
                stage_query(m, h, q_ref[m, :, h * HEAD_DIM : (h + 1) * HEAD_DIM])

    for m in range(MICRO):
        for one in loads[m][:4]:
            one.wait()
        for i in (2, 3, 0, 1):
            @pl.when((far(i) < z) & direct(i))
            def _():
                z_send_copy(m, far(i)).start()
    for m in range(MICRO):
        for i in range(1, FAR):
            @pl.when(near(i) < z)
            def _():
                z_send_copy(m, near(i)).start()
    @pl.when(xh == 1)
    def _():
        for m in range(MICRO):
            x_copy(m, z, xh).start()

    def answer_near(i):
        @pl.when(near(i) > z)
        def _():
            pl.semaphore_wait(z_in.at[near(i)], 1)
            for m in range(MICRO):
                z_send_copy(m, near(i)).start()

    for copy in small:
        copy.wait()
    prepare(0)
    answer_near(1)
    answer_near(2)

    @pl.when(xh == 0)
    def _():
        pl.semaphore_wait(x_in, 1)

        for m in range(MICRO):
            x_copy(m, z, xh).start()

    @pl.when(core == 1)
    def _():
        pl.semaphore_wait(s_in, 1)

    answer_near(3)
    prepare(1)
    for i in range(1, FAR):
        for m in range(MICRO):
            pass_z(m, near(i))

    @pl.when(half == 0)
    def _():
        for i in range(FAR):
            @pl.when(direct(i))
            def _():
                pl.semaphore_wait(z_in.at[far(i)], 1)
                z_send_copy(0, far(i)).start()
        for i in range(FAR):
            @pl.when(direct(i))
            def _():
                z_send_copy(1, far(i)).start()

    for i in range(FAR - 1):
        for m in range(MICRO):
            pass_x(m, near(i))

    @pl.when(seg == 0)
    def _():
        pl.semaphore_wait(seg_in, 1)

        @pl.when(rank < N_HEAD - 1)
        def _():
            pl.semaphore_wait(y_in, N_HEAD - 1 - rank)

        for h in range(N_HEAD):
            @pl.when(head != h)
            def _():
                tell(y_all, (0, dc, h))

    nears = tuple(near(i) for i in range(FAR))
    fars = tuple(far(i) for i in range(FAR))

    @pl.when(side == 0)
    def _():
        for i in range(FAR):
            pass_far(0, i)
        for i in range(2):
            pass_far(1, i)

    @pl.when(side == 1)
    def _():
        for m in range(MICRO):
            for i in range(2):
                pass_far(m, i)
        for i in range(2, FAR):
            pass_far(0, i)

    for m in range(MICRO):
        pass_x(m, near(FAR - 1))

    pass_far(1, 2)
    pass_far(1, 3)
    pass_x(0, far(0))
    pass_x(0, far(1))
    @pl.when(seg == 0)
    def _():
        fold_four(0, nears)

    pass_x(0, far(2))
    pass_x(0, far(3))
    @pl.when(seg == 0)
    def _():
        fold_four(1, nears)

    @pl.when(seg == 0)
    def _():
        fold_four(0, fars, last=True)

    pass_x(1, far(0))
    pass_x(1, far(1))
    pass_x(1, far(2))
    @pl.when(seg == 0)
    def _():
        pl.semaphore_wait(y_all, N_HEAD - 1)
        hand_over(0)

    pass_x(1, far(3))
    @pl.when(seg == 0)
    def _():
        fold_four(1, fars, last=True)
        hand_over(1)
        for m in range(MICRO):
            for h in range(HEADS_LOCAL):
                a_copy(m, h).wait_send()
                n_copy(m, h).wait_send()

    @pl.when(seg == 1)
    def _():
        for m in range(MICRO):
            for z_at in range(NZ):
                wait_s(m, z_at)
            inverse_copy(m).wait()
        for m in range(MICRO):
            cut_windows(m)
            for own in range(2):
                part = slice(own * BLOCK, (own + 1) * BLOCK)
                for h in range(HEADS_LOCAL):
                    rows = slice(own * GROUP_ROWS + h * BLOCK, own * GROUP_ROWS + (h + 1) * BLOCK)
                    qx[m, rows, HEAD_DIM:] = query_mask[m, part, :]
            for h in range(N_HEAD):
                n_arrival(m, h).wait_recv()
            total = ss_in[m, 0]
            for h in range(1, N_HEAD):
                total = total + ss_in[m, h]
            wide_total = jnp.broadcast_to(total[:, :ROWS], (HEAD_DIM, ROWS))
            norm = lax.rsqrt(jnp.transpose(wide_total) / FEATURES + 1e-05)
            for h in range(HEADS_LOCAL):
                a_copy(m, h).wait_recv()
                lifted = (
                    q_ref[m, :, h * HEAD_DIM : (h + 1) * HEAD_DIM].astype(jnp.float32)
                    + att[m, h].astype(jnp.float32) * norm
                ).astype(jnp.bfloat16)
                for own in range(2):
                    rows = slice(own * GROUP_ROWS + h * BLOCK, own * GROUP_ROWS + (h + 1) * BLOCK)
                    part = slice(own * BLOCK, (own + 1) * BLOCK)
                    qx[m, rows, :HEAD_DIM] = lifted[part]
            scores = []
            for own, rows in enumerate(groups):
                kx = jnp.concatenate([k_win[m, own], b_win[m, own]], axis=1)
                scores.append(score(m, rows, kx))
            for own, rows in enumerate(groups):
                values = v_win[m, own]
                vx = jnp.concatenate([values, jnp.ones_like(values)], axis=1)
                out = settle(vx, scores[own])
                for h in range(HEADS_LOCAL):
                    o_ref[
                        0, m, own * BLOCK : (own + 1) * BLOCK, h * HEAD_DIM : (h + 1) * HEAD_DIM
                    ] = out[h * BLOCK : (h + 1) * BLOCK]

    for m in range(MICRO):
        finish_sends(m)


def on_device(queries, keys, values, block_order, doc_lengths):
    dma = pltpu.SemaphoreType.DMA
    regular = pltpu.SemaphoreType.REGULAR
    rows = HEADS_LOCAL * ROWS
    operands = [
        pltpu.with_memory_space_constraint(one, pltpu.HBM)
        for one in (block_order, doc_lengths, queries, keys, values)
    ]
    return pl.pallas_call(
        kernel,
        out_shape=jax.ShapeDtypeStruct(queries.shape, jnp.bfloat16),
        in_specs=[pl.BlockSpec(memory_space=pltpu.HBM)] * 5,
        out_specs=pl.BlockSpec(memory_space=pltpu.VMEM),
        scratch_shapes=[
            pltpu.SMEM((MICRO, 64), jnp.int32),
            pltpu.SMEM((MICRO, DOCS), jnp.int32),
            pltpu.VMEM((MICRO, ROWS, HEADS_LOCAL * HEAD_DIM), jnp.bfloat16),
            pltpu.VMEM((MICRO, 2, NZ, 2, 2, 2, BLOCK, HEAD_DIM), jnp.bfloat16),
            pltpu.VMEM((MICRO, NZ, 2, 2, 2, BLOCK, 128), jnp.bfloat16),
            pltpu.VMEM((MICRO, ROWS, 128), jnp.bfloat16),
            pltpu.VMEM((MICRO, rows, 256), jnp.bfloat16),
            pltpu.VMEM((MICRO, rows, 256), jnp.float32),
            pltpu.VMEM((MICRO, rows, 128), jnp.float32),
            pltpu.VMEM((MICRO, HEADS_LOCAL, ROWS, HEAD_DIM), jnp.bfloat16),
            pltpu.VMEM((MICRO, 1, 128), jnp.float32),
            pltpu.VMEM((MICRO, N_HEAD, 1, 128), jnp.float32),
            pltpu.VMEM((MICRO, 1, 128), jnp.int32),
            pltpu.SMEM((MICRO, 1, 128), jnp.int32),
            pltpu.VMEM((MICRO, 2, WINDOW * BLOCK, HEAD_DIM), jnp.bfloat16),
            pltpu.VMEM((MICRO, 2, WINDOW * BLOCK, HEAD_DIM), jnp.bfloat16),
            pltpu.VMEM((MICRO, 2, WINDOW * BLOCK, 128), jnp.bfloat16),
            dma((MICRO, 5)),
            dma((2,)),
            dma((MICRO,)),
            dma((MICRO, NZ)),
            dma((MICRO, NZ)),
            dma((MICRO, 2, 2)),
            dma((MICRO, NZ)),
            dma((MICRO, NZ)),
            dma((MICRO, NZ)),
            dma((MICRO, NZ)),
            dma((MICRO, HEADS_LOCAL)),
            dma((MICRO, HEADS_LOCAL)),
            dma((MICRO, N_HEAD)),
            dma((MICRO, N_HEAD)),
            pltpu.SemaphoreType.REGULAR((NZ,)),
            regular,
            regular,
            regular,
            regular,
            regular,
        ],
        compiler_params=pltpu.CompilerParams(
            collective_id=0, has_side_effects=True, vmem_limit_bytes=48 * 1024 * 1024
        ),
        name="attend_two_layers",
    )(*operands)


def solution(mesh):
    placed = (
        P("segment", None, "dc", "head"),
        P("segment", None, "dc", "head"),
        P("segment", None, "dc", "head"),
        P(),
        P(),
    )
    return jax.shard_map(
        on_device,
        mesh=mesh,
        in_specs=placed,
        out_specs=P("segment", None, "dc", "head"),
        check_vma=False,
    )
```

```python
import math

import jax
import jax.numpy as jnp
from jax import lax
from jax.experimental import pallas as pl
from jax.experimental.pallas import tpu as pltpu
from jax.sharding import PartitionSpec as P

HEAD_DIM = 128
BLOCK = 32
MICRO = 2
DOCS = 16
HEADS_LOCAL = 8
N_HEAD = 8
ROWS = 64
FEATURES = 8192
NZ = 8
FAR = NZ // 2
HIDDEN = -1e30
MESH = pl.DeviceIdType.MESH
EXP_SCALE = math.log2(math.e) / math.sqrt(HEAD_DIM)
GROUP_ROWS = 256
WINDOW = 1024 // BLOCK + 1


def start_rank(head):
    if isinstance(head, int):
        return 2 * head - 1 if 1 <= head <= N_HEAD // 2 else 2 * ((N_HEAD - head) % N_HEAD)
    return jnp.where(
        (head >= 1) & (head <= N_HEAD // 2), 2 * head - 1, 2 * ((N_HEAD - head) % N_HEAD)
    )


def kernel(
    order_hbm,
    lengths_hbm,
    q_hbm,
    k_hbm,
    v_hbm,
    o_ref,
    order_ref,
    lengths_ref,
    q_ref,
    buf,
    key_mask,
    query_mask,
    qx,
    acc,
    peak,
    att,
    ss_out,
    ss_in,
    inverse_v,
    inverse,
    k_win,
    v_win,
    b_win,
    load_sem,
    small_sem,
    inverse_sem,
    z_send,
    z_recv,
    r_send,
    x_send,
    x_recv,
    s_send,
    s_recv,
    a_send,
    a_recv,
    n_send,
    n_recv,
    z_in,
    x_in,
    s_in,
    seg_in,
    y_in,
    y_all,
):
    seg = lax.axis_index("segment")
    dc = lax.axis_index("dc")
    head = lax.axis_index("head")
    core = dc % 2
    z = (dc // 2) % NZ
    xh = dc // (2 * NZ)
    half = z // FAR
    side = (z % FAR) // 2
    rank = start_rank(head)

    def place(x_hi, z_at, core_at):
        return (x_hi * NZ + z_at) * 2 + core_at

    sibling = (seg, place(xh, z, 1 - core), head)
    x_peer = (seg, place(1 - xh, z, core), head)

    def z_peer(z_at):
        return (seg, place(xh, z_at, core), head)

    def tell(sem, device):
        pl.semaphore_signal(sem, inc=1, device_id=device, device_id_type=MESH)

    small = (
        pltpu.make_async_copy(order_hbm, order_ref, small_sem.at[0]),
        pltpu.make_async_copy(lengths_hbm, lengths_ref, small_sem.at[1]),
    )
    loads = []
    for m in range(MICRO):
        mine = buf.at[m, core, z, xh]
        loads.append(
            [
                pltpu.make_async_copy(
                    source.at[0, m, pl.ds(part * BLOCK, BLOCK)],
                    mine.at[which, part],
                    load_sem.at[m, which * 2 + part],
                )
                for which, source in enumerate((k_hbm, v_hbm))
                for part in range(2)
            ]
            + [pltpu.make_async_copy(q_hbm.at[0, m], q_ref.at[m], load_sem.at[m, 4])]
        )
    for m in range(MICRO):
        for one in loads[m][:4]:
            one.start()
    for copy in small:
        copy.start()
    for m in range(MICRO):
        loads[m][4].start()

    def near(i):
        return half * FAR + (z + i) % FAR

    def far(i):
        return (1 - half) * FAR + jnp.where(i < 2, 1 - side, side) * 2 + (z + i) % 2

    def direct(i):
        return (side == 0) | (i < 2)

    def across(i):
        return half * FAR + (1 - side) * 2 + i

    barrier = pltpu.get_barrier_semaphore()
    for i in range(1, FAR):
        @pl.when(near(i) > z)
        def _():
            tell(barrier, z_peer(near(i)))
    for i in range(FAR):
        @pl.when((far(i) > z) & direct(i))
        def _():
            tell(barrier, z_peer(far(i)))

    @pl.when(xh == 0)
    def _():
        tell(barrier, x_peer)

    @pl.when(core == 1)
    def _():
        tell(barrier, sibling)

    @pl.when(seg == 0)
    def _():
        tell(barrier, (1, dc, head))
        for h in range(N_HEAD):
            @pl.when(start_rank(h) > rank)
            def _():
                tell(barrier, (0, dc, h))

    greetings = z % FAR + half * (4 - 2 * side) + xh + (1 - core) + seg + (1 - seg) * rank

    @pl.when(greetings > 0)
    def _():
        pl.semaphore_wait(barrier, greetings)

    for i in range(1, FAR):
        @pl.when(near(i) < z)
        def _():
            tell(z_in.at[z], z_peer(near(i)))
    for i in range(FAR):
        @pl.when((far(i) < z) & direct(i))
        def _():
            tell(z_in.at[z], z_peer(far(i)))

    @pl.when(xh == 1)
    def _():
        tell(x_in, x_peer)

    @pl.when(core == 0)
    def _():
        tell(s_in, sibling)

    @pl.when(seg == 1)
    def _():
        tell(seg_in, (0, dc, head))

    @pl.when(seg == 0)
    def _():
        for h in range(N_HEAD):
            @pl.when(start_rank(h) < rank)
            def _():
                tell(y_in, (0, dc, h))

    def z_send_copy(m, z_at):
        block = buf.at[m, core, z, xh]
        return pltpu.make_async_remote_copy(
            src_ref=block,
            dst_ref=block,
            send_sem=z_send.at[m, z_at],
            recv_sem=z_recv.at[m, z],
            device_id=z_peer(z_at),
            device_id_type=MESH,
        )

    def z_arrival(m, z_at):
        block = buf.at[m, core, z_at, xh]
        return pltpu.make_async_remote_copy(
            src_ref=block,
            dst_ref=block,
            send_sem=z_send.at[m, z_at],
            recv_sem=z_recv.at[m, z_at],
            device_id=z_peer(z_at),
            device_id_type=MESH,
        )

    def x_copy(m, z_at, x_at):
        block = buf.at[m, core, z_at, x_at]
        return pltpu.make_async_remote_copy(
            src_ref=block,
            dst_ref=block,
            send_sem=x_send.at[m, z_at],
            recv_sem=x_recv.at[m, z_at],
            device_id=x_peer,
            device_id_type=MESH,
        )

    def s_copy(m, z_at, core_at):
        block = buf.at[m, core_at, z_at]
        return pltpu.make_async_remote_copy(
            src_ref=block,
            dst_ref=block,
            send_sem=s_send.at[m, z_at],
            recv_sem=s_recv.at[m, z_at],
            device_id=sibling,
            device_id_type=MESH,
        )

    def relays():
        return z % FAR == 1

    def relay_copy(m, i, j):
        block = buf.at[m, core, far(i), xh]
        return pltpu.make_async_remote_copy(
            src_ref=block,
            dst_ref=block,
            send_sem=r_send.at[m, i, j],
            recv_sem=z_recv.at[m, far(i)],
            device_id=z_peer(across(j)),
            device_id_type=MESH,
        )

    def pass_far(m, i):
        z_arrival(m, far(i)).wait_recv()
        if i < 2:
            @pl.when(relays())
            def _():
                for j in range(2):
                    relay_copy(m, i, j).start()

        x_copy(m, far(i), xh).start()

    def pass_z(m, z_at):
        z_arrival(m, z_at).wait_recv()
        x_copy(m, z_at, xh).start()

    def pass_x(m, z_at):
        x_copy(m, z_at, 1 - xh).wait_recv()
        s_copy(m, z_at, core).start()

    def wait_s(m, z_at):
        s_copy(m, z_at, 1 - core).wait_recv()

    def finish_sends(m):
        for i in range(1, FAR):
            z_send_copy(m, near(i)).wait_send()
        for i in range(FAR):
            @pl.when(direct(i))
            def _():
                z_send_copy(m, far(i)).wait_send()

        @pl.when(relays())
        def _():
            for i in range(2):
                for j in range(2):
                    relay_copy(m, i, j).wait_send()

        for z_at in range(NZ):
            x_copy(m, z_at, xh).wait_send()
            s_copy(m, z_at, core).wait_send()

    def build_masks(m):
        lane = lax.broadcasted_iota(jnp.int32, (1, 128), 1)
        none = jnp.int32(1 << 20)
        low = jnp.full((1, 128), none, jnp.int32)
        high = jnp.zeros((1, 128), jnp.int32)
        run = jnp.int32(0)
        for d in range(DOCS):
            low = jnp.where(lane == d, run, low)
            run = run + lengths_ref[m, d]
            high = jnp.where(lane == d, run, high)
        for half in range(2):
            first = order_ref[m, dc * 2 + half] * BLOCK
            low = jnp.where(lane == DOCS + half, first + BLOCK, low)
            high = jnp.where(lane == DOCS + half, none, high)
            fine = (lane >= 32 + 32 * half) & (lane < 64 + 32 * half)
            low = jnp.where(fine, first + lane - (32 + 32 * half), low)
            high = jnp.where(fine, first + lane - (31 + 32 * half), high)
        high_q = jnp.where(lane < DOCS, high, none)
        row = lax.broadcasted_iota(jnp.int32, (BLOCK, 128), 0)
        for half in range(2):
            pos = order_ref[m, dc * 2 + half] * BLOCK + row
            hidden = (pos < low) | (pos >= high_q)
            query_mask[m, half * BLOCK : (half + 1) * BLOCK, :] = jnp.where(
                hidden, HIDDEN, 0.0
            ).astype(jnp.bfloat16)

        def one_z(z_at, carry):
            for c_at in range(2):
                for x_at in range(2):
                    for half in range(2):
                        number = place(x_at, z_at, c_at) * 2 + half
                        pos = order_ref[m, number] * BLOCK + row
                        inside = (pos >= low) & (pos < high)
                        key_mask[m, z_at, c_at, x_at, half] = jnp.where(inside, 1.0, 0.0).astype(jnp.bfloat16)
            return carry

        lax.fori_loop(0, NZ, one_z, 0)

    def gathered(m, z_list):
        keys, values = [], []
        for z_at in z_list:
            k = buf[m, :, z_at, :, 0].reshape(256, HEAD_DIM)
            v = buf[m, :, z_at, :, 1].reshape(256, HEAD_DIM)
            b = key_mask[m, z_at].reshape(256, 128)
            keys.append(jnp.concatenate([k, b], axis=1))
            values.append(jnp.concatenate([v, jnp.ones_like(v)], axis=1))
        return jnp.concatenate(keys, axis=0), jnp.concatenate(values, axis=0)

    def score(m, rows, kx):
        return lax.dot_general(
            qx[m, rows, :], kx, (((1,), (1,)), ((), ())), preferred_element_type=jnp.float32
        )

    groups = [
        slice(start, start + GROUP_ROWS) for start in range(0, HEADS_LOCAL * ROWS, GROUP_ROWS)
    ]

    def fold(m, z_list, last=False):
        opening = not last
        kx, vx = gathered(m, z_list)
        scores = [score(m, rows, kx) for rows in groups]
        for rows, one in zip(groups, scores):
            if opening:
                top = jnp.max(one, axis=1, keepdims=True)
                weights = jnp.exp2((one - top) * EXP_SCALE).astype(jnp.bfloat16)
                peak[m, rows, :] = jnp.broadcast_to(top, (GROUP_ROWS, 128))
                acc[m, rows, :] = jnp.dot(weights, vx, preferred_element_type=jnp.float32)
                continue
            old = peak[m, rows, :]
            new = jnp.maximum(old, jnp.max(one, axis=1, keepdims=True))
            weights = jnp.exp2((one - new[:, :1]) * EXP_SCALE).astype(jnp.bfloat16)
            fade = jnp.exp2((old - new) * EXP_SCALE)
            mixed = acc[m, rows, :] * jnp.concatenate([fade, fade], axis=1) + jnp.dot(
                weights, vx, preferred_element_type=jnp.float32
            )
            out = (mixed[:, :HEAD_DIM] / mixed[:, HEAD_DIM:]).astype(jnp.bfloat16)
            for part in range(GROUP_ROWS // ROWS):
                att[m, rows.start // ROWS + part] = out[part * ROWS : (part + 1) * ROWS]

    def settle(vx, scores):
        top = jnp.max(scores, axis=1, keepdims=True)
        weights = jnp.exp2((scores - top) * EXP_SCALE).astype(jnp.bfloat16)
        mixed = jnp.dot(weights, vx, preferred_element_type=jnp.float32)
        return (mixed[:, :HEAD_DIM] / mixed[:, HEAD_DIM:]).astype(jnp.bfloat16)

    def put(m, h, out):
        o_ref[0, m, :, h * HEAD_DIM : (h + 1) * HEAD_DIM] = out

    def a_copy(m, h):
        return pltpu.make_async_remote_copy(
            src_ref=att.at[m, h],
            dst_ref=att.at[m, h],
            send_sem=a_send.at[m, h],
            recv_sem=a_recv.at[m, h],
            device_id=(1, dc, head),
            device_id_type=MESH,
        )

    def n_copy(m, h):
        return pltpu.make_async_remote_copy(
            src_ref=ss_out.at[m],
            dst_ref=ss_in.at[m, head],
            send_sem=n_send.at[m, h],
            recv_sem=n_recv.at[m, head],
            device_id=(1, dc, h),
            device_id_type=MESH,
        )

    def n_arrival(m, h):
        return pltpu.make_async_remote_copy(
            src_ref=ss_out.at[m],
            dst_ref=ss_in.at[m, h],
            send_sem=n_send.at[m, h],
            recv_sem=n_recv.at[m, h],
            device_id=(0, dc, h),
            device_id_type=MESH,
        )

    def stage_query(m, h, value):
        rows = slice(h * ROWS, (h + 1) * ROWS)
        qx[m, rows, :HEAD_DIM] = value
        qx[m, rows, HEAD_DIM:] = query_mask[m]

    def hand_over(m):
        squares = jnp.zeros((ROWS, HEAD_DIM), jnp.float32)
        for h in range(HEADS_LOCAL):
            wide = att[m, h].astype(jnp.float32)
            squares = squares + wide * wide
        ss_out[m, :, :ROWS] = jnp.sum(jnp.transpose(squares), axis=0, keepdims=True)
        for h in range(N_HEAD):
            n_copy(m, h).start()
        for h in range(HEADS_LOCAL):
            a_copy(m, h).start()
        for h in range(HEADS_LOCAL):
            put(m, h, att[m, h])

    def inverse_copy(m):
        return pltpu.make_async_copy(inverse_v.at[m], inverse.at[m], inverse_sem.at[m])

    def invert_order(m):
        lane = lax.broadcasted_iota(jnp.int32, (1, 128), 1)
        slot_block = jnp.zeros((1, 128), jnp.int32)
        for number in range(64):
            slot_block = jnp.where(lane == order_ref[m, number], number, slot_block)
        inverse_v[m] = slot_block
        inverse_copy(m).start()

    def cut_windows(m):
        for own in range(2):
            base = jnp.maximum(order_ref[m, dc * 2 + own] - (WINDOW - 1), 0)

            def one_block(j, carry, own=own, base=base):
                number = inverse[m, 0, base + j]
                c_at = (number >> 1) & 1
                z_at = (number >> 2) & (NZ - 1)
                x_at = number >> 5
                h_at = number & 1
                target = pl.ds(pl.multiple_of(j * BLOCK, BLOCK), BLOCK)
                k_win[m, own, target, :] = buf[m, c_at, z_at, x_at, 0, h_at]
                v_win[m, own, target, :] = buf[m, c_at, z_at, x_at, 1, h_at]
                b_win[m, own, target, :] = key_mask[m, z_at, c_at, x_at, h_at]
                return carry

            lax.fori_loop(0, WINDOW, one_block, 0, unroll=3)

    def fold_four(m, z_list, last=False):
        for z_at in z_list:
            wait_s(m, z_at)
        fold(m, z_list, last)

    def prepare(m):
        build_masks(m)
        loads[m][4].wait()

        @pl.when(seg == 1)
        def _():
            invert_order(m)

        @pl.when(seg == 0)
        def _():
            for h in range(HEADS_LOCAL):
                stage_query(m, h, q_ref[m, :, h * HEAD_DIM : (h + 1) * HEAD_DIM])

    for m in range(MICRO):
        for one in loads[m][:4]:
            one.wait()
        for i in (2, 3, 0, 1):
            @pl.when((far(i) < z) & direct(i))
            def _():
                z_send_copy(m, far(i)).start()
    for m in range(MICRO):
        for i in range(1, FAR):
            @pl.when(near(i) < z)
            def _():
                z_send_copy(m, near(i)).start()
    @pl.when(xh == 1)
    def _():
        for m in range(MICRO):
            x_copy(m, z, xh).start()

    def answer_near(i):
        @pl.when(near(i) > z)
        def _():
            pl.semaphore_wait(z_in.at[near(i)], 1)
            for m in range(MICRO):
                z_send_copy(m, near(i)).start()

    for copy in small:
        copy.wait()
    prepare(0)
    answer_near(1)
    answer_near(2)

    @pl.when(xh == 0)
    def _():
        pl.semaphore_wait(x_in, 1)

        for m in range(MICRO):
            x_copy(m, z, xh).start()

    @pl.when(core == 1)
    def _():
        pl.semaphore_wait(s_in, 1)

    answer_near(3)
    prepare(1)
    for i in range(1, FAR):
        for m in range(MICRO):
            pass_z(m, near(i))

    @pl.when(half == 0)
    def _():
        for i in range(FAR):
            @pl.when(direct(i))
            def _():
                pl.semaphore_wait(z_in.at[far(i)], 1)
                z_send_copy(0, far(i)).start()
        for i in range(FAR):
            @pl.when(direct(i))
            def _():
                z_send_copy(1, far(i)).start()

    for i in range(FAR - 1):
        for m in range(MICRO):
            pass_x(m, near(i))

    @pl.when(seg == 0)
    def _():
        pl.semaphore_wait(seg_in, 1)

        @pl.when(rank < N_HEAD - 1)
        def _():
            pl.semaphore_wait(y_in, N_HEAD - 1 - rank)

        for h in range(N_HEAD):
            @pl.when(head != h)
            def _():
                tell(y_all, (0, dc, h))

    nears = tuple(near(i) for i in range(FAR))
    fars = tuple(far(i) for i in range(FAR))

    @pl.when(side == 0)
    def _():
        for i in range(FAR):
            pass_far(0, i)
        for i in range(2):
            pass_far(1, i)

    @pl.when(side == 1)
    def _():
        for m in range(MICRO):
            for i in range(2):
                pass_far(m, i)
        for i in range(2, FAR):
            pass_far(0, i)

    for m in range(MICRO):
        pass_x(m, near(FAR - 1))

    pass_far(1, 2)
    pass_far(1, 3)
    pass_x(0, far(0))
    pass_x(0, far(1))
    @pl.when(seg == 0)
    def _():
        fold_four(0, nears)

    pass_x(0, far(2))
    pass_x(0, far(3))
    @pl.when(seg == 0)
    def _():
        fold_four(1, nears)

    @pl.when(seg == 0)
    def _():
        fold_four(0, fars, last=True)

    pass_x(1, far(0))
    pass_x(1, far(1))
    pass_x(1, far(2))
    @pl.when(seg == 0)
    def _():
        pl.semaphore_wait(y_all, N_HEAD - 1)
        hand_over(0)

    pass_x(1, far(3))
    @pl.when(seg == 0)
    def _():
        fold_four(1, fars, last=True)
        hand_over(1)
        for m in range(MICRO):
            for h in range(HEADS_LOCAL):
                a_copy(m, h).wait_send()
                n_copy(m, h).wait_send()

    @pl.when(seg == 1)
    def _():
        for m in range(MICRO):
            for z_at in range(NZ):
                wait_s(m, z_at)
            inverse_copy(m).wait()
        for m in range(MICRO):
            cut_windows(m)
            for own in range(2):
                part = slice(own * BLOCK, (own + 1) * BLOCK)
                for h in range(HEADS_LOCAL):
                    rows = slice(own * GROUP_ROWS + h * BLOCK, own * GROUP_ROWS + (h + 1) * BLOCK)
                    qx[m, rows, HEAD_DIM:] = query_mask[m, part, :]
            for h in range(N_HEAD):
                n_arrival(m, h).wait_recv()
            total = ss_in[m, 0]
            for h in range(1, N_HEAD):
                total = total + ss_in[m, h]
            wide_total = jnp.broadcast_to(total[:, :ROWS], (HEAD_DIM, ROWS))
            norm = lax.rsqrt(jnp.transpose(wide_total) / FEATURES + 1e-05)
            for h in range(HEADS_LOCAL):
                a_copy(m, h).wait_recv()
                lifted = (
                    q_ref[m, :, h * HEAD_DIM : (h + 1) * HEAD_DIM].astype(jnp.float32)
                    + att[m, h].astype(jnp.float32) * norm
                ).astype(jnp.bfloat16)
                for own in range(2):
                    rows = slice(own * GROUP_ROWS + h * BLOCK, own * GROUP_ROWS + (h + 1) * BLOCK)
                    part = slice(own * BLOCK, (own + 1) * BLOCK)
                    qx[m, rows, :HEAD_DIM] = lifted[part]
            scores = []
            for own, rows in enumerate(groups):
                kx = jnp.concatenate([k_win[m, own], b_win[m, own]], axis=1)
                scores.append(score(m, rows, kx))
            for own, rows in enumerate(groups):
                values = v_win[m, own]
                vx = jnp.concatenate([values, jnp.ones_like(values)], axis=1)
                out = settle(vx, scores[own])
                for h in range(HEADS_LOCAL):
                    o_ref[
                        0, m, own * BLOCK : (own + 1) * BLOCK, h * HEAD_DIM : (h + 1) * HEAD_DIM
                    ] = out[h * BLOCK : (h + 1) * BLOCK]

    for m in range(MICRO):
        finish_sends(m)


def on_device(queries, keys, values, block_order, doc_lengths):
    dma = pltpu.SemaphoreType.DMA
    regular = pltpu.SemaphoreType.REGULAR
    rows = HEADS_LOCAL * ROWS
    operands = [
        pltpu.with_memory_space_constraint(one, pltpu.HBM)
        for one in (block_order, doc_lengths, queries, keys, values)
    ]
    return pl.pallas_call(
        kernel,
        out_shape=jax.ShapeDtypeStruct(queries.shape, jnp.bfloat16),
        in_specs=[pl.BlockSpec(memory_space=pltpu.HBM)] * 5,
        out_specs=pl.BlockSpec(memory_space=pltpu.VMEM),
        scratch_shapes=[
            pltpu.SMEM((MICRO, 64), jnp.int32),
            pltpu.SMEM((MICRO, DOCS), jnp.int32),
            pltpu.VMEM((MICRO, ROWS, HEADS_LOCAL * HEAD_DIM), jnp.bfloat16),
            pltpu.VMEM((MICRO, 2, NZ, 2, 2, 2, BLOCK, HEAD_DIM), jnp.bfloat16),
            pltpu.VMEM((MICRO, NZ, 2, 2, 2, BLOCK, 128), jnp.bfloat16),
            pltpu.VMEM((MICRO, ROWS, 128), jnp.bfloat16),
            pltpu.VMEM((MICRO, rows, 256), jnp.bfloat16),
            pltpu.VMEM((MICRO, rows, 256), jnp.float32),
            pltpu.VMEM((MICRO, rows, 128), jnp.float32),
            pltpu.VMEM((MICRO, HEADS_LOCAL, ROWS, HEAD_DIM), jnp.bfloat16),
            pltpu.VMEM((MICRO, 1, 128), jnp.float32),
            pltpu.VMEM((MICRO, N_HEAD, 1, 128), jnp.float32),
            pltpu.VMEM((MICRO, 1, 128), jnp.int32),
            pltpu.SMEM((MICRO, 1, 128), jnp.int32),
            pltpu.VMEM((MICRO, 2, WINDOW * BLOCK, HEAD_DIM), jnp.bfloat16),
            pltpu.VMEM((MICRO, 2, WINDOW * BLOCK, HEAD_DIM), jnp.bfloat16),
            pltpu.VMEM((MICRO, 2, WINDOW * BLOCK, 128), jnp.bfloat16),
            dma((MICRO, 5)),
            dma((2,)),
            dma((MICRO,)),
            dma((MICRO, NZ)),
            dma((MICRO, NZ)),
            dma((MICRO, 2, 2)),
            dma((MICRO, NZ)),
            dma((MICRO, NZ)),
            dma((MICRO, NZ)),
            dma((MICRO, NZ)),
            dma((MICRO, HEADS_LOCAL)),
            dma((MICRO, HEADS_LOCAL)),
            dma((MICRO, N_HEAD)),
            dma((MICRO, N_HEAD)),
            pltpu.SemaphoreType.REGULAR((NZ,)),
            regular,
            regular,
            regular,
            regular,
            regular,
        ],
        compiler_params=pltpu.CompilerParams(
            collective_id=0, has_side_effects=True, vmem_limit_bytes=48 * 1024 * 1024
        ),
        name="attend_two_layers",
    )(*operands)


def solution(mesh):
    placed = (
        P("segment", None, "dc", "head"),
        P("segment", None, "dc", "head"),
        P("segment", None, "dc", "head"),
        P(),
        P(),
    )
    return jax.shard_map(
        on_device,
        mesh=mesh,
        in_specs=placed,
        out_specs=P("segment", None, "dc", "head"),
        check_vma=False,
    )
```

```python
import math

import jax
import jax.numpy as jnp
from jax import lax
from jax.experimental import pallas as pl
from jax.experimental.pallas import tpu as pltpu
from jax.sharding import PartitionSpec as P

HEAD_DIM = 128
BLOCK = 32
MICRO = 2
DOCS = 16
HEADS_LOCAL = 8
N_HEAD = 8
ROWS = 64
FEATURES = 8192
NZ = 8
FAR = NZ // 2
HIDDEN = -1e30
MESH = pl.DeviceIdType.MESH
EXP_SCALE = math.log2(math.e) / math.sqrt(HEAD_DIM)
GROUP_ROWS = 256
WINDOW = 1024 // BLOCK + 1


def start_rank(head):
    if isinstance(head, int):
        return 2 * head - 1 if 1 <= head <= N_HEAD // 2 else 2 * ((N_HEAD - head) % N_HEAD)
    return jnp.where(
        (head >= 1) & (head <= N_HEAD // 2), 2 * head - 1, 2 * ((N_HEAD - head) % N_HEAD)
    )


def kernel(
    order_hbm,
    lengths_hbm,
    q_hbm,
    k_hbm,
    v_hbm,
    o_ref,
    order_ref,
    lengths_ref,
    q_ref,
    buf,
    key_mask,
    query_mask,
    qx,
    acc,
    peak,
    att,
    ss_out,
    ss_in,
    inverse_v,
    inverse,
    k_win,
    v_win,
    b_win,
    load_sem,
    small_sem,
    inverse_sem,
    z_send,
    z_recv,
    r_send,
    x_send,
    x_recv,
    s_send,
    s_recv,
    a_send,
    a_recv,
    n_send,
    n_recv,
    z_in,
    x_in,
    s_in,
    seg_in,
    y_in,
    y_all,
):
    seg = lax.axis_index("segment")
    dc = lax.axis_index("dc")
    head = lax.axis_index("head")
    core = dc % 2
    z = (dc // 2) % NZ
    xh = dc // (2 * NZ)
    half = z // FAR
    side = (z % FAR) // 2
    rank = start_rank(head)

    def place(x_hi, z_at, core_at):
        return (x_hi * NZ + z_at) * 2 + core_at

    sibling = (seg, place(xh, z, 1 - core), head)
    x_peer = (seg, place(1 - xh, z, core), head)

    def z_peer(z_at):
        return (seg, place(xh, z_at, core), head)

    def tell(sem, device):
        pl.semaphore_signal(sem, inc=1, device_id=device, device_id_type=MESH)

    small = (
        pltpu.make_async_copy(order_hbm, order_ref, small_sem.at[0]),
        pltpu.make_async_copy(lengths_hbm, lengths_ref, small_sem.at[1]),
    )
    loads = []
    for m in range(MICRO):
        mine = buf.at[m, core, z, xh]
        loads.append(
            [
                pltpu.make_async_copy(
                    source.at[0, m, pl.ds(part * BLOCK, BLOCK)],
                    mine.at[which, part],
                    load_sem.at[m, which * 2 + part],
                )
                for which, source in enumerate((k_hbm, v_hbm))
                for part in range(2)
            ]
            + [pltpu.make_async_copy(q_hbm.at[0, m], q_ref.at[m], load_sem.at[m, 4])]
        )
    for m in range(MICRO):
        for one in loads[m][:4]:
            one.start()
    for copy in small:
        copy.start()
    for m in range(MICRO):
        loads[m][4].start()

    def near(i):
        return half * FAR + (z + i) % FAR

    def far(i):
        return (1 - half) * FAR + jnp.where(i < 2, 1 - side, side) * 2 + (z + i) % 2

    def direct(i):
        return (side == 0) | (i < 2)

    def across(i):
        return half * FAR + (1 - side) * 2 + i

    barrier = pltpu.get_barrier_semaphore()
    for i in range(1, FAR):
        @pl.when(near(i) > z)
        def _():
            tell(barrier, z_peer(near(i)))
    for i in range(FAR):
        @pl.when((far(i) > z) & direct(i))
        def _():
            tell(barrier, z_peer(far(i)))

    @pl.when(xh == 0)
    def _():
        tell(barrier, x_peer)

    @pl.when(core == 1)
    def _():
        tell(barrier, sibling)

    @pl.when(seg == 0)
    def _():
        tell(barrier, (1, dc, head))
        for h in range(N_HEAD):
            @pl.when(start_rank(h) > rank)
            def _():
                tell(barrier, (0, dc, h))

    greetings = z % FAR + half * (4 - 2 * side) + xh + (1 - core) + seg + (1 - seg) * rank

    @pl.when(greetings > 0)
    def _():
        pl.semaphore_wait(barrier, greetings)

    for i in range(1, FAR):
        @pl.when(near(i) < z)
        def _():
            tell(z_in.at[z], z_peer(near(i)))
    for i in range(FAR):
        @pl.when((far(i) < z) & direct(i))
        def _():
            tell(z_in.at[z], z_peer(far(i)))

    @pl.when(xh == 1)
    def _():
        tell(x_in, x_peer)

    @pl.when(core == 0)
    def _():
        tell(s_in, sibling)

    @pl.when(seg == 1)
    def _():
        tell(seg_in, (0, dc, head))

    @pl.when(seg == 0)
    def _():
        for h in range(N_HEAD):
            @pl.when(start_rank(h) < rank)
            def _():
                tell(y_in, (0, dc, h))

    def z_send_copy(m, z_at):
        block = buf.at[m, core, z, xh]
        return pltpu.make_async_remote_copy(
            src_ref=block,
            dst_ref=block,
            send_sem=z_send.at[m, z_at],
            recv_sem=z_recv.at[m, z],
            device_id=z_peer(z_at),
            device_id_type=MESH,
        )

    def z_arrival(m, z_at):
        block = buf.at[m, core, z_at, xh]
        return pltpu.make_async_remote_copy(
            src_ref=block,
            dst_ref=block,
            send_sem=z_send.at[m, z_at],
            recv_sem=z_recv.at[m, z_at],
            device_id=z_peer(z_at),
            device_id_type=MESH,
        )

    def x_copy(m, z_at, x_at):
        block = buf.at[m, core, z_at, x_at]
        return pltpu.make_async_remote_copy(
            src_ref=block,
            dst_ref=block,
            send_sem=x_send.at[m, z_at],
            recv_sem=x_recv.at[m, z_at],
            device_id=x_peer,
            device_id_type=MESH,
        )

    def s_copy(m, z_at, core_at):
        block = buf.at[m, core_at, z_at]
        return pltpu.make_async_remote_copy(
            src_ref=block,
            dst_ref=block,
            send_sem=s_send.at[m, z_at],
            recv_sem=s_recv.at[m, z_at],
            device_id=sibling,
            device_id_type=MESH,
        )

    def relays():
        return z % FAR == 1

    def relay_copy(m, i, j):
        block = buf.at[m, core, far(i), xh]
        return pltpu.make_async_remote_copy(
            src_ref=block,
            dst_ref=block,
            send_sem=r_send.at[m, i, j],
            recv_sem=z_recv.at[m, far(i)],
            device_id=z_peer(across(j)),
            device_id_type=MESH,
        )

    def pass_far(m, i):
        z_arrival(m, far(i)).wait_recv()
        if i < 2:
            @pl.when(relays())
            def _():
                for j in range(2):
                    relay_copy(m, i, j).start()

        x_copy(m, far(i), xh).start()

    def pass_z(m, z_at):
        z_arrival(m, z_at).wait_recv()
        x_copy(m, z_at, xh).start()

    def pass_x(m, z_at):
        x_copy(m, z_at, 1 - xh).wait_recv()
        s_copy(m, z_at, core).start()

    def wait_s(m, z_at):
        s_copy(m, z_at, 1 - core).wait_recv()

    def finish_sends(m):
        for i in range(1, FAR):
            z_send_copy(m, near(i)).wait_send()
        for i in range(FAR):
            @pl.when(direct(i))
            def _():
                z_send_copy(m, far(i)).wait_send()

        @pl.when(relays())
        def _():
            for i in range(2):
                for j in range(2):
                    relay_copy(m, i, j).wait_send()

        for z_at in range(NZ):
            x_copy(m, z_at, xh).wait_send()
            s_copy(m, z_at, core).wait_send()

    def build_masks(m):
        lane = lax.broadcasted_iota(jnp.int32, (1, 128), 1)
        none = jnp.int32(1 << 20)
        low = jnp.full((1, 128), none, jnp.int32)
        high = jnp.zeros((1, 128), jnp.int32)
        run = jnp.int32(0)
        for d in range(DOCS):
            low = jnp.where(lane == d, run, low)
            run = run + lengths_ref[m, d]
            high = jnp.where(lane == d, run, high)
        for half in range(2):
            first = order_ref[m, dc * 2 + half] * BLOCK
            low = jnp.where(lane == DOCS + half, first + BLOCK, low)
            high = jnp.where(lane == DOCS + half, none, high)
            fine = (lane >= 32 + 32 * half) & (lane < 64 + 32 * half)
            low = jnp.where(fine, first + lane - (32 + 32 * half), low)
            high = jnp.where(fine, first + lane - (31 + 32 * half), high)
        high_q = jnp.where(lane < DOCS, high, none)
        row = lax.broadcasted_iota(jnp.int32, (BLOCK, 128), 0)
        for half in range(2):
            pos = order_ref[m, dc * 2 + half] * BLOCK + row
            hidden = (pos < low) | (pos >= high_q)
            query_mask[m, half * BLOCK : (half + 1) * BLOCK, :] = jnp.where(
                hidden, HIDDEN, 0.0
            ).astype(jnp.bfloat16)

        def one_z(z_at, carry):
            for c_at in range(2):
                for x_at in range(2):
                    for half in range(2):
                        number = place(x_at, z_at, c_at) * 2 + half
                        pos = order_ref[m, number] * BLOCK + row
                        inside = (pos >= low) & (pos < high)
                        key_mask[m, z_at, c_at, x_at, half] = jnp.where(inside, 1.0, 0.0).astype(jnp.bfloat16)
            return carry

        lax.fori_loop(0, NZ, one_z, 0)

    def gathered(m, z_list):
        keys, values = [], []
        for z_at in z_list:
            k = buf[m, :, z_at, :, 0].reshape(256, HEAD_DIM)
            v = buf[m, :, z_at, :, 1].reshape(256, HEAD_DIM)
            b = key_mask[m, z_at].reshape(256, 128)
            keys.append(jnp.concatenate([k, b], axis=1))
            values.append(jnp.concatenate([v, jnp.ones_like(v)], axis=1))
        return jnp.concatenate(keys, axis=0), jnp.concatenate(values, axis=0)

    def score(m, rows, kx):
        return lax.dot_general(
            qx[m, rows, :], kx, (((1,), (1,)), ((), ())), preferred_element_type=jnp.float32
        )

    groups = [
        slice(start, start + GROUP_ROWS) for start in range(0, HEADS_LOCAL * ROWS, GROUP_ROWS)
    ]

    def fold(m, z_list, last=False):
        opening = not last
        kx, vx = gathered(m, z_list)
        scores = [score(m, rows, kx) for rows in groups]
        for rows, one in zip(groups, scores):
            if opening:
                top = jnp.max(one, axis=1, keepdims=True)
                weights = jnp.exp2((one - top) * EXP_SCALE).astype(jnp.bfloat16)
                peak[m, rows, :] = jnp.broadcast_to(top, (GROUP_ROWS, 128))
                acc[m, rows, :] = jnp.dot(weights, vx, preferred_element_type=jnp.float32)
                continue
            old = peak[m, rows, :]
            new = jnp.maximum(old, jnp.max(one, axis=1, keepdims=True))
            weights = jnp.exp2((one - new[:, :1]) * EXP_SCALE).astype(jnp.bfloat16)
            fade = jnp.exp2((old - new) * EXP_SCALE)
            mixed = acc[m, rows, :] * jnp.concatenate([fade, fade], axis=1) + jnp.dot(
                weights, vx, preferred_element_type=jnp.float32
            )
            out = (mixed[:, :HEAD_DIM] / mixed[:, HEAD_DIM:]).astype(jnp.bfloat16)
            for part in range(GROUP_ROWS // ROWS):
                att[m, rows.start // ROWS + part] = out[part * ROWS : (part + 1) * ROWS]

    def settle(vx, scores):
        top = jnp.max(scores, axis=1, keepdims=True)
        weights = jnp.exp2((scores - top) * EXP_SCALE).astype(jnp.bfloat16)
        mixed = jnp.dot(weights, vx, preferred_element_type=jnp.float32)
        return (mixed[:, :HEAD_DIM] / mixed[:, HEAD_DIM:]).astype(jnp.bfloat16)

    def put(m, h, out):
        o_ref[0, m, :, h * HEAD_DIM : (h + 1) * HEAD_DIM] = out

    def a_copy(m, h):
        return pltpu.make_async_remote_copy(
            src_ref=att.at[m, h],
            dst_ref=att.at[m, h],
            send_sem=a_send.at[m, h],
            recv_sem=a_recv.at[m, h],
            device_id=(1, dc, head),
            device_id_type=MESH,
        )

    def n_copy(m, h):
        return pltpu.make_async_remote_copy(
            src_ref=ss_out.at[m],
            dst_ref=ss_in.at[m, head],
            send_sem=n_send.at[m, h],
            recv_sem=n_recv.at[m, head],
            device_id=(1, dc, h),
            device_id_type=MESH,
        )

    def n_arrival(m, h):
        return pltpu.make_async_remote_copy(
            src_ref=ss_out.at[m],
            dst_ref=ss_in.at[m, h],
            send_sem=n_send.at[m, h],
            recv_sem=n_recv.at[m, h],
            device_id=(0, dc, h),
            device_id_type=MESH,
        )

    def stage_query(m, h, value):
        rows = slice(h * ROWS, (h + 1) * ROWS)
        qx[m, rows, :HEAD_DIM] = value
        qx[m, rows, HEAD_DIM:] = query_mask[m]

    def hand_over(m):
        squares = jnp.zeros((ROWS, HEAD_DIM), jnp.float32)
        for h in range(HEADS_LOCAL):
            wide = att[m, h].astype(jnp.float32)
            squares = squares + wide * wide
        ss_out[m, :, :ROWS] = jnp.sum(jnp.transpose(squares), axis=0, keepdims=True)
        for h in range(N_HEAD):
            n_copy(m, h).start()
        for h in range(HEADS_LOCAL):
            a_copy(m, h).start()
    def inverse_copy(m):
        return pltpu.make_async_copy(inverse_v.at[m], inverse.at[m], inverse_sem.at[m])

    def invert_order(m):
        lane = lax.broadcasted_iota(jnp.int32, (1, 128), 1)
        slot_block = jnp.zeros((1, 128), jnp.int32)
        for number in range(64):
            slot_block = jnp.where(lane == order_ref[m, number], number, slot_block)
        inverse_v[m] = slot_block
        inverse_copy(m).start()

    def cut_windows(m):
        for own in range(2):
            base = jnp.maximum(order_ref[m, dc * 2 + own] - (WINDOW - 1), 0)

            def one_block(j, carry, own=own, base=base):
                number = inverse[m, 0, base + j]
                c_at = (number >> 1) & 1
                z_at = (number >> 2) & (NZ - 1)
                x_at = number >> 5
                h_at = number & 1
                target = pl.ds(pl.multiple_of(j * BLOCK, BLOCK), BLOCK)
                k_win[m, own, target, :] = buf[m, c_at, z_at, x_at, 0, h_at]
                v_win[m, own, target, :] = buf[m, c_at, z_at, x_at, 1, h_at]
                b_win[m, own, target, :] = key_mask[m, z_at, c_at, x_at, h_at]
                return carry

            lax.fori_loop(0, WINDOW, one_block, 0, unroll=3)

    def fold_four(m, z_list, last=False):
        for z_at in z_list:
            wait_s(m, z_at)
        fold(m, z_list, last)

    def prepare(m):
        build_masks(m)
        loads[m][4].wait()

        @pl.when(seg == 1)
        def _():
            invert_order(m)

        @pl.when(seg == 0)
        def _():
            for h in range(HEADS_LOCAL):
                stage_query(m, h, q_ref[m, :, h * HEAD_DIM : (h + 1) * HEAD_DIM])

    for m in range(MICRO):
        for one in loads[m][:4]:
            one.wait()
        for i in (2, 3, 0, 1):
            @pl.when((far(i) < z) & direct(i))
            def _():
                z_send_copy(m, far(i)).start()
    for m in range(MICRO):
        for i in range(1, FAR):
            @pl.when(near(i) < z)
            def _():
                z_send_copy(m, near(i)).start()
    @pl.when(xh == 1)
    def _():
        for m in range(MICRO):
            x_copy(m, z, xh).start()

    def answer_near(i):
        @pl.when(near(i) > z)
        def _():
            pl.semaphore_wait(z_in.at[near(i)], 1)
            for m in range(MICRO):
                z_send_copy(m, near(i)).start()

    for copy in small:
        copy.wait()
    prepare(0)
    answer_near(1)
    answer_near(2)

    @pl.when(xh == 0)
    def _():
        pl.semaphore_wait(x_in, 1)

        for m in range(MICRO):
            x_copy(m, z, xh).start()

    @pl.when(core == 1)
    def _():
        pl.semaphore_wait(s_in, 1)

    answer_near(3)
    prepare(1)
    for i in range(1, FAR):
        for m in range(MICRO):
            pass_z(m, near(i))

    @pl.when(half == 0)
    def _():
        for i in range(FAR):
            @pl.when(direct(i))
            def _():
                pl.semaphore_wait(z_in.at[far(i)], 1)
                z_send_copy(0, far(i)).start()
        for i in range(FAR):
            @pl.when(direct(i))
            def _():
                z_send_copy(1, far(i)).start()

    for i in range(FAR - 1):
        for m in range(MICRO):
            pass_x(m, near(i))

    @pl.when(seg == 0)
    def _():
        pl.semaphore_wait(seg_in, 1)

        @pl.when(rank < N_HEAD - 1)
        def _():
            pl.semaphore_wait(y_in, N_HEAD - 1 - rank)

        for h in range(N_HEAD):
            @pl.when(head != h)
            def _():
                tell(y_all, (0, dc, h))

    nears = tuple(near(i) for i in range(FAR))
    fars = tuple(far(i) for i in range(FAR))

    @pl.when(side == 0)
    def _():
        for i in range(FAR):
            pass_far(0, i)
        for i in range(2):
            pass_far(1, i)

    @pl.when(side == 1)
    def _():
        for m in range(MICRO):
            for i in range(2):
                pass_far(m, i)
        for i in range(2, FAR):
            pass_far(0, i)

    for m in range(MICRO):
        pass_x(m, near(FAR - 1))

    pass_far(1, 2)
    pass_far(1, 3)
    pass_x(0, far(0))
    pass_x(0, far(1))
    @pl.when(seg == 0)
    def _():
        fold_four(0, nears)

    pass_x(0, far(2))
    pass_x(0, far(3))
    @pl.when(seg == 0)
    def _():
        fold_four(1, nears)

    @pl.when(seg == 0)
    def _():
        fold_four(0, fars, last=True)

    pass_x(1, far(0))
    pass_x(1, far(1))
    pass_x(1, far(2))
    @pl.when(seg == 0)
    def _():
        pl.semaphore_wait(y_all, N_HEAD - 1)
        hand_over(0)

    pass_x(1, far(3))
    @pl.when(seg == 0)
    def _():
        fold_four(1, fars, last=True)
        hand_over(1)
        for m in range(MICRO):
            for h in range(HEADS_LOCAL):
                put(m, h, att[m, h])
        for m in range(MICRO):
            for h in range(HEADS_LOCAL):
                a_copy(m, h).wait_send()
                n_copy(m, h).wait_send()

    @pl.when(seg == 1)
    def _():
        for m in range(MICRO):
            for z_at in range(NZ):
                wait_s(m, z_at)
            inverse_copy(m).wait()
        for m in range(MICRO):
            cut_windows(m)
            for own in range(2):
                part = slice(own * BLOCK, (own + 1) * BLOCK)
                for h in range(HEADS_LOCAL):
                    rows = slice(own * GROUP_ROWS + h * BLOCK, own * GROUP_ROWS + (h + 1) * BLOCK)
                    qx[m, rows, HEAD_DIM:] = query_mask[m, part, :]
            for h in range(N_HEAD):
                n_arrival(m, h).wait_recv()
            total = ss_in[m, 0]
            for h in range(1, N_HEAD):
                total = total + ss_in[m, h]
            wide_total = jnp.broadcast_to(total[:, :ROWS], (HEAD_DIM, ROWS))
            norm = lax.rsqrt(jnp.transpose(wide_total) / FEATURES + 1e-05)
            for h in range(HEADS_LOCAL):
                a_copy(m, h).wait_recv()
                lifted = (
                    q_ref[m, :, h * HEAD_DIM : (h + 1) * HEAD_DIM].astype(jnp.float32)
                    + att[m, h].astype(jnp.float32) * norm
                ).astype(jnp.bfloat16)
                for own in range(2):
                    rows = slice(own * GROUP_ROWS + h * BLOCK, own * GROUP_ROWS + (h + 1) * BLOCK)
                    part = slice(own * BLOCK, (own + 1) * BLOCK)
                    qx[m, rows, :HEAD_DIM] = lifted[part]
            scores = []
            for own, rows in enumerate(groups):
                kx = jnp.concatenate([k_win[m, own], b_win[m, own]], axis=1)
                scores.append(score(m, rows, kx))
            for own, rows in enumerate(groups):
                values = v_win[m, own]
                vx = jnp.concatenate([values, jnp.ones_like(values)], axis=1)
                out = settle(vx, scores[own])
                for h in range(HEADS_LOCAL):
                    o_ref[
                        0, m, own * BLOCK : (own + 1) * BLOCK, h * HEAD_DIM : (h + 1) * HEAD_DIM
                    ] = out[h * BLOCK : (h + 1) * BLOCK]

    for m in range(MICRO):
        finish_sends(m)


def on_device(queries, keys, values, block_order, doc_lengths):
    dma = pltpu.SemaphoreType.DMA
    regular = pltpu.SemaphoreType.REGULAR
    rows = HEADS_LOCAL * ROWS
    operands = [
        pltpu.with_memory_space_constraint(one, pltpu.HBM)
        for one in (block_order, doc_lengths, queries, keys, values)
    ]
    return pl.pallas_call(
        kernel,
        out_shape=jax.ShapeDtypeStruct(queries.shape, jnp.bfloat16),
        in_specs=[pl.BlockSpec(memory_space=pltpu.HBM)] * 5,
        out_specs=pl.BlockSpec(memory_space=pltpu.VMEM),
        scratch_shapes=[
            pltpu.SMEM((MICRO, 64), jnp.int32),
            pltpu.SMEM((MICRO, DOCS), jnp.int32),
            pltpu.VMEM((MICRO, ROWS, HEADS_LOCAL * HEAD_DIM), jnp.bfloat16),
            pltpu.VMEM((MICRO, 2, NZ, 2, 2, 2, BLOCK, HEAD_DIM), jnp.bfloat16),
            pltpu.VMEM((MICRO, NZ, 2, 2, 2, BLOCK, 128), jnp.bfloat16),
            pltpu.VMEM((MICRO, ROWS, 128), jnp.bfloat16),
            pltpu.VMEM((MICRO, rows, 256), jnp.bfloat16),
            pltpu.VMEM((MICRO, rows, 256), jnp.float32),
            pltpu.VMEM((MICRO, rows, 128), jnp.float32),
            pltpu.VMEM((MICRO, HEADS_LOCAL, ROWS, HEAD_DIM), jnp.bfloat16),
            pltpu.VMEM((MICRO, 1, 128), jnp.float32),
            pltpu.VMEM((MICRO, N_HEAD, 1, 128), jnp.float32),
            pltpu.VMEM((MICRO, 1, 128), jnp.int32),
            pltpu.SMEM((MICRO, 1, 128), jnp.int32),
            pltpu.VMEM((MICRO, 2, WINDOW * BLOCK, HEAD_DIM), jnp.bfloat16),
            pltpu.VMEM((MICRO, 2, WINDOW * BLOCK, HEAD_DIM), jnp.bfloat16),
            pltpu.VMEM((MICRO, 2, WINDOW * BLOCK, 128), jnp.bfloat16),
            dma((MICRO, 5)),
            dma((2,)),
            dma((MICRO,)),
            dma((MICRO, NZ)),
            dma((MICRO, NZ)),
            dma((MICRO, 2, 2)),
            dma((MICRO, NZ)),
            dma((MICRO, NZ)),
            dma((MICRO, NZ)),
            dma((MICRO, NZ)),
            dma((MICRO, HEADS_LOCAL)),
            dma((MICRO, HEADS_LOCAL)),
            dma((MICRO, N_HEAD)),
            dma((MICRO, N_HEAD)),
            pltpu.SemaphoreType.REGULAR((NZ,)),
            regular,
            regular,
            regular,
            regular,
            regular,
        ],
        compiler_params=pltpu.CompilerParams(
            collective_id=0, has_side_effects=True, vmem_limit_bytes=48 * 1024 * 1024
        ),
        name="attend_two_layers",
    )(*operands)


def solution(mesh):
    placed = (
        P("segment", None, "dc", "head"),
        P("segment", None, "dc", "head"),
        P("segment", None, "dc", "head"),
        P(),
        P(),
    )
    return jax.shard_map(
        on_device,
        mesh=mesh,
        in_specs=placed,
        out_specs=P("segment", None, "dc", "head"),
        check_vma=False,
    )
```

```python
import math

import jax
import jax.numpy as jnp
from jax import lax
from jax.experimental import pallas as pl
from jax.experimental.pallas import tpu as pltpu
from jax.sharding import PartitionSpec as P

HEAD_DIM = 128
BLOCK = 32
MICRO = 2
DOCS = 16
HEADS_LOCAL = 8
N_HEAD = 8
ROWS = 64
FEATURES = 8192
NZ = 8
FAR = NZ // 2
HIDDEN = -1e30
MESH = pl.DeviceIdType.MESH
EXP_SCALE = math.log2(math.e) / math.sqrt(HEAD_DIM)
GROUP_ROWS = 256
WINDOW = 1024 // BLOCK + 1


def start_rank(head):
    if isinstance(head, int):
        return 2 * head - 1 if 1 <= head <= N_HEAD // 2 else 2 * ((N_HEAD - head) % N_HEAD)
    return jnp.where(
        (head >= 1) & (head <= N_HEAD // 2), 2 * head - 1, 2 * ((N_HEAD - head) % N_HEAD)
    )


def kernel(
    order_hbm,
    lengths_hbm,
    q_hbm,
    k_hbm,
    v_hbm,
    o_ref,
    order_ref,
    lengths_ref,
    q_ref,
    buf,
    key_mask,
    query_mask,
    qx,
    acc,
    peak,
    att,
    ss_out,
    ss_in,
    inverse_v,
    inverse,
    k_win,
    v_win,
    b_win,
    load_sem,
    small_sem,
    inverse_sem,
    z_send,
    z_recv,
    r_send,
    x_send,
    x_recv,
    s_send,
    s_recv,
    a_send,
    a_recv,
    n_send,
    n_recv,
    z_in,
    x_in,
    s_in,
    seg_in,
    y_in,
    y_all,
):
    seg = lax.axis_index("segment")
    dc = lax.axis_index("dc")
    head = lax.axis_index("head")
    core = dc % 2
    z = (dc // 2) % NZ
    xh = dc // (2 * NZ)
    half = z // FAR
    side = (z % FAR) // 2
    rank = start_rank(head)

    def place(x_hi, z_at, core_at):
        return (x_hi * NZ + z_at) * 2 + core_at

    sibling = (seg, place(xh, z, 1 - core), head)
    x_peer = (seg, place(1 - xh, z, core), head)

    def z_peer(z_at):
        return (seg, place(xh, z_at, core), head)

    def tell(sem, device):
        pl.semaphore_signal(sem, inc=1, device_id=device, device_id_type=MESH)

    small = (
        pltpu.make_async_copy(order_hbm, order_ref, small_sem.at[0]),
        pltpu.make_async_copy(lengths_hbm, lengths_ref, small_sem.at[1]),
    )
    loads = []
    for m in range(MICRO):
        mine = buf.at[m, core, z, xh]
        loads.append(
            [
                pltpu.make_async_copy(
                    source.at[0, m, pl.ds(part * BLOCK, BLOCK)],
                    mine.at[which, part],
                    load_sem.at[m, which * 2 + part],
                )
                for which, source in enumerate((k_hbm, v_hbm))
                for part in range(2)
            ]
            + [pltpu.make_async_copy(q_hbm.at[0, m], q_ref.at[m], load_sem.at[m, 4])]
        )
    for m in range(MICRO):
        for one in loads[m][:4]:
            one.start()
    for copy in small:
        copy.start()
    for m in range(MICRO):
        loads[m][4].start()

    def near(i):
        return half * FAR + (z + i) % FAR

    def far(i):
        return (1 - half) * FAR + jnp.where(i < 2, 1 - side, side) * 2 + (z + i) % 2

    def direct(i):
        return (side == 0) | (i < 2)

    def across(i):
        return half * FAR + (1 - side) * 2 + i

    barrier = pltpu.get_barrier_semaphore()
    for i in range(1, FAR):
        @pl.when(near(i) > z)
        def _():
            tell(barrier, z_peer(near(i)))
    for i in range(FAR):
        @pl.when((far(i) > z) & direct(i))
        def _():
            tell(barrier, z_peer(far(i)))

    @pl.when(xh == 0)
    def _():
        tell(barrier, x_peer)

    @pl.when(core == 1)
    def _():
        tell(barrier, sibling)

    @pl.when(seg == 0)
    def _():
        tell(barrier, (1, dc, head))
        for h in range(N_HEAD):
            @pl.when(start_rank(h) > rank)
            def _():
                tell(barrier, (0, dc, h))

    greetings = z % FAR + half * (4 - 2 * side) + xh + (1 - core) + seg + (1 - seg) * rank

    @pl.when(greetings > 0)
    def _():
        pl.semaphore_wait(barrier, greetings)

    for i in range(1, FAR):
        @pl.when(near(i) < z)
        def _():
            tell(z_in.at[z], z_peer(near(i)))
    for i in range(FAR):
        @pl.when((far(i) < z) & direct(i))
        def _():
            tell(z_in.at[z], z_peer(far(i)))

    @pl.when(xh == 1)
    def _():
        tell(x_in, x_peer)

    @pl.when(core == 0)
    def _():
        tell(s_in, sibling)

    @pl.when(seg == 1)
    def _():
        tell(seg_in, (0, dc, head))

    @pl.when(seg == 0)
    def _():
        for h in range(N_HEAD):
            @pl.when(start_rank(h) < rank)
            def _():
                tell(y_in, (0, dc, h))

    def z_send_copy(m, z_at):
        block = buf.at[m, core, z, xh]
        return pltpu.make_async_remote_copy(
            src_ref=block,
            dst_ref=block,
            send_sem=z_send.at[m, z_at],
            recv_sem=z_recv.at[m, z],
            device_id=z_peer(z_at),
            device_id_type=MESH,
        )

    def z_arrival(m, z_at):
        block = buf.at[m, core, z_at, xh]
        return pltpu.make_async_remote_copy(
            src_ref=block,
            dst_ref=block,
            send_sem=z_send.at[m, z_at],
            recv_sem=z_recv.at[m, z_at],
            device_id=z_peer(z_at),
            device_id_type=MESH,
        )

    def x_copy(m, z_at, x_at):
        block = buf.at[m, core, z_at, x_at]
        return pltpu.make_async_remote_copy(
            src_ref=block,
            dst_ref=block,
            send_sem=x_send.at[m, z_at],
            recv_sem=x_recv.at[m, z_at],
            device_id=x_peer,
            device_id_type=MESH,
        )

    def s_copy(m, z_at, core_at):
        block = buf.at[m, core_at, z_at]
        return pltpu.make_async_remote_copy(
            src_ref=block,
            dst_ref=block,
            send_sem=s_send.at[m, z_at],
            recv_sem=s_recv.at[m, z_at],
            device_id=sibling,
            device_id_type=MESH,
        )

    def relays():
        return z % FAR == 1

    def relay_copy(m, i, j):
        block = buf.at[m, core, far(i), xh]
        return pltpu.make_async_remote_copy(
            src_ref=block,
            dst_ref=block,
            send_sem=r_send.at[m, i, j],
            recv_sem=z_recv.at[m, far(i)],
            device_id=z_peer(across(j)),
            device_id_type=MESH,
        )

    def pass_far(m, i):
        z_arrival(m, far(i)).wait_recv()
        if i < 2:
            @pl.when(relays())
            def _():
                for j in range(2):
                    relay_copy(m, i, j).start()

        x_copy(m, far(i), xh).start()

    def pass_z(m, z_at):
        z_arrival(m, z_at).wait_recv()
        x_copy(m, z_at, xh).start()

    def pass_x(m, z_at):
        x_copy(m, z_at, 1 - xh).wait_recv()
        s_copy(m, z_at, core).start()

    def wait_s(m, z_at):
        s_copy(m, z_at, 1 - core).wait_recv()

    def finish_sends(m):
        for i in range(1, FAR):
            z_send_copy(m, near(i)).wait_send()
        for i in range(FAR):
            @pl.when(direct(i))
            def _():
                z_send_copy(m, far(i)).wait_send()

        @pl.when(relays())
        def _():
            for i in range(2):
                for j in range(2):
                    relay_copy(m, i, j).wait_send()

        for z_at in range(NZ):
            x_copy(m, z_at, xh).wait_send()
            s_copy(m, z_at, core).wait_send()

    def build_masks(m):
        lane = lax.broadcasted_iota(jnp.int32, (1, 128), 1)
        none = jnp.int32(1 << 20)
        low = jnp.full((1, 128), none, jnp.int32)
        high = jnp.zeros((1, 128), jnp.int32)
        run = jnp.int32(0)
        for d in range(DOCS):
            low = jnp.where(lane == d, run, low)
            run = run + lengths_ref[m, d]
            high = jnp.where(lane == d, run, high)
        for half in range(2):
            first = order_ref[m, dc * 2 + half] * BLOCK
            low = jnp.where(lane == DOCS + half, first + BLOCK, low)
            high = jnp.where(lane == DOCS + half, none, high)
            fine = (lane >= 32 + 32 * half) & (lane < 64 + 32 * half)
            low = jnp.where(fine, first + lane - (32 + 32 * half), low)
            high = jnp.where(fine, first + lane - (31 + 32 * half), high)
        high_q = jnp.where(lane < DOCS, high, none)
        row = lax.broadcasted_iota(jnp.int32, (BLOCK, 128), 0)
        for half in range(2):
            pos = order_ref[m, dc * 2 + half] * BLOCK + row
            hidden = (pos < low) | (pos >= high_q)
            query_mask[m, half * BLOCK : (half + 1) * BLOCK, :] = jnp.where(
                hidden, HIDDEN, 0.0
            ).astype(jnp.bfloat16)

        def one_z(z_at, carry):
            for c_at in range(2):
                for x_at in range(2):
                    for half in range(2):
                        number = place(x_at, z_at, c_at) * 2 + half
                        pos = order_ref[m, number] * BLOCK + row
                        inside = (pos >= low) & (pos < high)
                        key_mask[m, z_at, c_at, x_at, half] = jnp.where(inside, 1.0, 0.0).astype(jnp.bfloat16)
            return carry

        lax.fori_loop(0, NZ, one_z, 0)

    def start_rows(m):
        acc[m] = jnp.zeros((HEADS_LOCAL * ROWS, 256), jnp.float32)
        peak[m] = jnp.full((HEADS_LOCAL * ROWS, 128), HIDDEN, jnp.float32)

    def gathered(m, z_list):
        keys, values = [], []
        for z_at in z_list:
            k = buf[m, :, z_at, :, 0].reshape(256, HEAD_DIM)
            v = buf[m, :, z_at, :, 1].reshape(256, HEAD_DIM)
            b = key_mask[m, z_at].reshape(256, 128)
            keys.append(jnp.concatenate([k, b], axis=1))
            values.append(jnp.concatenate([v, jnp.ones_like(v)], axis=1))
        return jnp.concatenate(keys, axis=0), jnp.concatenate(values, axis=0)

    def score(m, rows, kx):
        return lax.dot_general(
            qx[m, rows, :], kx, (((1,), (1,)), ((), ())), preferred_element_type=jnp.float32
        )

    groups = [
        slice(start, start + GROUP_ROWS) for start in range(0, HEADS_LOCAL * ROWS, GROUP_ROWS)
    ]

    def fold(m, z_list, last=False):
        kx, vx = gathered(m, z_list)
        scores = [score(m, rows, kx) for rows in groups]
        for rows, one in zip(groups, scores):
            old = peak[m, rows, :]
            new = jnp.maximum(old, jnp.max(one, axis=1, keepdims=True))
            peak[m, rows, :] = new
            weights = jnp.exp2((one - new[:, :1]) * EXP_SCALE).astype(jnp.bfloat16)
            fade = jnp.exp2((old - new) * EXP_SCALE)
            mixed = acc[m, rows, :] * jnp.concatenate([fade, fade], axis=1) + jnp.dot(
                weights, vx, preferred_element_type=jnp.float32
            )
            if last:
                out = (mixed[:, :HEAD_DIM] / mixed[:, HEAD_DIM:]).astype(jnp.bfloat16)
                for part in range(GROUP_ROWS // ROWS):
                    att[m, rows.start // ROWS + part] = out[part * ROWS : (part + 1) * ROWS]
            else:
                acc[m, rows, :] = mixed

    def settle(vx, scores):
        top = jnp.max(scores, axis=1, keepdims=True)
        weights = jnp.exp2((scores - top) * EXP_SCALE).astype(jnp.bfloat16)
        mixed = jnp.dot(weights, vx, preferred_element_type=jnp.float32)
        return (mixed[:, :HEAD_DIM] / mixed[:, HEAD_DIM:]).astype(jnp.bfloat16)

    def put(m, h, out):
        o_ref[0, m, :, h * HEAD_DIM : (h + 1) * HEAD_DIM] = out

    def a_copy(m, h):
        return pltpu.make_async_remote_copy(
            src_ref=att.at[m, h],
            dst_ref=att.at[m, h],
            send_sem=a_send.at[m, h],
            recv_sem=a_recv.at[m, h],
            device_id=(1, dc, head),
            device_id_type=MESH,
        )

    def n_copy(m, h):
        return pltpu.make_async_remote_copy(
            src_ref=ss_out.at[m],
            dst_ref=ss_in.at[m, head],
            send_sem=n_send.at[m, h],
            recv_sem=n_recv.at[m, head],
            device_id=(1, dc, h),
            device_id_type=MESH,
        )

    def n_arrival(m, h):
        return pltpu.make_async_remote_copy(
            src_ref=ss_out.at[m],
            dst_ref=ss_in.at[m, h],
            send_sem=n_send.at[m, h],
            recv_sem=n_recv.at[m, h],
            device_id=(0, dc, h),
            device_id_type=MESH,
        )

    def stage_query(m, h, value):
        rows = slice(h * ROWS, (h + 1) * ROWS)
        qx[m, rows, :HEAD_DIM] = value
        qx[m, rows, HEAD_DIM:] = query_mask[m]

    def hand_over(m):
        squares = jnp.zeros((ROWS, HEAD_DIM), jnp.float32)
        for h in range(HEADS_LOCAL):
            wide = att[m, h].astype(jnp.float32)
            squares = squares + wide * wide
        ss_out[m, :, :ROWS] = jnp.sum(jnp.transpose(squares), axis=0, keepdims=True)
        for h in (0, 1, 7, 2, 6, 3, 5, 4):
            n_copy(m, h).start()
        for h in range(HEADS_LOCAL):
            a_copy(m, h).start()
        for h in range(HEADS_LOCAL):
            put(m, h, att[m, h])

    def inverse_copy(m):
        return pltpu.make_async_copy(inverse_v.at[m], inverse.at[m], inverse_sem.at[m])

    def invert_order(m):
        lane = lax.broadcasted_iota(jnp.int32, (1, 128), 1)
        slot_block = jnp.zeros((1, 128), jnp.int32)
        for number in range(64):
            slot_block = jnp.where(lane == order_ref[m, number], number, slot_block)
        inverse_v[m] = slot_block
        inverse_copy(m).start()

    def cut_windows(m):
        for own in range(2):
            base = jnp.maximum(order_ref[m, dc * 2 + own] - (WINDOW - 1), 0)

            def one_block(j, carry, own=own, base=base):
                number = inverse[m, 0, base + j]
                c_at = (number >> 1) & 1
                z_at = (number >> 2) & (NZ - 1)
                x_at = number >> 5
                h_at = number & 1
                target = pl.ds(pl.multiple_of(j * BLOCK, BLOCK), BLOCK)
                k_win[m, own, target, :] = buf[m, c_at, z_at, x_at, 0, h_at]
                v_win[m, own, target, :] = buf[m, c_at, z_at, x_at, 1, h_at]
                b_win[m, own, target, :] = key_mask[m, z_at, c_at, x_at, h_at]
                return carry

            lax.fori_loop(0, WINDOW, one_block, 0, unroll=3)

    def fold_four(m, z_list, last=False):
        for z_at in z_list:
            wait_s(m, z_at)
        fold(m, z_list, last)

    def prepare(m):
        build_masks(m)
        loads[m][4].wait()

        @pl.when(seg == 1)
        def _():
            invert_order(m)

        @pl.when(seg == 0)
        def _():
            start_rows(m)
            for h in range(HEADS_LOCAL):
                stage_query(m, h, q_ref[m, :, h * HEAD_DIM : (h + 1) * HEAD_DIM])

    for m in range(MICRO):
        for one in loads[m][:4]:
            one.wait()
        for i in (2, 3, 0, 1):
            @pl.when((far(i) < z) & direct(i))
            def _():
                z_send_copy(m, far(i)).start()
    for m in range(MICRO):
        for i in range(1, FAR):
            @pl.when(near(i) < z)
            def _():
                z_send_copy(m, near(i)).start()
    @pl.when(xh == 1)
    def _():
        for m in range(MICRO):
            x_copy(m, z, xh).start()

    def answer_near(i):
        @pl.when(near(i) > z)
        def _():
            pl.semaphore_wait(z_in.at[near(i)], 1)
            for m in range(MICRO):
                z_send_copy(m, near(i)).start()

    for copy in small:
        copy.wait()
    prepare(0)
    answer_near(1)
    answer_near(2)

    @pl.when(xh == 0)
    def _():
        pl.semaphore_wait(x_in, 1)

        for m in range(MICRO):
            x_copy(m, z, xh).start()

    @pl.when(core == 1)
    def _():
        pl.semaphore_wait(s_in, 1)

    answer_near(3)
    prepare(1)
    for i in range(1, FAR):
        for m in range(MICRO):
            pass_z(m, near(i))

    @pl.when(half == 0)
    def _():
        for i in range(FAR):
            @pl.when(direct(i))
            def _():
                pl.semaphore_wait(z_in.at[far(i)], 1)
                z_send_copy(0, far(i)).start()
        for i in range(FAR):
            @pl.when(direct(i))
            def _():
                z_send_copy(1, far(i)).start()

    for i in range(FAR - 1):
        for m in range(MICRO):
            pass_x(m, near(i))

    @pl.when(seg == 0)
    def _():
        pl.semaphore_wait(seg_in, 1)

        @pl.when(rank < N_HEAD - 1)
        def _():
            pl.semaphore_wait(y_in, N_HEAD - 1 - rank)

        for h in range(N_HEAD):
            @pl.when(head != h)
            def _():
                tell(y_all, (0, dc, h))

    nears = tuple(near(i) for i in range(FAR))
    fars = tuple(far(i) for i in range(FAR))

    @pl.when(side == 0)
    def _():
        for i in range(FAR):
            pass_far(0, i)
        for i in range(2):
            pass_far(1, i)

    @pl.when(side == 1)
    def _():
        for m in range(MICRO):
            for i in range(2):
                pass_far(m, i)
        for i in range(2, FAR):
            pass_far(0, i)

    for m in range(MICRO):
        pass_x(m, near(FAR - 1))

    pass_far(1, 2)
    pass_far(1, 3)
    pass_x(0, far(0))
    pass_x(0, far(1))
    @pl.when(seg == 0)
    def _():
        fold_four(0, nears)

    pass_x(0, far(2))
    pass_x(0, far(3))
    @pl.when(seg == 0)
    def _():
        fold_four(1, nears)

    @pl.when(seg == 0)
    def _():
        fold_four(0, fars, last=True)

    pass_x(1, far(0))
    pass_x(1, far(1))
    pass_x(1, far(2))
    @pl.when(seg == 0)
    def _():
        pl.semaphore_wait(y_all, N_HEAD - 1)
        hand_over(0)

    pass_x(1, far(3))
    @pl.when(seg == 0)
    def _():
        fold_four(1, fars, last=True)
        hand_over(1)
        for m in range(MICRO):
            for h in range(HEADS_LOCAL):
                a_copy(m, h).wait_send()
                n_copy(m, h).wait_send()

    @pl.when(seg == 1)
    def _():
        for m in range(MICRO):
            for z_at in range(NZ):
                wait_s(m, z_at)
            inverse_copy(m).wait()
        for m in range(MICRO):
            cut_windows(m)
            for own in range(2):
                part = slice(own * BLOCK, (own + 1) * BLOCK)
                for h in range(HEADS_LOCAL):
                    rows = slice(own * GROUP_ROWS + h * BLOCK, own * GROUP_ROWS + (h + 1) * BLOCK)
                    qx[m, rows, HEAD_DIM:] = query_mask[m, part, :]
            for h in range(N_HEAD):
                n_arrival(m, h).wait_recv()
            total = ss_in[m, 0]
            for h in range(1, N_HEAD):
                total = total + ss_in[m, h]
            wide_total = jnp.broadcast_to(total[:, :ROWS], (HEAD_DIM, ROWS))
            norm = lax.rsqrt(jnp.transpose(wide_total) / FEATURES + 1e-05)
            for h in range(HEADS_LOCAL):
                a_copy(m, h).wait_recv()
                lifted = (
                    q_ref[m, :, h * HEAD_DIM : (h + 1) * HEAD_DIM].astype(jnp.float32)
                    + att[m, h].astype(jnp.float32) * norm
                ).astype(jnp.bfloat16)
                for own in range(2):
                    rows = slice(own * GROUP_ROWS + h * BLOCK, own * GROUP_ROWS + (h + 1) * BLOCK)
                    part = slice(own * BLOCK, (own + 1) * BLOCK)
                    qx[m, rows, :HEAD_DIM] = lifted[part]
            scores = []
            for own, rows in enumerate(groups):
                kx = jnp.concatenate([k_win[m, own], b_win[m, own]], axis=1)
                scores.append(score(m, rows, kx))
            for own, rows in enumerate(groups):
                values = v_win[m, own]
                vx = jnp.concatenate([values, jnp.ones_like(values)], axis=1)
                out = settle(vx, scores[own])
                for h in range(HEADS_LOCAL):
                    o_ref[
                        0, m, own * BLOCK : (own + 1) * BLOCK, h * HEAD_DIM : (h + 1) * HEAD_DIM
                    ] = out[h * BLOCK : (h + 1) * BLOCK]

    for m in range(MICRO):
        finish_sends(m)


def on_device(queries, keys, values, block_order, doc_lengths):
    dma = pltpu.SemaphoreType.DMA
    regular = pltpu.SemaphoreType.REGULAR
    rows = HEADS_LOCAL * ROWS
    operands = [
        pltpu.with_memory_space_constraint(one, pltpu.HBM)
        for one in (block_order, doc_lengths, queries, keys, values)
    ]
    return pl.pallas_call(
        kernel,
        out_shape=jax.ShapeDtypeStruct(queries.shape, jnp.bfloat16),
        in_specs=[pl.BlockSpec(memory_space=pltpu.HBM)] * 5,
        out_specs=pl.BlockSpec(memory_space=pltpu.VMEM),
        scratch_shapes=[
            pltpu.SMEM((MICRO, 64), jnp.int32),
            pltpu.SMEM((MICRO, DOCS), jnp.int32),
            pltpu.VMEM((MICRO, ROWS, HEADS_LOCAL * HEAD_DIM), jnp.bfloat16),
            pltpu.VMEM((MICRO, 2, NZ, 2, 2, 2, BLOCK, HEAD_DIM), jnp.bfloat16),
            pltpu.VMEM((MICRO, NZ, 2, 2, 2, BLOCK, 128), jnp.bfloat16),
            pltpu.VMEM((MICRO, ROWS, 128), jnp.bfloat16),
            pltpu.VMEM((MICRO, rows, 256), jnp.bfloat16),
            pltpu.VMEM((MICRO, rows, 256), jnp.float32),
            pltpu.VMEM((MICRO, rows, 128), jnp.float32),
            pltpu.VMEM((MICRO, HEADS_LOCAL, ROWS, HEAD_DIM), jnp.bfloat16),
            pltpu.VMEM((MICRO, 1, 128), jnp.float32),
            pltpu.VMEM((MICRO, N_HEAD, 1, 128), jnp.float32),
            pltpu.VMEM((MICRO, 1, 128), jnp.int32),
            pltpu.SMEM((MICRO, 1, 128), jnp.int32),
            pltpu.VMEM((MICRO, 2, WINDOW * BLOCK, HEAD_DIM), jnp.bfloat16),
            pltpu.VMEM((MICRO, 2, WINDOW * BLOCK, HEAD_DIM), jnp.bfloat16),
            pltpu.VMEM((MICRO, 2, WINDOW * BLOCK, 128), jnp.bfloat16),
            dma((MICRO, 5)),
            dma((2,)),
            dma((MICRO,)),
            dma((MICRO, NZ)),
            dma((MICRO, NZ)),
            dma((MICRO, 2, 2)),
            dma((MICRO, NZ)),
            dma((MICRO, NZ)),
            dma((MICRO, NZ)),
            dma((MICRO, NZ)),
            dma((MICRO, HEADS_LOCAL)),
            dma((MICRO, HEADS_LOCAL)),
            dma((MICRO, N_HEAD)),
            dma((MICRO, N_HEAD)),
            pltpu.SemaphoreType.REGULAR((NZ,)),
            regular,
            regular,
            regular,
            regular,
            regular,
        ],
        compiler_params=pltpu.CompilerParams(
            collective_id=0, has_side_effects=True, vmem_limit_bytes=48 * 1024 * 1024
        ),
        name="attend_two_layers",
    )(*operands)


def solution(mesh):
    placed = (
        P("segment", None, "dc", "head"),
        P("segment", None, "dc", "head"),
        P("segment", None, "dc", "head"),
        P(),
        P(),
    )
    return jax.shard_map(
        on_device,
        mesh=mesh,
        in_specs=placed,
        out_specs=P("segment", None, "dc", "head"),
        check_vma=False,
    )
```
